128 devices in a mesh: seq: 8 (over y_lo, x), ctx: 16 (over y_hi, z, core).
Axes of the slice: x: 4, y: 4 (y_hi: 2, y_lo: 2; y = y_hi * 2 + y_lo), z: 4, core: 2. Of those that a mesh axis runs over, the one named last changes fastest.
Arguments:
- tokens: bfloat16 [8, 3072, 1024], P('seq', 'ctx'), may hold values from -6 to 6
- cotangent: bfloat16 [8, 3072, 1024], P('seq', 'ctx'), may hold values from -6 to 6
- w_query: bfloat16 [1024, 1024], P('seq'), may hold values from -0.1875 to 0.1875
- b_query: bfloat16 [1024], P('seq'), may hold values from -3 to 3
- w_key: bfloat16 [1024, 1024], P('seq'), may hold values from -0.1875 to 0.1875
- w_value: bfloat16 [1024, 1024], P('seq'), may hold values from -0.1875 to 0.1875
- b_value: bfloat16 [1024], P('seq'), may hold values from -3 to 3
- w_output: bfloat16 [1024, 1024], P('seq'), may hold values from -2.5 to 2.5
- b_output: bfloat16 [1024], P('seq'), may hold values from -3 to 3
- first_gain: bfloat16 [1024], P('seq'), may hold values from 0.5 to 1.5
- first_shift: bfloat16 [1024], P('seq'), may hold values from -3 to 3
- w_inner: bfloat16 [1024, 4096], P('seq'), may hold values from -0.1875 to 0.1875
- b_inner: bfloat16 [4096], P('seq'), may hold values from -3 to 3
- w_outer: bfloat16 [4096, 1024], P('seq'), may hold values from -0.09375 to 0.09375
- b_outer: bfloat16 [1024], P('seq'), may hold values from -3 to 3
- second_gain: bfloat16 [1024], P('seq'), may hold values from 0.5 to 1.5
- second_shift: bfloat16 [1024], P('seq'), may hold values from -3 to 3
Outputs:
- result: bfloat16 [8, 3072, 1024], P('seq', 'ctx')
- token_grad: float32 [8, 3072, 1024], P('seq', 'ctx')
- query_weight_grad: float32 [1024, 1024], P('seq')
- query_bias_grad: float32 [1024], P('seq')
- key_weight_grad: float32 [1024, 1024], P('seq')
- value_weight_grad: float32 [1024, 1024], P('seq')
- value_bias_grad: float32 [1024], P('seq')
- output_weight_grad: float32 [1024, 1024], P('seq')
- output_bias_grad: float32 [1024], P('seq')
- first_gain_grad: float32 [1024], P('seq')
- first_shift_grad: float32 [1024], P('seq')
- inner_weight_grad: float32 [1024, 4096], P('seq')
- inner_bias_grad: float32 [4096], P('seq')
- outer_weight_grad: float32 [4096, 1024], P('seq')
- outer_bias_grad: float32 [1024], P('seq')
- second_gain_grad: float32 [1024], P('seq')
- second_shift_grad: float32 [1024], P('seq')
The draws below stay inside these ranges and needn't reach their ends.
All inputs are finite; a program needn't handle non-finite values.
Results may differ from the reference program's by a relative error of at most 0.028.
Values may be sent and summed in bfloat16 or wider, within the bound.
A program may use at most 192 MiB of HBM per device.

```python
import math
import jax
import jax.numpy as jnp
from jax import lax

D = 1024
HEADS = 16
HD = 64
FF = 4096
SEQS = 8
LENGTH = 3072


def steps_of(own_key, extent, split, smallest, top_value):
    level, own = 1.0, jax.random.fold_in(own_key, 6)
    for axis_at, blocks in split:
        steps = jnp.exp(jax.random.uniform(jax.random.fold_in(own, axis_at), (blocks,), jnp.float32, smallest / len(split), top_value / len(split)))
        level = level * jnp.repeat(steps, extent[axis_at] // blocks).reshape([-1 if axis == axis_at else 1 for axis in range(len(extent))])
    return level


def noise(rng, extent, width, bound, split=(), kind=jnp.bfloat16):
    drawn = jax.random.normal(rng, extent, jnp.float32) * width
    if len(split) > 0:
        drawn = steps_of(rng, extent, split, -0.22, 0.18) * drawn
    return jnp.clip(drawn, min=-bound, max=bound).astype(kind)


def setup_inputs(seed: int = 0) -> dict:
    key_list = jax.random.split(jax.random.key(seed), 18)
    tokens = noise(key_list[0], (SEQS, LENGTH, D), 1.0, 6.0, ((0, 8), (1, 16)))
    cotangent = noise(key_list[1], (SEQS, LENGTH, D), 1.0, 6.0, ((0, 8), (1, 16)))
    w_query = noise(key_list[2], (D, D), D ** -0.5, 0.1875, ((0, 8),))
    b_query = noise(key_list[3], (D,), 0.5, 3.0, ((0, 8),))
    w_key = noise(key_list[4], (D, D), D ** -0.5, 0.1875, ((0, 8),))
    w_value = noise(key_list[5], (D, D), D ** -0.5, 0.1875, ((0, 8),))
    b_value = noise(key_list[6], (D,), 0.5, 3.0, ((0, 8),))
    w_output = noise(key_list[7], (D, D), (max(D * 16 // LENGTH, 1)) ** -0.5, 2.5, ((0, 8),))
    b_output = noise(key_list[8], (D,), 0.5, 3.0, ((0, 8),))
    first_gain = jnp.clip(1.0 + 0.1 * jax.random.normal(key_list[9], (D,), jnp.float32), 0.5, 1.5).astype(jnp.bfloat16)
    first_shift = noise(key_list[10], (D,), 0.5, 3.0, ((0, 8),))
    w_inner = noise(key_list[11], (D, FF), D ** -0.5, 0.1875, ((0, 8),))
    b_inner = noise(key_list[12], (FF,), 0.5, 3.0, ((0, 8),))
    w_outer = noise(key_list[13], (FF, D), FF ** -0.5, 0.09375, ((0, 8),))
    b_outer = noise(key_list[14], (D,), 0.5, 3.0, ((0, 8),))
    second_gain = jnp.clip(1.0 + 0.1 * jax.random.normal(key_list[15], (D,), jnp.float32), 0.5, 1.5).astype(jnp.bfloat16)
    second_shift = noise(key_list[16], (D,), 0.5, 3.0, ((0, 8),))
    return {"tokens": tokens, "cotangent": cotangent, "w_query": w_query, "b_query": b_query, "w_key": w_key, "w_value": w_value, "b_value": b_value, "w_output": w_output, "b_output": b_output, "first_gain": first_gain, "first_shift": first_shift, "w_inner": w_inner, "b_inner": b_inner, "w_outer": w_outer, "b_outer": b_outer, "second_gain": second_gain, "second_shift": second_shift}


@jax.custom_vjp
def low(v):
    return lax.optimization_barrier(v.astype(jnp.bfloat16)).astype(jnp.float32)

@jax.custom_vjp
def low_back(v):
    return v

def low_keep(v):
    return (low(v), None)

def low_pass(kept, grad):
    return (grad,)

def back_keep(v):
    return (v, None)

def back_low(kept, grad):
    return (low(grad),)
low.defvjp(low_keep, low_pass)
low_back.defvjp(back_keep, back_low)

def product(left, right):
    return jnp.matmul(left, right, precision=lax.Precision.HIGHEST)

def normalize(hidden, gain, shift):
    mean = lax.optimization_barrier(jnp.mean(hidden, axis=-1, keepdims=True))
    centered = hidden - mean
    variance = lax.optimization_barrier(jnp.mean(centered * centered, axis=-1, keepdims=True))
    return centered * lax.rsqrt(variance + 1e-05) * gain + shift

def attend(query, key, value):
    length = query.shape[0]
    block = math.gcd(length, 512)
    scale = HD ** (-0.5)
    blocks = query.reshape(length // block, block, HEADS, HD)

    def one_block(query_block):
        scores = jnp.einsum('thd,shd->hts', query_block, key, precision=lax.Precision.HIGHEST) * scale
        scores = low_back(scores)
        probs = low(jax.nn.softmax(scores, axis=-1))
        return jnp.einsum('hts,shd->thd', probs, value, precision=lax.Precision.HIGHEST)
    out = lax.map(jax.checkpoint(one_block), blocks)
    return out.reshape(length, HEADS * HD)

def layer(inputs, w_query, b_query, w_key, w_value, b_value, w_output, b_output, first_gain, first_shift, w_inner, b_inner, w_outer, b_outer, second_gain, second_shift):
    length = inputs.shape[0]
    query = low(low_back(product(inputs, w_query) + b_query))
    key = low(low_back(product(inputs, w_key)))
    value = low(low_back(product(inputs, w_value) + b_value))
    attended = attend(query.reshape(length, HEADS, HD), key.reshape(length, HEADS, HD), value.reshape(length, HEADS, HD))
    attended = low(low_back(attended))
    branch = low_back(product(attended, w_output) + b_output)
    middle = normalize(inputs + branch, first_gain, first_shift)
    middle_low = low(middle)
    inner = low_back(product(middle_low, w_inner) + b_inner)
    active = low(jax.nn.gelu(inner, approximate=False))
    outer = low_back(product(active, w_outer) + b_outer)
    return normalize(middle + outer, second_gain, second_shift)

def reference(tokens, cotangent, w_query, b_query, w_key, w_value, b_value, w_output, b_output, first_gain, first_shift, w_inner, b_inner, w_outer, b_outer, second_gain, second_shift):
    params = tuple((w.astype(jnp.float32) for w in (w_query, b_query, w_key, w_value, b_value, w_output, b_output, first_gain, first_shift, w_inner, b_inner, w_outer, b_outer, second_gain, second_shift)))

    def step(totals, pair):
        inputs, upstream = pair
        output, pull = jax.vjp(layer, inputs.astype(jnp.float32), *params)
        grads = pull(upstream.astype(jnp.float32))
        totals = tuple((total + grad for total, grad in zip(totals, grads[1:])))
        return (totals, (output.astype(jnp.bfloat16), grads[0]))
    start = tuple((jnp.zeros(p.shape, jnp.float32) for p in params))
    totals, (outputs, token_grads) = lax.scan(step, start, (tokens, cotangent))
    return (outputs, token_grads, totals[0], totals[1], totals[2], totals[3], totals[4], totals[5], totals[6], totals[7], totals[8], totals[9], totals[10], totals[11], totals[12], totals[13], totals[14])
```

```python
import functools
import math

import jax
import jax.numpy as jnp
from jax import lax
from jax.experimental import pallas as pl
from jax.experimental.pallas import tpu as pltpu
from jax.sharding import PartitionSpec as P

D = 1024
HEADS = 16
HD = 64
FF = 4096
SEQ = 8
CHIPS = 8
ROWS = 192
PAIR = 2 * ROWS
LENGTH = CHIPS * PAIR
SCALE2 = HD ** (-0.5) * math.log2(math.e)
BLOCK = 512
BF = jnp.bfloat16
F32 = jnp.float32
ANY = pl.BlockSpec(memory_space=pl.ANY)
VMEM = pl.BlockSpec(memory_space=pltpu.VMEM)


def dot(left, right, dims=((1,), (0,))):
    return lax.dot_general(left, right, (dims, ((), ())), preferred_element_type=F32)


def group_size(group):
    return 2 if group == "core" else 8


def group_me(group):
    if group == "seq":
        return lax.axis_index("seq")
    ctx = lax.axis_index("ctx")
    return lax.rem(ctx, 2) if group == "core" else lax.div(ctx, 2)


def group_device(group, index):
    seq, ctx = lax.axis_index("seq"), lax.axis_index("ctx")
    if group == "seq":
        return (index, ctx)
    if group == "chip":
        return (seq, index * 2 + lax.rem(ctx, 2))
    return (seq, lax.div(ctx, 2) * 2 + index)


def enter(groups):
    barrier = pltpu.get_barrier_semaphore()
    count = 0
    for group in groups:
        size, me = group_size(group), group_me(group)
        for step in range(1, size):
            pl.semaphore_signal(
                barrier,
                inc=1,
                device_id=group_device(group, lax.rem(me + step, size)),
                device_id_type=pl.DeviceIdType.MESH,
            )
            count += 1
    pl.semaphore_wait(barrier, count)


class Exchange:
    def __init__(self, kind, group, source, target, send, recv, own):
        self.kind, self.group = kind, group
        self.source, self.target = source, target
        self.send, self.recv, self.own = send, recv, own

    def copies(self):
        size, me = group_size(self.group), group_me(self.group)
        made = []
        for step in range(1, size):
            peer = lax.rem(me + step, size)
            piece = self.source if self.kind == "ag" else self.source.at[peer]
            made.append(
                pltpu.make_async_remote_copy(
                    src_ref=piece,
                    dst_ref=self.target.at[me],
                    send_sem=self.send.at[step - 1],
                    recv_sem=self.recv.at[step - 1],
                    device_id=group_device(self.group, peer),
                    device_id_type=pl.DeviceIdType.MESH,
                )
            )
        piece = self.source if self.kind == "ag" else self.source.at[me]
        return made, pltpu.make_async_copy(piece, self.target.at[me], self.own)

    def start(self):
        made, own = self.copies()
        for copy in made:
            copy.start()
        own.start()

    def wait(self):
        made, own = self.copies()
        own.wait()
        for copy in made:
            copy.wait()


def target_shape(kind, group, value):
    shape = value.shape if kind == "a2a" else (group_size(group),) + value.shape
    return jax.ShapeDtypeStruct(shape, value.dtype)


def sems(group):
    count = group_size(group) - 1
    return [
        pltpu.SemaphoreType.DMA((count,)),
        pltpu.SemaphoreType.DMA((count,)),
        pltpu.SemaphoreType.DMA,
    ]


def exchange(identifier, *items):
    number = len(items)

    def kernel(*refs):
        enter(sorted({item[1] for item in items}))
        made = [
            Exchange(
                items[at][0],
                items[at][1],
                refs[at],
                refs[number + at],
                *refs[2 * number + 3 * at : 2 * number + 3 * at + 3],
            )
            for at in range(number)
        ]
        for one in made:
            one.start()
        for one in made:
            one.wait()

    return pl.pallas_call(
        kernel,
        out_shape=[target_shape(*item) for item in items],
        in_specs=[ANY] * number,
        out_specs=[ANY] * number,
        scratch_shapes=[sem for item in items for sem in sems(item[1])],
        compiler_params=pltpu.CompilerParams(
            collective_id=identifier, has_side_effects=True
        ),
        name="exchange%d" % identifier,
    )(*[item[2] for item in items])


def attend_forward(identifier, qkv, extra):
    number = len(extra)

    def kernel(*refs):
        qkv_ref, refs = refs[0], refs[1:]
        extra_in, refs = refs[:number], refs[number:]
        qkv_got, summed_ref, back_ref, stat_ref = refs[:4]
        extra_out, refs = refs[4 : 4 + number], refs[4 + number :]
        query_t, keys, value_t, low, refs = refs[0], refs[1], refs[2], refs[3], refs[4:]
        enter(sorted({"chip"} | {item[1] for item in extra}))
        first = Exchange("a2a", "chip", qkv_ref, qkv_got, *refs[:3])
        last = Exchange("a2a", "chip", low, back_ref, *refs[3:6])
        others = [
            Exchange(*extra[at][:2], extra_in[at], extra_out[at], *refs[6 + 3 * at : 9 + 3 * at])
            for at in range(number)
        ]
        first.start()
        for other in others:
            other.start()
        first.wait()
        for chip in range(CHIPS):
            at = pl.ds(chip * PAIR, PAIR)
            query_t[:, at] = qkv_got[chip, 0:HD, :]
            keys[at, :] = qkv_got[chip, HD : 2 * HD, :].astype(F32).T.astype(BF)
            value_t[:, at] = qkv_got[chip, 2 * HD : 3 * HD, :]

        def one_block(block, carry):
            at = pl.ds(pl.multiple_of(block * BLOCK, BLOCK), BLOCK)
            query = query_t[:, at]
            top = jnp.full((1, BLOCK), -1e30, F32)
            total = jnp.zeros((1, BLOCK), F32)
            summed = jnp.zeros((HD, BLOCK), F32)
            for part in range(LENGTH // BLOCK):
                here = slice(part * BLOCK, (part + 1) * BLOCK)
                scores = dot(keys[here, :], query) * SCALE2
                new_top = jnp.maximum(top, jnp.max(scores, axis=0, keepdims=True))
                factor = jnp.exp2(top - new_top)
                weights = jnp.exp2(scores - new_top)
                total = total * factor + jnp.sum(weights, axis=0, keepdims=True)
                summed = summed * factor + dot(value_t[:, here], weights.astype(BF))
                top = new_top
            summed_ref[:, at] = summed / total
            stat_ref[:, at] = top + jnp.log2(total)
            return carry

        lax.fori_loop(0, LENGTH // BLOCK, one_block, 0)
        for chip in range(CHIPS):
            low[chip] = summed_ref[:, chip * PAIR : (chip + 1) * PAIR].astype(BF)
        last.start()
        last.wait()
        for other in others:
            other.wait()

    return pl.pallas_call(
        kernel,
        out_shape=[
            jax.ShapeDtypeStruct((CHIPS, 3 * HD, PAIR), BF),
            jax.ShapeDtypeStruct((HD, LENGTH), F32),
            jax.ShapeDtypeStruct((CHIPS, HD, PAIR), BF),
            jax.ShapeDtypeStruct((1, LENGTH), F32),
        ]
        + [target_shape(*item) for item in extra],
        in_specs=[VMEM] + [ANY] * number,
        out_specs=[VMEM] * 4 + [ANY] * number,
        scratch_shapes=[
            pltpu.VMEM((HD, LENGTH), BF),
            pltpu.VMEM((LENGTH, HD), BF),
            pltpu.VMEM((HD, LENGTH), BF),
            pltpu.VMEM((CHIPS, HD, PAIR), BF),
        ]
        + sems("chip")
        + sems("chip")
        + [sem for item in extra for sem in sems(item[1])],
        compiler_params=pltpu.CompilerParams(
            collective_id=identifier,
            has_side_effects=True,
            vmem_limit_bytes=40 * 1024 * 1024,
        ),
        name="attend_forward",
    )(qkv, *[item[2] for item in extra])


def attend_backward(identifier, qkv_got, summed, stat, grad, extra):
    number = len(extra)

    def kernel(*refs):
        qkv_ref, summed_ref, stat_ref, grad_ref, refs = *refs[:4], refs[4:]
        extra_in, refs = refs[:number], refs[number:]
        grad_got, back_ref, refs = refs[0], refs[1], refs[2:]
        extra_out, refs = refs[:number], refs[number:]
        query_t, queries, key_t, keys, values, up_t, ups, delta_ref = refs[:8]
        grad_query, grad_key, grad_value, low, refs = *refs[8:12], refs[12:]
        enter(sorted({"chip"} | {item[1] for item in extra}))
        first = Exchange("a2a", "chip", grad_ref, grad_got, *refs[:3])
        last = Exchange("a2a", "chip", low, back_ref, *refs[3:6])
        others = [
            Exchange(*extra[at][:2], extra_in[at], extra_out[at], *refs[6 + 3 * at : 9 + 3 * at])
            for at in range(number)
        ]
        first.start()
        for other in others:
            other.start()
        for chip in range(CHIPS):
            at = pl.ds(chip * PAIR, PAIR)
            query_t[:, at] = qkv_ref[chip, 0:HD, :]
            queries[at, :] = qkv_ref[chip, 0:HD, :].astype(F32).T.astype(BF)
            key_t[:, at] = qkv_ref[chip, HD : 2 * HD, :]
            keys[at, :] = qkv_ref[chip, HD : 2 * HD, :].astype(F32).T.astype(BF)
            values[at, :] = qkv_ref[chip, 2 * HD : 3 * HD, :].astype(F32).T.astype(BF)
        grad_key[...] = jnp.zeros_like(grad_key)
        grad_value[...] = jnp.zeros_like(grad_value)
        first.wait()
        for chip in range(CHIPS):
            at = pl.ds(chip * PAIR, PAIR)
            up = grad_got[chip].astype(F32)
            up_t[:, at] = grad_got[chip]
            ups[at, :] = up.T.astype(BF)
            delta_ref[:, at] = jnp.sum(up * summed_ref[:, at], axis=0, keepdims=True)

        def one_block(block, carry):
            at = pl.ds(pl.multiple_of(block * BLOCK, BLOCK), BLOCK)
            query, up = query_t[:, at], up_t[:, at]
            query_rows, up_rows = queries[at, :], ups[at, :]
            stat, delta = stat_ref[:, at], delta_ref[:, at]
            gathered = jnp.zeros((HD, BLOCK), F32)
            for part in range(LENGTH // BLOCK):
                here = slice(part * BLOCK, (part + 1) * BLOCK)
                scores = dot(keys[here, :], query) * SCALE2
                probs = jnp.exp2(scores - stat)
                grad_value[here, :] += dot(probs.astype(BF), up_rows)
                slope = dot(values[here, :], up) - delta
                grad_scores = (probs * slope).astype(BF)
                grad_key[here, :] += dot(grad_scores, query_rows)
                gathered += dot(key_t[:, here], grad_scores)
            grad_query[:, at] = gathered
            return carry

        lax.fori_loop(0, LENGTH // BLOCK, one_block, 0)
        scale = HD ** (-0.5)
        for chip in range(CHIPS):
            at = slice(chip * PAIR, (chip + 1) * PAIR)
            low[chip, 0:HD, :] = (grad_query[:, at] * scale).astype(BF)
            low[chip, HD : 2 * HD, :] = (grad_key[at, :] * scale).T.astype(BF)
            low[chip, 2 * HD : 3 * HD, :] = grad_value[at, :].T.astype(BF)
        last.start()
        last.wait()
        for other in others:
            other.wait()

    return pl.pallas_call(
        kernel,
        out_shape=[
            jax.ShapeDtypeStruct((CHIPS, HD, PAIR), BF),
            jax.ShapeDtypeStruct((CHIPS, 3 * HD, PAIR), BF),
        ]
        + [target_shape(*item) for item in extra],
        in_specs=[VMEM] * 4 + [ANY] * number,
        out_specs=[VMEM] * 2 + [ANY] * number,
        scratch_shapes=[
            pltpu.VMEM((HD, LENGTH), BF),
            pltpu.VMEM((LENGTH, HD), BF),
            pltpu.VMEM((HD, LENGTH), BF),
            pltpu.VMEM((LENGTH, HD), BF),
            pltpu.VMEM((LENGTH, HD), BF),
            pltpu.VMEM((HD, LENGTH), BF),
            pltpu.VMEM((LENGTH, HD), BF),
            pltpu.VMEM((1, LENGTH), F32),
            pltpu.VMEM((HD, LENGTH), F32),
            pltpu.VMEM((LENGTH, HD), F32),
            pltpu.VMEM((LENGTH, HD), F32),
            pltpu.VMEM((CHIPS, 3 * HD, PAIR), BF),
        ]
        + sems("chip")
        + sems("chip")
        + [sem for item in extra for sem in sems(item[1])],
        compiler_params=pltpu.CompilerParams(
            collective_id=identifier,
            has_side_effects=True,
            vmem_limit_bytes=44 * 1024 * 1024,
        ),
        name="attend_backward",
    )(qkv_got, summed, stat, grad, *[item[2] for item in extra])


def normalize(hidden, gain, shift):
    centered = hidden - jnp.mean(hidden, axis=-1, keepdims=True)
    inverse = lax.rsqrt(jnp.mean(centered * centered, axis=-1, keepdims=True) + 1e-05)
    normed = centered * inverse
    return (normed * gain + shift, normed, inverse)


def normalize_back(upstream, normed, inverse, gain):
    scaled = upstream * gain
    inner = (
        scaled
        - jnp.mean(scaled, axis=-1, keepdims=True)
        - normed * jnp.mean(scaled * normed, axis=-1, keepdims=True)
    )
    return (inverse * inner, jnp.sum(upstream * normed, axis=0), jnp.sum(upstream, axis=0))


def gelu_exact(value):
    return jax.nn.gelu(value, approximate=False)


def per_device(
    tokens,
    cotangent,
    w_query,
    b_query,
    w_key,
    w_value,
    b_value,
    w_output,
    b_output,
    first_gain,
    first_shift,
    w_inner,
    b_inner,
    w_outer,
    b_outer,
    second_gain,
    second_shift,
):
    core = lax.rem(lax.axis_index("ctx"), 2)
    rows = tokens[0]

    def pick(value, axis):
        return lax.dynamic_index_in_dim(value, core, axis, keepdims=False)

    qkv_part = pick(
        jnp.stack([w_query, w_key, w_value]).reshape(3, 128, SEQ, 2, HD), 3
    )
    qkv_part = jnp.transpose(qkv_part, (1, 2, 0, 3)).reshape(128, SEQ * 3 * HD)
    output_part = pick(w_output.reshape(2, HD, D), 0)
    inner_part = pick(w_inner.reshape(128, SEQ, 2, 256), 2).reshape(128, FF // 2)
    outer_part = pick(w_outer.reshape(2, 256, D), 0)
    small_part = jnp.concatenate(
        [
            jnp.stack(
                [b_query, b_value, b_output, first_gain, first_shift, b_outer, second_gain, second_shift]
            ),
            b_inner.reshape(4, 128),
            jnp.zeros((4, 128), BF),
        ]
    )
    qkv_weight, small, rows_pair = exchange(
        0, ("ag", "seq", qkv_part), ("ag", "seq", small_part), ("ag", "core", rows)
    )
    qkv_weight = qkv_weight.reshape(D, SEQ * 3 * HD)
    rows_pair = rows_pair.reshape(PAIR, D)
    small = small.astype(F32)
    query_bias = pick(small[:, 0].reshape(SEQ, 2, HD), 1)
    value_bias = pick(small[:, 1].reshape(SEQ, 2, HD), 1)
    qkv_bias = jnp.stack([query_bias, jnp.zeros_like(query_bias), value_bias], axis=1)
    output_bias, norm_gain, norm_shift, outer_bias, final_gain, final_shift = (
        small[:, at].reshape(D) for at in range(2, 8)
    )
    inner_bias = pick(small[:, 8:12].reshape(SEQ, 2, 256), 1).reshape(FF // 2)

    qkv = (dot(qkv_weight, rows_pair, ((0,), (1,))) + qkv_bias.reshape(-1, 1)).astype(BF)
    qkv_got, summed, attended, stat, output_weight, inner_weight, outer_weight = attend_forward(
        1,
        qkv.reshape(CHIPS, 3 * HD, PAIR),
        [("ag", "seq", output_part), ("ag", "seq", inner_part), ("ag", "seq", outer_part)],
    )
    attended = attended.reshape(D // 2, PAIR)
    output_weight = output_weight.reshape(D // 2, D)
    inner_weight = inner_weight.reshape(D, FF // 2)
    outer_weight = outer_weight.reshape(FF // 2, D)

    def core_sum(identifier, partial):
        (got,) = exchange(identifier, ("a2a", "core", partial.reshape(2, ROWS, D)))
        return got[0] + got[1]

    def core_pair(identifier, value):
        (got,) = exchange(identifier, ("ag", "core", value))
        return got.reshape(PAIR, D)

    branch = core_sum(2, dot(attended, output_weight, ((0,), (0,)))) + output_bias
    middle, unit_one, inverse_one = normalize(rows.astype(F32) + branch, norm_gain, norm_shift)
    middle_pair = core_pair(3, middle.astype(BF))
    inner = dot(middle_pair, inner_weight) + inner_bias
    active, gelu_pull = jax.vjp(gelu_exact, inner)
    active_low = active.astype(BF)
    outer = core_sum(4, dot(active_low, outer_weight)) + outer_bias
    result, unit_two, inverse_two = normalize(middle + outer, final_gain, final_shift)
    upstream = cotangent[0].astype(F32)
    grad_mid, grad_final_gain, grad_final_shift = normalize_back(
        upstream, unit_two, inverse_two, final_gain
    )
    grad_outer_low = grad_mid.astype(BF)
    grad_outer_bias = jnp.sum(grad_outer_low.astype(F32), axis=0)
    grad_outer_pair = core_pair(5, grad_outer_low)
    grad_outer_weight = dot(active_low, grad_outer_pair, ((0,), (0,))).astype(BF)
    grad_active = dot(grad_outer_pair, outer_weight, ((1,), (1,)))
    grad_inner_low = gelu_pull(grad_active)[0].astype(BF)
    grad_inner_weight = dot(middle_pair, grad_inner_low, ((0,), (0,))).astype(BF)
    grad_inner_bias = jnp.sum(grad_inner_low.astype(F32), axis=0)
    grad_middle = core_sum(6, dot(grad_inner_low, inner_weight, ((1,), (1,)))) + grad_mid
    grad_residual, grad_norm_gain, grad_norm_shift = normalize_back(
        grad_middle, unit_one, inverse_one, norm_gain
    )
    grad_branch_low = grad_residual.astype(BF)
    grad_output_bias = jnp.sum(grad_branch_low.astype(F32), axis=0)
    grad_branch_pair = core_pair(7, grad_branch_low)
    grad_output_weight = dot(attended, grad_branch_pair).astype(BF)
    grad_attended = dot(output_weight, grad_branch_pair, ((1,), (1,))).astype(BF)

    ignored, grad_qkv, output_terms, inner_terms, outer_terms = attend_backward(
        8,
        qkv_got,
        summed,
        stat,
        grad_attended.reshape(CHIPS, HD, PAIR),
        [
            ("a2a", "seq", grad_output_weight.reshape(SEQ, HD, D)),
            ("a2a", "seq", grad_inner_weight.reshape(SEQ, 128, FF // 2)),
            ("a2a", "seq", grad_outer_weight.reshape(SEQ, 256, D)),
        ],
    )
    grad_qkv = grad_qkv.reshape(SEQ * 3 * HD, PAIR)
    grad_qkv_weight = dot(rows_pair, grad_qkv, ((0,), (1,))).astype(BF)
    token_part = dot(grad_qkv, qkv_weight, ((0,), (1,)))
    grad_qkv_bias = jnp.sum(grad_qkv.astype(F32), axis=1).reshape(SEQ, 3, HD)

    vectors = jnp.concatenate(
        [
            jnp.stack(
                [
                    grad_output_bias,
                    grad_norm_gain,
                    grad_norm_shift,
                    grad_outer_bias,
                    grad_final_gain,
                    grad_final_shift,
                ]
            )
            .reshape(6, SEQ, 128)
            .transpose(1, 0, 2),
            jnp.concatenate([grad_qkv_bias[:, 0], grad_qkv_bias[:, 2]], axis=1)[:, None],
            grad_inner_bias.reshape(SEQ, 2, 128),
            jnp.zeros((SEQ, 7, 128), F32),
        ],
        axis=1,
    )
    qkv_terms, vector_terms, token_terms = exchange(
        9,
        ("a2a", "seq", grad_qkv_weight.reshape(SEQ, 128, SEQ * 3 * HD)),
        ("a2a", "seq", vectors),
        ("a2a", "core", token_part.reshape(2, ROWS, D)),
    )
    grad_tokens = grad_residual + token_terms[0] + token_terms[1]

    def total(terms):
        return jnp.sum(terms.astype(F32), axis=0).astype(BF).reshape(-1, D)

    shares = jnp.concatenate(
        [total(qkv_terms), total(output_terms), total(inner_terms), total(outer_terms)]
    )
    piece = shares.shape[0] // CHIPS
    share_terms, vector_all = exchange(
        10,
        ("a2a", "chip", shares.reshape(CHIPS, piece, D)),
        ("ag", "chip", jnp.sum(vector_terms, axis=0)),
    )
    own = jnp.sum(share_terms.astype(F32), axis=0).astype(BF)
    vector_own = jnp.sum(vector_all, axis=0)
    (own_all,) = exchange(11, ("ag", "chip", own))
    shares_both, vector_both = exchange(
        12, ("ag", "core", own_all.reshape(-1, D)), ("ag", "core", vector_own)
    )
    q_rows = 128 * SEQ * 3 * HD // D
    grad_qkv_all = shares_both[:, :q_rows].reshape(2, 128, SEQ, 3, HD).astype(F32)
    grad_qkv_all = grad_qkv_all.transpose(3, 1, 2, 0, 4).reshape(3, 128, D)
    at = q_rows
    grad_output_all = shares_both[:, at : at + HD].reshape(128, D).astype(F32)
    at += HD
    grad_inner_all = shares_both[:, at : at + 256].reshape(2, 128, SEQ, 256)
    grad_inner_all = grad_inner_all.transpose(1, 2, 0, 3).reshape(128, FF).astype(F32)
    at += 256
    grad_outer_all = shares_both[:, at : at + 256].reshape(512, D).astype(F32)
    whole = vector_both[0, :6] + vector_both[1, :6]
    grad_query_bias = vector_both[:, 6, :HD].reshape(128)
    grad_value_bias = vector_both[:, 6, HD:].reshape(128)
    grad_inner_bias = vector_both[:, 7:9].reshape(512)
    return (
        result.astype(BF)[None],
        grad_tokens[None],
        grad_qkv_all[0],
        grad_query_bias,
        grad_qkv_all[1],
        grad_qkv_all[2],
        grad_value_bias,
        grad_output_all,
        whole[0],
        whole[1],
        whole[2],
        grad_inner_all,
        grad_inner_bias,
        grad_outer_all,
        whole[3],
        whole[4],
        whole[5],
    )


def solution(mesh):
    row = P("seq", None)
    vector = P("seq")
    placed = P("seq", "ctx", None)
    return jax.shard_map(
        per_device,
        mesh=mesh,
        in_specs=(
            placed,
            placed,
            row,
            vector,
            row,
            row,
            vector,
            row,
            vector,
            vector,
            vector,
            row,
            vector,
            row,
            vector,
            vector,
            vector,
        ),
        out_specs=(
            placed,
            placed,
            row,
            vector,
            row,
            row,
            vector,
            row,
            vector,
            vector,
            vector,
            row,
            vector,
            row,
            vector,
            vector,
            vector,
        ),
        check_vma=False,
    )
```

```python
import functools
import math

import jax
import jax.numpy as jnp
from jax import lax
from jax.experimental import pallas as pl
from jax.experimental.pallas import tpu as pltpu
from jax.sharding import PartitionSpec as P

D = 1024
HEADS = 16
HD = 64
FF = 4096
SEQ = 8
CHIPS = 8
ROWS = 192
PAIR = 2 * ROWS
LENGTH = CHIPS * PAIR
SCALE2 = HD ** (-0.5) * math.log2(math.e)
BLOCK = 512
BF = jnp.bfloat16
F32 = jnp.float32
ANY = pl.BlockSpec(memory_space=pl.ANY)
VMEM = pl.BlockSpec(memory_space=pltpu.VMEM)


def dot(left, right, dims=((1,), (0,))):
    return lax.dot_general(left, right, (dims, ((), ())), preferred_element_type=F32)


def group_size(group):
    return 2 if group == "core" else 8


def group_me(group):
    if group == "seq":
        return lax.axis_index("seq")
    ctx = lax.axis_index("ctx")
    return lax.rem(ctx, 2) if group == "core" else lax.div(ctx, 2)


def group_device(group, index):
    seq, ctx = lax.axis_index("seq"), lax.axis_index("ctx")
    if group == "seq":
        return (index, ctx)
    if group == "chip":
        return (seq, index * 2 + lax.rem(ctx, 2))
    return (seq, lax.div(ctx, 2) * 2 + index)


def enter(groups):
    barrier = pltpu.get_barrier_semaphore()
    count = 0
    for group in groups:
        size, me = group_size(group), group_me(group)
        for step in range(1, size):
            pl.semaphore_signal(
                barrier,
                inc=1,
                device_id=group_device(group, lax.rem(me + step, size)),
                device_id_type=pl.DeviceIdType.MESH,
            )
            count += 1
    pl.semaphore_wait(barrier, count)


class Exchange:
    def __init__(self, kind, group, source, target, send, recv, own, own_held):
        self.kind, self.group = kind, group
        self.source, self.target = source, target
        self.send, self.recv, self.own, self.own_held = send, recv, own, own_held

    def copies(self):
        size, me = group_size(self.group), group_me(self.group)
        made = []
        for step in range(1, size):
            peer = lax.rem(me + step, size)
            piece = self.source if self.kind == "ag" else self.source.at[peer]
            made.append(
                pltpu.make_async_remote_copy(
                    src_ref=piece,
                    dst_ref=self.target.at[me],
                    send_sem=self.send.at[step - 1],
                    recv_sem=self.recv.at[step - 1],
                    device_id=group_device(self.group, peer),
                    device_id_type=pl.DeviceIdType.MESH,
                )
            )
        piece = self.source if self.kind == "ag" else self.source.at[me]
        own_in = pltpu.make_async_copy(piece, self.own_held, self.own.at[0])
        own_out = pltpu.make_async_copy(self.own_held, self.target.at[me], self.own.at[1])
        return made, own_in, own_out

    def start(self):
        made, own_in, own_out = self.copies()
        for copy in made:
            copy.start()
        own_in.start()

    def wait(self):
        made, own_in, own_out = self.copies()
        own_in.wait()
        own_out.start()
        own_out.wait()
        for copy in made:
            copy.wait()


def target_shape(kind, group, value):
    shape = value.shape if kind == "a2a" else (group_size(group),) + value.shape
    return jax.ShapeDtypeStruct(shape, value.dtype)


SCRATCH = 4


def scratch(kind, group, value):
    count = group_size(group) - 1
    return [
        pltpu.SemaphoreType.DMA((count,)),
        pltpu.SemaphoreType.DMA((count,)),
        pltpu.SemaphoreType.DMA((2,)),
        pltpu.VMEM(value.shape if kind == "ag" else value.shape[1:], value.dtype),
    ]


def exchange(identifier, *items):
    number = len(items)

    def kernel(*refs):
        enter(sorted({item[1] for item in items}))
        made = [
            Exchange(
                items[at][0],
                items[at][1],
                refs[at],
                refs[number + at],
                *refs[2 * number + SCRATCH * at : 2 * number + SCRATCH * (at + 1)],
            )
            for at in range(number)
        ]
        for one in made:
            one.start()
        for one in made:
            one.wait()

    return pl.pallas_call(
        kernel,
        out_shape=[target_shape(*item) for item in items],
        in_specs=[ANY] * number,
        out_specs=[ANY] * number,
        scratch_shapes=[ref for item in items for ref in scratch(*item)],
        compiler_params=pltpu.CompilerParams(
            collective_id=identifier, has_side_effects=True
        ),
        name="exchange%d" % identifier,
    )(*[item[2] for item in items])


def attend_forward(identifier, qkv, extra):
    number = len(extra)

    def kernel(*refs):
        qkv_ref, refs = refs[0], refs[1:]
        extra_in, refs = refs[:number], refs[number:]
        qkv_got, summed_ref, back_ref, stat_ref = refs[:4]
        extra_out, refs = refs[4 : 4 + number], refs[4 + number :]
        query_t, keys, value_t, low, refs = refs[0], refs[1], refs[2], refs[3], refs[4:]
        enter(sorted({"chip"} | {item[1] for item in extra}))
        first = Exchange("a2a", "chip", qkv_ref, qkv_got, *refs[:4])
        last = Exchange("a2a", "chip", low, back_ref, *refs[4:8])
        others = [
            Exchange(
                *extra[at][:2],
                extra_in[at],
                extra_out[at],
                *refs[8 + SCRATCH * at : 8 + SCRATCH * (at + 1)],
            )
            for at in range(number)
        ]
        first.start()
        for other in others:
            other.start()
        first.wait()
        for chip in range(CHIPS):
            at = pl.ds(chip * PAIR, PAIR)
            query_t[:, at] = qkv_got[chip, 0:HD, :]
            keys[at, :] = qkv_got[chip, HD : 2 * HD, :].astype(F32).T.astype(BF)
            value_t[:, at] = qkv_got[chip, 2 * HD : 3 * HD, :]

        def one_block(block, carry):
            at = pl.ds(pl.multiple_of(block * BLOCK, BLOCK), BLOCK)
            query = query_t[:, at]
            top = jnp.full((1, BLOCK), -1e30, F32)
            total = jnp.zeros((1, BLOCK), F32)
            summed = jnp.zeros((HD, BLOCK), F32)
            for part in range(LENGTH // BLOCK):
                here = slice(part * BLOCK, (part + 1) * BLOCK)
                scores = dot(keys[here, :], query) * SCALE2
                new_top = jnp.maximum(top, jnp.max(scores, axis=0, keepdims=True))
                factor = jnp.exp2(top - new_top)
                weights = jnp.exp2(scores - new_top)
                total = total * factor + jnp.sum(weights, axis=0, keepdims=True)
                summed = summed * factor + dot(value_t[:, here], weights.astype(BF))
                top = new_top
            summed_ref[:, at] = summed / total
            stat_ref[:, at] = top + jnp.log2(total)
            return carry

        lax.fori_loop(0, LENGTH // BLOCK, one_block, 0)
        for chip in range(CHIPS):
            low[chip] = summed_ref[:, chip * PAIR : (chip + 1) * PAIR].astype(BF)
        last.start()
        last.wait()
        for other in others:
            other.wait()

    return pl.pallas_call(
        kernel,
        out_shape=[
            jax.ShapeDtypeStruct((CHIPS, 3 * HD, PAIR), BF),
            jax.ShapeDtypeStruct((HD, LENGTH), F32),
            jax.ShapeDtypeStruct((CHIPS, HD, PAIR), BF),
            jax.ShapeDtypeStruct((1, LENGTH), F32),
        ]
        + [target_shape(*item) for item in extra],
        in_specs=[VMEM] + [ANY] * number,
        out_specs=[VMEM] * 4 + [ANY] * number,
        scratch_shapes=[
            pltpu.VMEM((HD, LENGTH), BF),
            pltpu.VMEM((LENGTH, HD), BF),
            pltpu.VMEM((HD, LENGTH), BF),
            pltpu.VMEM((CHIPS, HD, PAIR), BF),
        ]
        + scratch("a2a", "chip", qkv)
        + scratch("a2a", "chip", jax.ShapeDtypeStruct((CHIPS, HD, PAIR), BF))
        + [ref for item in extra for ref in scratch(*item)],
        compiler_params=pltpu.CompilerParams(
            collective_id=identifier,
            has_side_effects=True,
            vmem_limit_bytes=40 * 1024 * 1024,
        ),
        name="attend_forward",
    )(qkv, *[item[2] for item in extra])


def attend_backward(identifier, qkv_got, summed, stat, grad, extra):
    number = len(extra)

    def kernel(*refs):
        qkv_ref, summed_ref, stat_ref, grad_ref, refs = *refs[:4], refs[4:]
        extra_in, refs = refs[:number], refs[number:]
        grad_got, back_ref, refs = refs[0], refs[1], refs[2:]
        extra_out, refs = refs[:number], refs[number:]
        query_t, queries, key_t, keys, values, up_t, ups, delta_ref = refs[:8]
        grad_query, grad_key, grad_value, low, refs = *refs[8:12], refs[12:]
        enter(sorted({"chip"} | {item[1] for item in extra}))
        first = Exchange("a2a", "chip", grad_ref, grad_got, *refs[:4])
        last = Exchange("a2a", "chip", low, back_ref, *refs[4:8])
        others = [
            Exchange(
                *extra[at][:2],
                extra_in[at],
                extra_out[at],
                *refs[8 + SCRATCH * at : 8 + SCRATCH * (at + 1)],
            )
            for at in range(number)
        ]
        first.start()
        for other in others:
            other.start()
        for chip in range(CHIPS):
            at = pl.ds(chip * PAIR, PAIR)
            query_t[:, at] = qkv_ref[chip, 0:HD, :]
            queries[at, :] = qkv_ref[chip, 0:HD, :].astype(F32).T.astype(BF)
            key_t[:, at] = qkv_ref[chip, HD : 2 * HD, :]
            keys[at, :] = qkv_ref[chip, HD : 2 * HD, :].astype(F32).T.astype(BF)
            values[at, :] = qkv_ref[chip, 2 * HD : 3 * HD, :].astype(F32).T.astype(BF)
        grad_key[...] = jnp.zeros_like(grad_key)
        grad_value[...] = jnp.zeros_like(grad_value)
        first.wait()
        for chip in range(CHIPS):
            at = pl.ds(chip * PAIR, PAIR)
            up = grad_got[chip].astype(F32)
            up_t[:, at] = grad_got[chip]
            ups[at, :] = up.T.astype(BF)
            delta_ref[:, at] = jnp.sum(up * summed_ref[:, at], axis=0, keepdims=True)

        def one_block(block, carry):
            at = pl.ds(pl.multiple_of(block * BLOCK, BLOCK), BLOCK)
            query, up = query_t[:, at], up_t[:, at]
            query_rows, up_rows = queries[at, :], ups[at, :]
            stat, delta = stat_ref[:, at], delta_ref[:, at]
            gathered = jnp.zeros((HD, BLOCK), F32)
            for part in range(LENGTH // BLOCK):
                here = slice(part * BLOCK, (part + 1) * BLOCK)
                scores = dot(keys[here, :], query) * SCALE2
                probs = jnp.exp2(scores - stat)
                grad_value[here, :] += dot(probs.astype(BF), up_rows)
                slope = dot(values[here, :], up) - delta
                grad_scores = (probs * slope).astype(BF)
                grad_key[here, :] += dot(grad_scores, query_rows)
                gathered += dot(key_t[:, here], grad_scores)
            grad_query[:, at] = gathered
            return carry

        lax.fori_loop(0, LENGTH // BLOCK, one_block, 0)
        scale = HD ** (-0.5)
        for chip in range(CHIPS):
            at = slice(chip * PAIR, (chip + 1) * PAIR)
            low[chip, 0:HD, :] = (grad_query[:, at] * scale).astype(BF)
            low[chip, HD : 2 * HD, :] = (grad_key[at, :] * scale).T.astype(BF)
            low[chip, 2 * HD : 3 * HD, :] = grad_value[at, :].T.astype(BF)
        last.start()
        last.wait()
        for other in others:
            other.wait()

    return pl.pallas_call(
        kernel,
        out_shape=[
            jax.ShapeDtypeStruct((CHIPS, HD, PAIR), BF),
            jax.ShapeDtypeStruct((CHIPS, 3 * HD, PAIR), BF),
        ]
        + [target_shape(*item) for item in extra],
        in_specs=[VMEM] * 4 + [ANY] * number,
        out_specs=[VMEM] * 2 + [ANY] * number,
        scratch_shapes=[
            pltpu.VMEM((HD, LENGTH), BF),
            pltpu.VMEM((LENGTH, HD), BF),
            pltpu.VMEM((HD, LENGTH), BF),
            pltpu.VMEM((LENGTH, HD), BF),
            pltpu.VMEM((LENGTH, HD), BF),
            pltpu.VMEM((HD, LENGTH), BF),
            pltpu.VMEM((LENGTH, HD), BF),
            pltpu.VMEM((1, LENGTH), F32),
            pltpu.VMEM((HD, LENGTH), F32),
            pltpu.VMEM((LENGTH, HD), F32),
            pltpu.VMEM((LENGTH, HD), F32),
            pltpu.VMEM((CHIPS, 3 * HD, PAIR), BF),
        ]
        + scratch("a2a", "chip", grad)
        + scratch("a2a", "chip", qkv_got)
        + [ref for item in extra for ref in scratch(*item)],
        compiler_params=pltpu.CompilerParams(
            collective_id=identifier,
            has_side_effects=True,
            vmem_limit_bytes=44 * 1024 * 1024,
        ),
        name="attend_backward",
    )(qkv_got, summed, stat, grad, *[item[2] for item in extra])


def normalize(hidden, gain, shift):
    centered = hidden - jnp.mean(hidden, axis=-1, keepdims=True)
    inverse = lax.rsqrt(jnp.mean(centered * centered, axis=-1, keepdims=True) + 1e-05)
    normed = centered * inverse
    return (normed * gain + shift, normed, inverse)


def normalize_back(upstream, normed, inverse, gain):
    scaled = upstream * gain
    inner = (
        scaled
        - jnp.mean(scaled, axis=-1, keepdims=True)
        - normed * jnp.mean(scaled * normed, axis=-1, keepdims=True)
    )
    return (inverse * inner, jnp.sum(upstream * normed, axis=0), jnp.sum(upstream, axis=0))


def gelu_exact(value):
    return jax.nn.gelu(value, approximate=False)


def per_device(
    tokens,
    cotangent,
    w_query,
    b_query,
    w_key,
    w_value,
    b_value,
    w_output,
    b_output,
    first_gain,
    first_shift,
    w_inner,
    b_inner,
    w_outer,
    b_outer,
    second_gain,
    second_shift,
):
    core = lax.rem(lax.axis_index("ctx"), 2)
    rows = tokens[0]

    def pick(value, axis):
        return lax.dynamic_index_in_dim(value, core, axis, keepdims=False)

    qkv_part = pick(
        jnp.stack([w_query, w_key, w_value]).reshape(3, 128, SEQ, 2, HD), 3
    )
    qkv_part = jnp.transpose(qkv_part, (1, 2, 0, 3)).reshape(128, SEQ * 3 * HD)
    output_part = pick(w_output.reshape(2, HD, D), 0)
    inner_part = pick(w_inner.reshape(128, SEQ, 2, 256), 2).reshape(128, FF // 2)
    outer_part = pick(w_outer.reshape(2, 256, D), 0)
    small_part = jnp.concatenate(
        [
            jnp.stack(
                [b_query, b_value, b_output, first_gain, first_shift, b_outer, second_gain, second_shift]
            ),
            b_inner.reshape(4, 128),
            jnp.zeros((4, 128), BF),
        ]
    )
    qkv_weight, small, rows_pair = exchange(
        0, ("ag", "seq", qkv_part), ("ag", "seq", small_part), ("ag", "core", rows)
    )
    qkv_weight = qkv_weight.reshape(D, SEQ * 3 * HD)
    rows_pair = rows_pair.reshape(PAIR, D)
    small = small.astype(F32)
    query_bias = pick(small[:, 0].reshape(SEQ, 2, HD), 1)
    value_bias = pick(small[:, 1].reshape(SEQ, 2, HD), 1)
    qkv_bias = jnp.stack([query_bias, jnp.zeros_like(query_bias), value_bias], axis=1)
    output_bias, norm_gain, norm_shift, outer_bias, final_gain, final_shift = (
        small[:, at].reshape(D) for at in range(2, 8)
    )
    inner_bias = pick(small[:, 8:12].reshape(SEQ, 2, 256), 1).reshape(FF // 2)

    qkv = (dot(qkv_weight, rows_pair, ((0,), (1,))) + qkv_bias.reshape(-1, 1)).astype(BF)
    qkv_got, summed, attended, stat, output_weight, inner_weight, outer_weight = attend_forward(
        1,
        qkv.reshape(CHIPS, 3 * HD, PAIR),
        [("ag", "seq", output_part), ("ag", "seq", inner_part), ("ag", "seq", outer_part)],
    )
    attended = attended.reshape(D // 2, PAIR)
    output_weight = output_weight.reshape(D // 2, D)
    inner_weight = inner_weight.reshape(D, FF // 2)
    outer_weight = outer_weight.reshape(FF // 2, D)

    def core_sum(identifier, partial):
        (got,) = exchange(identifier, ("a2a", "core", partial.reshape(2, ROWS, D)))
        return got[0] + got[1]

    def core_pair(identifier, value):
        (got,) = exchange(identifier, ("ag", "core", value))
        return got.reshape(PAIR, D)

    branch = core_sum(2, dot(attended, output_weight, ((0,), (0,)))) + output_bias
    middle, unit_one, inverse_one = normalize(rows.astype(F32) + branch, norm_gain, norm_shift)
    middle_pair = core_pair(3, middle.astype(BF))
    inner = dot(middle_pair, inner_weight) + inner_bias
    active, gelu_pull = jax.vjp(gelu_exact, inner)
    active_low = active.astype(BF)
    outer = core_sum(4, dot(active_low, outer_weight)) + outer_bias
    result, unit_two, inverse_two = normalize(middle + outer, final_gain, final_shift)
    upstream = cotangent[0].astype(F32)
    grad_mid, grad_final_gain, grad_final_shift = normalize_back(
        upstream, unit_two, inverse_two, final_gain
    )
    grad_outer_low = grad_mid.astype(BF)
    grad_outer_bias = jnp.sum(grad_outer_low.astype(F32), axis=0)
    grad_outer_pair = core_pair(5, grad_outer_low)
    grad_outer_weight = dot(active_low, grad_outer_pair, ((0,), (0,))).astype(BF)
    grad_active = dot(grad_outer_pair, outer_weight, ((1,), (1,)))
    grad_inner_low = gelu_pull(grad_active)[0].astype(BF)
    grad_inner_weight = dot(middle_pair, grad_inner_low, ((0,), (0,))).astype(BF)
    grad_inner_bias = jnp.sum(grad_inner_low.astype(F32), axis=0)
    grad_middle = core_sum(6, dot(grad_inner_low, inner_weight, ((1,), (1,)))) + grad_mid
    grad_residual, grad_norm_gain, grad_norm_shift = normalize_back(
        grad_middle, unit_one, inverse_one, norm_gain
    )
    grad_branch_low = grad_residual.astype(BF)
    grad_output_bias = jnp.sum(grad_branch_low.astype(F32), axis=0)
    grad_branch_pair = core_pair(7, grad_branch_low)
    grad_output_weight = dot(attended, grad_branch_pair).astype(BF)
    grad_attended = dot(output_weight, grad_branch_pair, ((1,), (1,))).astype(BF)

    ignored, grad_qkv, output_terms, inner_terms, outer_terms = attend_backward(
        8,
        qkv_got,
        summed,
        stat,
        grad_attended.reshape(CHIPS, HD, PAIR),
        [
            ("a2a", "seq", grad_output_weight.reshape(SEQ, HD, D)),
            ("a2a", "seq", grad_inner_weight.reshape(SEQ, 128, FF // 2)),
            ("a2a", "seq", grad_outer_weight.reshape(SEQ, 256, D)),
        ],
    )
    grad_qkv = grad_qkv.reshape(SEQ * 3 * HD, PAIR)
    grad_qkv_weight = dot(rows_pair, grad_qkv, ((0,), (1,))).astype(BF)
    token_part = dot(grad_qkv, qkv_weight, ((0,), (1,)))
    grad_qkv_bias = jnp.sum(grad_qkv.astype(F32), axis=1).reshape(SEQ, 3, HD)

    vectors = jnp.concatenate(
        [
            jnp.stack(
                [
                    grad_output_bias,
                    grad_norm_gain,
                    grad_norm_shift,
                    grad_outer_bias,
                    grad_final_gain,
                    grad_final_shift,
                ]
            )
            .reshape(6, SEQ, 128)
            .transpose(1, 0, 2),
            jnp.concatenate([grad_qkv_bias[:, 0], grad_qkv_bias[:, 2]], axis=1)[:, None],
            grad_inner_bias.reshape(SEQ, 2, 128),
            jnp.zeros((SEQ, 7, 128), F32),
        ],
        axis=1,
    )
    qkv_terms, vector_terms, token_terms = exchange(
        9,
        ("a2a", "seq", grad_qkv_weight.reshape(SEQ, 128, SEQ * 3 * HD)),
        ("a2a", "seq", vectors),
        ("a2a", "core", token_part.reshape(2, ROWS, D)),
    )
    grad_tokens = grad_residual + token_terms[0] + token_terms[1]

    def total(terms):
        return jnp.sum(terms.astype(F32), axis=0).astype(BF).reshape(-1, D)

    shares = jnp.concatenate(
        [total(qkv_terms), total(output_terms), total(inner_terms), total(outer_terms)]
    )
    piece = shares.shape[0] // CHIPS
    share_terms, vector_all = exchange(
        10,
        ("a2a", "chip", shares.reshape(CHIPS, piece, D)),
        ("ag", "chip", jnp.sum(vector_terms, axis=0)),
    )
    own = jnp.sum(share_terms.astype(F32), axis=0).astype(BF)
    vector_own = jnp.sum(vector_all, axis=0)
    (own_all,) = exchange(11, ("ag", "chip", own))
    shares_both, vector_both = exchange(
        12, ("ag", "core", own_all.reshape(-1, D)), ("ag", "core", vector_own)
    )
    q_rows = 128 * SEQ * 3 * HD // D
    grad_qkv_all = shares_both[:, :q_rows].reshape(2, 128, SEQ, 3, HD).astype(F32)
    grad_qkv_all = grad_qkv_all.transpose(3, 1, 2, 0, 4).reshape(3, 128, D)
    at = q_rows
    grad_output_all = shares_both[:, at : at + HD].reshape(128, D).astype(F32)
    at += HD
    grad_inner_all = shares_both[:, at : at + 256].reshape(2, 128, SEQ, 256)
    grad_inner_all = grad_inner_all.transpose(1, 2, 0, 3).reshape(128, FF).astype(F32)
    at += 256
    grad_outer_all = shares_both[:, at : at + 256].reshape(512, D).astype(F32)
    whole = vector_both[0, :6] + vector_both[1, :6]
    grad_query_bias = vector_both[:, 6, :HD].reshape(128)
    grad_value_bias = vector_both[:, 6, HD:].reshape(128)
    grad_inner_bias = vector_both[:, 7:9].reshape(512)
    return (
        result.astype(BF)[None],
        grad_tokens[None],
        grad_qkv_all[0],
        grad_query_bias,
        grad_qkv_all[1],
        grad_qkv_all[2],
        grad_value_bias,
        grad_output_all,
        whole[0],
        whole[1],
        whole[2],
        grad_inner_all,
        grad_inner_bias,
        grad_outer_all,
        whole[3],
        whole[4],
        whole[5],
    )


def solution(mesh):
    row = P("seq", None)
    vector = P("seq")
    placed = P("seq", "ctx", None)
    return jax.shard_map(
        per_device,
        mesh=mesh,
        in_specs=(
            placed,
            placed,
            row,
            vector,
            row,
            row,
            vector,
            row,
            vector,
            vector,
            vector,
            row,
            vector,
            row,
            vector,
            vector,
            vector,
        ),
        out_specs=(
            placed,
            placed,
            row,
            vector,
            row,
            row,
            vector,
            row,
            vector,
            vector,
            vector,
            row,
            vector,
            row,
            vector,
            vector,
            vector,
        ),
        check_vma=False,
    )
```

```python
import functools
import math

import jax
import jax.numpy as jnp
from jax import lax
from jax.experimental import pallas as pl
from jax.experimental.pallas import tpu as pltpu
from jax.sharding import PartitionSpec as P

D = 1024
HEADS = 16
HD = 64
FF = 4096
SEQ = 8
CHIPS = 8
ROWS = 192
PAIR = 2 * ROWS
LENGTH = CHIPS * PAIR
SCALE2 = HD ** (-0.5) * math.log2(math.e)
BLOCK = 512
BF = jnp.bfloat16
F32 = jnp.float32
ANY = pl.BlockSpec(memory_space=pl.ANY)
VMEM = pl.BlockSpec(memory_space=pltpu.VMEM)


def dot(left, right, dims=((1,), (0,))):
    return lax.dot_general(left, right, (dims, ((), ())), preferred_element_type=F32)


SIZES = {"seq": 8, "chip": 8, "z": 4, "half": 2, "core": 2}


def group_size(group):
    return SIZES[group]


def group_me(group):
    if group == "seq":
        return lax.axis_index("seq")
    ctx = lax.axis_index("ctx")
    if group == "core":
        return lax.rem(ctx, 2)
    if group == "half":
        return lax.div(ctx, 8)
    if group == "z":
        return lax.rem(lax.div(ctx, 2), 4)
    return lax.div(ctx, 2)


def group_device(group, index):
    seq, ctx = lax.axis_index("seq"), lax.axis_index("ctx")
    if group == "seq":
        return (index, ctx)
    if group == "core":
        return (seq, lax.div(ctx, 2) * 2 + index)
    if group == "half":
        return (seq, index * 8 + lax.rem(ctx, 8))
    if group == "z":
        return (seq, lax.div(ctx, 8) * 8 + index * 2 + lax.rem(ctx, 2))
    return (seq, index * 2 + lax.rem(ctx, 2))


def group_peer(group, step):
    return lax.rem(group_me(group) + step, group_size(group))


def enter(groups):
    barrier = pltpu.get_barrier_semaphore()
    count = 0
    for group in groups:
        for step in range(1, group_size(group)):
            pl.semaphore_signal(
                barrier,
                inc=1,
                device_id=group_device(group, group_peer(group, step)),
                device_id_type=pl.DeviceIdType.MESH,
            )
            count += 1
    pl.semaphore_wait(barrier, count)


def remote(source, target, send, recv, group, peer):
    return pltpu.make_async_remote_copy(
        src_ref=source,
        dst_ref=target,
        send_sem=send,
        recv_sem=recv,
        device_id=group_device(group, peer),
        device_id_type=pl.DeviceIdType.MESH,
    )


def dma(*shape):
    return pltpu.SemaphoreType.DMA(shape)


class Exchange:
    def __init__(self, kind, group, source, target, refs, rows=None):
        self.kind, self.group = kind, group
        self.source, self.target, self.rows = source, target, rows
        self.send, self.recv = refs[:2]
        if rows is None:
            self.own, self.own_held = refs[2:]

    @staticmethod
    def scratch(kind, group, value, rows=None):
        count = group_size(group) - 1
        if rows is not None:
            return [dma(count), dma(count)]
        piece = value.shape if kind == "ag" else value.shape[1:]
        return [dma(count), dma(count), dma(2), pltpu.VMEM(piece, value.dtype)]

    def copies(self):
        me = group_me(self.group)
        made = []
        for step in range(1, group_size(self.group)):
            peer = group_peer(self.group, step)
            piece = self.source if self.kind == "ag" else self.source.at[peer]
            target = self.target.at[me]
            if self.rows is not None:
                piece, target = piece.at[pl.ds(*self.rows)], target.at[pl.ds(*self.rows)]
            made.append(
                remote(piece, target, self.send.at[step - 1], self.recv.at[step - 1], self.group, peer)
            )
        return made

    def own_copies(self):
        me = group_me(self.group)
        piece = self.source if self.kind == "ag" else self.source.at[me]
        return (
            pltpu.make_async_copy(piece, self.own_held, self.own.at[0]),
            pltpu.make_async_copy(self.own_held, self.target.at[me], self.own.at[1]),
        )

    def start(self):
        for copy in self.copies():
            copy.start()
        if self.rows is None:
            self.own_copies()[0].start()

    def wait(self):
        if self.rows is None:
            own_in, own_out = self.own_copies()
            own_in.wait()
            own_out.start()
            own_out.wait()
        for copy in self.copies():
            copy.wait()


class Own:
    def __init__(self, source, target, refs):
        self.source, self.target = source, target.at[group_me("seq")]
        self.sems, self.held = refs

    @staticmethod
    def scratch(value):
        return [dma(2), pltpu.VMEM(value.shape, value.dtype)]

    def start(self):
        pltpu.make_async_copy(self.source, self.held, self.sems.at[0]).start()

    def wait(self):
        pltpu.make_async_copy(self.source, self.held, self.sems.at[0]).wait()
        copy = pltpu.make_async_copy(self.held, self.target, self.sems.at[1])
        copy.start()
        copy.wait()


class SplitGather:
    def __init__(self, source, target, rows, refs):
        self.source, self.target, self.base = source, target, rows[0]
        self.quarter = rows[1] // 4
        self.send, self.recv, self.send_z, self.recv_z = refs

    @staticmethod
    def scratch():
        return [dma(7), dma(7), dma(21), dma(21)]

    def span(self):
        start = pl.multiple_of(self.base + group_me("z") * self.quarter, 16)
        return pl.ds(start, self.quarter)

    def first(self, step):
        span = self.span()
        return remote(
            self.source.at[span],
            self.target.at[group_me("seq"), span],
            self.send.at[step - 1],
            self.recv.at[step - 1],
            "seq",
            group_peer("seq", step),
        )

    def second(self, step, hop):
        owner, span, at = group_peer("seq", 8 - step), self.span(), (step - 1) * 3 + hop - 1
        piece = self.target.at[owner, span]
        return remote(
            piece, piece, self.send_z.at[at], self.recv_z.at[at], "z", group_peer("z", hop)
        )

    def start(self):
        for step in range(1, 8):
            self.first(step).start()

    def forward(self):
        for step in range(1, 8):
            self.first(step).wait_recv()
            for hop in range(1, 4):
                self.second(step, hop).start()

    def wait(self):
        for step in range(1, 8):
            self.first(step).wait_send()
            for hop in range(1, 4):
                self.second(step, hop).wait()


class Reduce:
    def __init__(self, source, rows, refs):
        self.source, self.span = source, pl.ds(*rows)
        self.send, self.recv, self.local, self.got, self.own = refs

    @staticmethod
    def scratch(value, rows):
        piece = (rows[1], value.shape[2])
        return [dma(7), dma(7), dma(), pltpu.VMEM((7,) + piece, BF), pltpu.VMEM(piece, BF)]

    def copies(self):
        return [
            remote(
                self.source.at[group_peer("seq", step), self.span],
                self.got.at[step - 1],
                self.send.at[step - 1],
                self.recv.at[step - 1],
                "seq",
                group_peer("seq", step),
            )
            for step in range(1, 8)
        ]

    def own_copy(self):
        return pltpu.make_async_copy(
            self.source.at[group_me("seq"), self.span], self.own, self.local
        )

    def start(self):
        for copy in self.copies():
            copy.start()
        self.own_copy().start()

    def wait(self, out):
        self.own_copy().wait()
        for copy in self.copies():
            copy.wait()
        out[...] = sum((self.got[at].astype(F32) for at in range(7)), self.own[...].astype(F32)).astype(BF)


class SplitReduce:
    def __init__(self, source, rows, refs):
        self.source, self.base, self.quarter = source, rows[0], rows[1] // 4
        self.send_z, self.recv_z, self.send, self.recv, self.local = refs[:5]
        self.got_z, self.total, self.got = refs[5:]

    @staticmethod
    def scratch(value, rows):
        piece = (rows[1] // 4, value.shape[2])
        return [dma(3), dma(3), dma(7), dma(7), dma()] + [
            pltpu.VMEM(lead + piece, BF) for lead in ((3, 8), (8,), (7,))
        ]

    def part(self, index):
        start = pl.multiple_of(self.base + index * self.quarter, 16)
        return self.source.at[:, pl.ds(start, self.quarter)]

    def first(self, hop):
        peer = group_peer("z", hop)
        return remote(
            self.part(peer), self.got_z.at[hop - 1], self.send_z.at[hop - 1], self.recv_z.at[hop - 1], "z", peer
        )

    def own_copy(self):
        return pltpu.make_async_copy(self.part(group_me("z")), self.total, self.local)

    def second(self, step):
        peer = group_peer("seq", step)
        return remote(
            self.total.at[peer], self.got.at[step - 1], self.send.at[step - 1], self.recv.at[step - 1], "seq", peer
        )

    def start(self):
        for hop in range(1, 4):
            self.first(hop).start()
        self.own_copy().start()

    def forward(self):
        self.own_copy().wait()
        for hop in range(1, 4):
            self.first(hop).wait()

        def add(at, carry):
            value = self.total[at].astype(F32)
            for hop in range(3):
                value += self.got_z[hop, at].astype(F32)
            self.total[at] = value.astype(BF)
            return carry

        lax.fori_loop(0, 8, add, 0)
        for step in range(1, 8):
            self.second(step).start()

    def wait(self, out):
        for step in range(1, 8):
            self.second(step).wait()
        out[...] = sum(
            (self.got[at].astype(F32) for at in range(7)), self.total[group_me("seq")].astype(F32)
        ).astype(BF)


class Refs:
    def __init__(self, refs):
        self.refs, self.at = refs, 0

    def take(self, count):
        self.at += count
        return self.refs[self.at - count : self.at]

    def left(self):
        return self.refs[self.at :]


def target_shape(kind, group, value):
    shape = value.shape if kind == "a2a" else (group_size(group),) + value.shape
    return jax.ShapeDtypeStruct(shape, value.dtype)


def params(identifier, mebibytes):
    return pltpu.CompilerParams(
        collective_id=identifier,
        has_side_effects=True,
        vmem_limit_bytes=mebibytes * 1024 * 1024,
    )


def exchange(identifier, *items):
    number = len(items)

    def kernel(*refs):
        refs = Refs(refs)
        sources, targets = refs.take(number), refs.take(number)
        enter(sorted({item[1] for item in items}))
        made = [
            Exchange(item[0], item[1], source, target, refs.take(4))
            for item, source, target in zip(items, sources, targets)
        ]
        for one in made:
            one.start()
        for one in made:
            one.wait()

    return pl.pallas_call(
        kernel,
        out_shape=[target_shape(*item) for item in items],
        in_specs=[ANY] * number,
        out_specs=[ANY] * number,
        scratch_shapes=[ref for item in items for ref in Exchange.scratch(*item)],
        compiler_params=params(identifier, 16),
        name="exchange%d" % identifier,
    )(*[item[2] for item in items])


def gather_first(identifier, qkv, small, rows):
    half = qkv.shape[0] // 2

    def kernel(*refs):
        refs = Refs(refs)
        qkv_ref, small_ref, rows_ref = refs.take(3)
        qkv_out, small_out, rows_out = refs.take(3)
        enter(["seq", "z", "core"])
        split = SplitGather(qkv_ref, qkv_out, (0, half), refs.take(4))
        direct = Exchange("ag", "seq", qkv_ref, qkv_out, refs.take(2), rows=(half, half))
        own = Own(qkv_ref, qkv_out, refs.take(2))
        smalls = Exchange("ag", "seq", small_ref, small_out, refs.take(4))
        pair = Exchange("ag", "core", rows_ref, rows_out, refs.take(4))
        split.start()
        for one in (direct, own, smalls, pair):
            one.start()
        split.forward()
        for one in (pair, own, smalls, direct, split):
            one.wait()

    return pl.pallas_call(
        kernel,
        out_shape=[
            target_shape("ag", "seq", qkv),
            target_shape("ag", "seq", small),
            target_shape("ag", "core", rows),
        ],
        in_specs=[ANY] * 3,
        out_specs=[ANY] * 3,
        scratch_shapes=SplitGather.scratch()
        + Exchange.scratch("ag", "seq", qkv, (half, half))
        + Own.scratch(qkv)
        + Exchange.scratch("ag", "seq", small)
        + Exchange.scratch("ag", "core", rows),
        compiler_params=params(identifier, 16),
        name="gather_first",
    )(qkv, small, rows)


def attend_forward(identifier, qkv, output_part, inner_part, outer_part):
    low_shape = jax.ShapeDtypeStruct((CHIPS, HD, PAIR), BF)

    def kernel(*refs):
        refs = Refs(refs)
        qkv_ref, output_ref, inner_ref, outer_ref = refs.take(4)
        qkv_got, summed_ref, back_ref, stat_ref = refs.take(4)
        output_out, inner_out, outer_out = refs.take(3)
        query_t, keys, value_t, low = refs.take(4)
        enter(["seq", "chip"])
        first = Exchange("a2a", "chip", qkv_ref, qkv_got, refs.take(4))
        last = Exchange("a2a", "chip", low, back_ref, refs.take(4))
        inner = SplitGather(inner_ref, inner_out, (0, inner_part.shape[0]), refs.take(4))
        inner_own = Own(inner_ref, inner_out, refs.take(2))
        output = Exchange("ag", "seq", output_ref, output_out, refs.take(4))
        outer = Exchange("ag", "seq", outer_ref, outer_out, refs.take(4))
        first.start()
        inner.start()
        inner_own.start()
        output.start()
        first.wait()
        inner.forward()
        outer.start()
        for chip in range(CHIPS):
            at = pl.ds(chip * PAIR, PAIR)
            query_t[:, at] = qkv_got[chip, 0:HD, :]
            keys[at, :] = qkv_got[chip, HD : 2 * HD, :].astype(F32).T.astype(BF)
            value_t[:, at] = qkv_got[chip, 2 * HD : 3 * HD, :]

        def one_block(block, carry):
            at = pl.ds(pl.multiple_of(block * BLOCK, BLOCK), BLOCK)
            query = query_t[:, at]
            top = jnp.full((1, BLOCK), -1e30, F32)
            total = jnp.zeros((1, BLOCK), F32)
            summed = jnp.zeros((HD, BLOCK), F32)
            for part in range(LENGTH // BLOCK):
                here = slice(part * BLOCK, (part + 1) * BLOCK)
                scores = dot(keys[here, :], query) * SCALE2
                new_top = jnp.maximum(top, jnp.max(scores, axis=0, keepdims=True))
                factor = jnp.exp2(top - new_top)
                weights = jnp.exp2(scores - new_top)
                total = total * factor + jnp.sum(weights, axis=0, keepdims=True)
                summed = summed * factor + dot(value_t[:, here], weights.astype(BF))
                top = new_top
            summed_ref[:, at] = summed / total
            stat_ref[:, at] = top + jnp.log2(total)
            return carry

        lax.fori_loop(0, LENGTH // BLOCK, one_block, 0)
        for chip in range(CHIPS):
            low[chip] = summed_ref[:, chip * PAIR : (chip + 1) * PAIR].astype(BF)
        last.start()
        for one in (last, output, inner_own, inner, outer):
            one.wait()

    return pl.pallas_call(
        kernel,
        out_shape=[
            jax.ShapeDtypeStruct(qkv.shape, BF),
            jax.ShapeDtypeStruct((HD, LENGTH), F32),
            low_shape,
            jax.ShapeDtypeStruct((1, LENGTH), F32),
        ]
        + [target_shape("ag", "seq", part) for part in (output_part, inner_part, outer_part)],
        in_specs=[VMEM] + [ANY] * 3,
        out_specs=[VMEM] * 4 + [ANY] * 3,
        scratch_shapes=[
            pltpu.VMEM((HD, LENGTH), BF),
            pltpu.VMEM((LENGTH, HD), BF),
            pltpu.VMEM((HD, LENGTH), BF),
            pltpu.VMEM((CHIPS, HD, PAIR), BF),
        ]
        + Exchange.scratch("a2a", "chip", qkv)
        + Exchange.scratch("a2a", "chip", low_shape)
        + SplitGather.scratch()
        + Own.scratch(inner_part)
        + Exchange.scratch("ag", "seq", output_part)
        + Exchange.scratch("ag", "seq", outer_part),
        compiler_params=params(identifier, 40),
        name="attend_forward",
    )(qkv, output_part, inner_part, outer_part)


def attend_backward(identifier, qkv_got, summed, stat, grad, output_grad, inner_grad, outer_grad):
    def kernel(*refs):
        refs = Refs(refs)
        qkv_ref, summed_ref, stat_ref, grad_ref = refs.take(4)
        output_ref, inner_ref, outer_ref = refs.take(3)
        grad_got, back_ref, output_out, inner_out, outer_out = refs.take(5)
        query_t, queries, key_t, keys, values, up_t, ups, delta_ref = refs.take(8)
        grad_query, grad_key, grad_value, low = refs.take(4)
        enter(["seq", "chip"])
        first = Exchange("a2a", "chip", grad_ref, grad_got, refs.take(4))
        last = Exchange("a2a", "chip", low, back_ref, refs.take(4))
        inner = SplitReduce(inner_ref, (0, 128), refs.take(8))
        output = Reduce(output_ref, (0, HD), refs.take(5))
        outer = Reduce(outer_ref, (0, 256), refs.take(5))
        first.start()
        inner.start()
        output.start()
        outer.start()
        for chip in range(CHIPS):
            at = pl.ds(chip * PAIR, PAIR)
            query_t[:, at] = qkv_ref[chip, 0:HD, :]
            queries[at, :] = qkv_ref[chip, 0:HD, :].astype(F32).T.astype(BF)
            key_t[:, at] = qkv_ref[chip, HD : 2 * HD, :]
            keys[at, :] = qkv_ref[chip, HD : 2 * HD, :].astype(F32).T.astype(BF)
            values[at, :] = qkv_ref[chip, 2 * HD : 3 * HD, :].astype(F32).T.astype(BF)
        grad_key[...] = jnp.zeros_like(grad_key)
        grad_value[...] = jnp.zeros_like(grad_value)
        first.wait()
        for chip in range(CHIPS):
            at = pl.ds(chip * PAIR, PAIR)
            up = grad_got[chip].astype(F32)
            up_t[:, at] = grad_got[chip]
            ups[at, :] = up.T.astype(BF)
            delta_ref[:, at] = jnp.sum(up * summed_ref[:, at], axis=0, keepdims=True)

        def one_block(block, carry):
            at = pl.ds(pl.multiple_of(block * BLOCK, BLOCK), BLOCK)
            query, up = query_t[:, at], up_t[:, at]
            query_rows, up_rows = queries[at, :], ups[at, :]
            stat, delta = stat_ref[:, at], delta_ref[:, at]
            gathered = jnp.zeros((HD, BLOCK), F32)
            for part in range(LENGTH // BLOCK):
                here = slice(part * BLOCK, (part + 1) * BLOCK)
                scores = dot(keys[here, :], query) * SCALE2
                probs = jnp.exp2(scores - stat)
                grad_value[here, :] += dot(probs.astype(BF), up_rows)
                slope = dot(values[here, :], up) - delta
                grad_scores = (probs * slope).astype(BF)
                grad_key[here, :] += dot(grad_scores, query_rows)
                gathered += dot(key_t[:, here], grad_scores)
            grad_query[:, at] = gathered
            return carry

        lax.fori_loop(0, LENGTH // BLOCK, one_block, 0)
        scale = HD ** (-0.5)
        for chip in range(CHIPS):
            at = slice(chip * PAIR, (chip + 1) * PAIR)
            low[chip, 0:HD, :] = (grad_query[:, at] * scale).astype(BF)
            low[chip, HD : 2 * HD, :] = (grad_key[at, :] * scale).T.astype(BF)
            low[chip, 2 * HD : 3 * HD, :] = grad_value[at, :].T.astype(BF)
        last.start()
        inner.forward()
        last.wait()
        output.wait(output_out)
        outer.wait(outer_out)
        inner.wait(inner_out)

    return pl.pallas_call(
        kernel,
        out_shape=[
            jax.ShapeDtypeStruct(grad.shape, BF),
            jax.ShapeDtypeStruct(qkv_got.shape, BF),
            jax.ShapeDtypeStruct(output_grad.shape[1:], BF),
            jax.ShapeDtypeStruct((32, FF // 2), BF),
            jax.ShapeDtypeStruct(outer_grad.shape[1:], BF),
        ],
        in_specs=[VMEM] * 4 + [ANY] * 3,
        out_specs=[VMEM] * 5,
        scratch_shapes=[
            pltpu.VMEM((HD, LENGTH), BF),
            pltpu.VMEM((LENGTH, HD), BF),
            pltpu.VMEM((HD, LENGTH), BF),
            pltpu.VMEM((LENGTH, HD), BF),
            pltpu.VMEM((LENGTH, HD), BF),
            pltpu.VMEM((HD, LENGTH), BF),
            pltpu.VMEM((LENGTH, HD), BF),
            pltpu.VMEM((1, LENGTH), F32),
            pltpu.VMEM((HD, LENGTH), F32),
            pltpu.VMEM((LENGTH, HD), F32),
            pltpu.VMEM((LENGTH, HD), F32),
            pltpu.VMEM((CHIPS, 3 * HD, PAIR), BF),
        ]
        + Exchange.scratch("a2a", "chip", grad)
        + Exchange.scratch("a2a", "chip", qkv_got)
        + SplitReduce.scratch(inner_grad, (0, 128))
        + Reduce.scratch(output_grad, (0, HD))
        + Reduce.scratch(outer_grad, (0, 256)),
        compiler_params=params(identifier, 48),
        name="attend_backward",
    )(qkv_got, summed, stat, grad, output_grad, inner_grad, outer_grad)


def reduce_last(identifier, qkv_grad, vectors, token_part):
    half = 64

    def kernel(*refs):
        refs = Refs(refs)
        qkv_ref, vectors_ref, token_ref = refs.take(3)
        split_out, direct_out, vectors_out, token_out = refs.take(4)
        enter(["seq", "z", "core"])
        split = SplitReduce(qkv_ref, (0, half), refs.take(8))
        direct = Reduce(qkv_ref, (half, half), refs.take(5))
        vector = Exchange("a2a", "seq", vectors_ref, vectors_out, refs.take(4))
        token = Exchange("a2a", "core", token_ref, token_out, refs.take(4))
        for one in (split, direct, vector, token):
            one.start()
        split.forward()
        token.wait()
        vector.wait()
        direct.wait(direct_out)
        split.wait(split_out)

    columns = qkv_grad.shape[2]
    return pl.pallas_call(
        kernel,
        out_shape=[
            jax.ShapeDtypeStruct((half // 4, columns), BF),
            jax.ShapeDtypeStruct((half, columns), BF),
            jax.ShapeDtypeStruct(vectors.shape, F32),
            jax.ShapeDtypeStruct(token_part.shape, F32),
        ],
        in_specs=[ANY] * 3,
        out_specs=[VMEM] * 2 + [ANY] * 2,
        scratch_shapes=SplitReduce.scratch(qkv_grad, (0, half))
        + Reduce.scratch(qkv_grad, (half, half))
        + Exchange.scratch("a2a", "seq", vectors)
        + Exchange.scratch("a2a", "core", token_part),
        compiler_params=params(identifier, 24),
        name="reduce_last",
    )(qkv_grad, vectors, token_part)


def normalize(hidden, gain, shift):
    centered = hidden - jnp.mean(hidden, axis=-1, keepdims=True)
    inverse = lax.rsqrt(jnp.mean(centered * centered, axis=-1, keepdims=True) + 1e-05)
    normed = centered * inverse
    return (normed * gain + shift, normed, inverse)


def normalize_back(upstream, normed, inverse, gain):
    scaled = upstream * gain
    inner = (
        scaled
        - jnp.mean(scaled, axis=-1, keepdims=True)
        - normed * jnp.mean(scaled * normed, axis=-1, keepdims=True)
    )
    return (inverse * inner, jnp.sum(upstream * normed, axis=0), jnp.sum(upstream, axis=0))


def gelu_exact(value):
    return jax.nn.gelu(value, approximate=False)


def per_device(
    tokens,
    cotangent,
    w_query,
    b_query,
    w_key,
    w_value,
    b_value,
    w_output,
    b_output,
    first_gain,
    first_shift,
    w_inner,
    b_inner,
    w_outer,
    b_outer,
    second_gain,
    second_shift,
):
    core = lax.rem(lax.axis_index("ctx"), 2)
    rows = tokens[0]

    def pick(value, axis):
        return lax.dynamic_index_in_dim(value, core, axis, keepdims=False)

    qkv_part = pick(
        jnp.stack([w_query, w_key, w_value]).reshape(3, 128, SEQ, 2, HD), 3
    )
    qkv_part = jnp.transpose(qkv_part, (1, 2, 0, 3)).reshape(128, SEQ * 3 * HD)
    output_part = pick(w_output.reshape(2, HD, D), 0)
    inner_part = pick(w_inner.reshape(128, SEQ, 2, 256), 2).reshape(128, FF // 2)
    outer_part = pick(w_outer.reshape(2, 256, D), 0)
    small_part = jnp.concatenate(
        [
            jnp.stack(
                [b_query, b_value, b_output, first_gain, first_shift, b_outer, second_gain, second_shift]
            ),
            b_inner.reshape(4, 128),
            jnp.zeros((4, 128), BF),
        ]
    )
    qkv_weight, small, rows_pair = gather_first(0, qkv_part, small_part, rows)
    qkv_weight = qkv_weight.reshape(D, SEQ * 3 * HD)
    rows_pair = rows_pair.reshape(PAIR, D)
    small = small.astype(F32)
    query_bias = pick(small[:, 0].reshape(SEQ, 2, HD), 1)
    value_bias = pick(small[:, 1].reshape(SEQ, 2, HD), 1)
    qkv_bias = jnp.stack([query_bias, jnp.zeros_like(query_bias), value_bias], axis=1)
    output_bias, norm_gain, norm_shift, outer_bias, final_gain, final_shift = (
        small[:, at].reshape(D) for at in range(2, 8)
    )
    inner_bias = pick(small[:, 8:12].reshape(SEQ, 2, 256), 1).reshape(FF // 2)

    qkv = (dot(qkv_weight, rows_pair, ((0,), (1,))) + qkv_bias.reshape(-1, 1)).astype(BF)
    qkv_got, summed, attended, stat, output_weight, inner_weight, outer_weight = attend_forward(
        1,
        qkv.reshape(CHIPS, 3 * HD, PAIR),
        output_part,
        inner_part,
        outer_part,
    )
    attended = attended.reshape(D // 2, PAIR)
    output_weight = output_weight.reshape(D // 2, D)
    inner_weight = inner_weight.reshape(D, FF // 2)
    outer_weight = outer_weight.reshape(FF // 2, D)

    def core_sum(identifier, partial):
        (got,) = exchange(identifier, ("a2a", "core", partial.reshape(2, ROWS, D)))
        return got[0] + got[1]

    def core_pair(identifier, value):
        (got,) = exchange(identifier, ("ag", "core", value))
        return got.reshape(PAIR, D)

    branch = core_sum(2, dot(attended, output_weight, ((0,), (0,)))) + output_bias
    middle, unit_one, inverse_one = normalize(rows.astype(F32) + branch, norm_gain, norm_shift)
    middle_pair = core_pair(3, middle.astype(BF))
    inner = dot(middle_pair, inner_weight) + inner_bias
    active, gelu_pull = jax.vjp(gelu_exact, inner)
    active_low = active.astype(BF)
    outer = core_sum(4, dot(active_low, outer_weight)) + outer_bias
    result, unit_two, inverse_two = normalize(middle + outer, final_gain, final_shift)
    upstream = cotangent[0].astype(F32)
    grad_mid, grad_final_gain, grad_final_shift = normalize_back(
        upstream, unit_two, inverse_two, final_gain
    )
    grad_outer_low = grad_mid.astype(BF)
    grad_outer_bias = jnp.sum(grad_outer_low.astype(F32), axis=0)
    grad_outer_pair = core_pair(5, grad_outer_low)
    grad_outer_weight = dot(active_low, grad_outer_pair, ((0,), (0,))).astype(BF)
    grad_active = dot(grad_outer_pair, outer_weight, ((1,), (1,)))
    grad_inner_low = gelu_pull(grad_active)[0].astype(BF)
    grad_inner_weight = dot(middle_pair, grad_inner_low, ((0,), (0,))).astype(BF)
    grad_inner_bias = jnp.sum(grad_inner_low.astype(F32), axis=0)
    grad_middle = core_sum(6, dot(grad_inner_low, inner_weight, ((1,), (1,)))) + grad_mid
    grad_residual, grad_norm_gain, grad_norm_shift = normalize_back(
        grad_middle, unit_one, inverse_one, norm_gain
    )
    grad_branch_low = grad_residual.astype(BF)
    grad_output_bias = jnp.sum(grad_branch_low.astype(F32), axis=0)
    grad_branch_pair = core_pair(7, grad_branch_low)
    grad_output_weight = dot(attended, grad_branch_pair).astype(BF)
    grad_attended = dot(output_weight, grad_branch_pair, ((1,), (1,))).astype(BF)

    ignored, grad_qkv, output_share, inner_share, outer_share = attend_backward(
        8,
        qkv_got,
        summed,
        stat,
        grad_attended.reshape(CHIPS, HD, PAIR),
        grad_output_weight.reshape(SEQ, HD, D),
        grad_inner_weight.reshape(SEQ, 128, FF // 2),
        grad_outer_weight.reshape(SEQ, 256, D),
    )
    grad_qkv = grad_qkv.reshape(SEQ * 3 * HD, PAIR)
    grad_qkv_weight = dot(rows_pair, grad_qkv, ((0,), (1,))).astype(BF)
    token_part = dot(grad_qkv, qkv_weight, ((0,), (1,)))
    grad_qkv_bias = jnp.sum(grad_qkv.astype(F32), axis=1).reshape(SEQ, 3, HD)

    vectors = jnp.concatenate(
        [
            jnp.stack(
                [
                    grad_output_bias,
                    grad_norm_gain,
                    grad_norm_shift,
                    grad_outer_bias,
                    grad_final_gain,
                    grad_final_shift,
                ]
            )
            .reshape(6, SEQ, 128)
            .transpose(1, 0, 2),
            jnp.concatenate([grad_qkv_bias[:, 0], grad_qkv_bias[:, 2]], axis=1)[:, None],
            grad_inner_bias.reshape(SEQ, 2, 128),
            jnp.zeros((SEQ, 7, 128), F32),
        ],
        axis=1,
    )
    qkv_share, qkv_terms, vector_terms, token_terms = reduce_last(
        9,
        grad_qkv_weight.reshape(SEQ, 128, SEQ * 3 * HD),
        vectors,
        token_part.reshape(2, ROWS, D),
    )
    grad_tokens = grad_residual + token_terms[0] + token_terms[1]

    shares = jnp.concatenate([qkv_terms.reshape(-1, D), output_share, outer_share])
    quarters = jnp.concatenate([qkv_share.reshape(-1, D), inner_share.reshape(-1, D)])
    piece = shares.shape[0] // CHIPS
    share_terms, quarter_terms, vector_all = exchange(
        10,
        ("a2a", "chip", shares.reshape(CHIPS, piece, D)),
        ("ag", "half", quarters),
        ("ag", "chip", jnp.sum(vector_terms, axis=0)),
    )
    own = jnp.sum(share_terms.astype(F32), axis=0).astype(BF)
    quarter_own = jnp.sum(quarter_terms.astype(F32), axis=0).astype(BF)
    vector_own = jnp.sum(vector_all, axis=0)
    own_all, quarter_all = exchange(11, ("ag", "chip", own), ("ag", "z", quarter_own))
    shares_both, quarters_both, vector_both = exchange(
        12,
        ("ag", "core", own_all.reshape(-1, D)),
        ("ag", "core", quarter_all.reshape(-1, D)),
        ("ag", "core", vector_own),
    )
    quarters_both = quarters_both.reshape(2, 4, -1, D)
    q_rows = 64 * SEQ * 3 * HD // D
    quarter_rows = q_rows // 4
    grad_qkv_all = jnp.concatenate(
        [
            quarters_both[:, :, :quarter_rows].reshape(2, 64, SEQ * 3 * HD),
            shares_both[:, :q_rows].reshape(2, 64, SEQ * 3 * HD),
        ],
        axis=1,
    )
    grad_qkv_all = grad_qkv_all.reshape(2, 128, SEQ, 3, HD).astype(F32)
    grad_qkv_all = grad_qkv_all.transpose(3, 1, 2, 0, 4).reshape(3, 128, D)
    at = q_rows
    grad_output_all = shares_both[:, at : at + HD].reshape(128, D).astype(F32)
    at += HD
    grad_inner_all = quarters_both[:, :, quarter_rows:].reshape(2, 128, SEQ, 256)
    grad_inner_all = grad_inner_all.transpose(1, 2, 0, 3).reshape(128, FF).astype(F32)
    grad_outer_all = shares_both[:, at : at + 256].reshape(512, D).astype(F32)
    whole = vector_both[0, :6] + vector_both[1, :6]
    grad_query_bias = vector_both[:, 6, :HD].reshape(128)
    grad_value_bias = vector_both[:, 6, HD:].reshape(128)
    grad_inner_bias = vector_both[:, 7:9].reshape(512)
    return (
        result.astype(BF)[None],
        grad_tokens[None],
        grad_qkv_all[0],
        grad_query_bias,
        grad_qkv_all[1],
        grad_qkv_all[2],
        grad_value_bias,
        grad_output_all,
        whole[0],
        whole[1],
        whole[2],
        grad_inner_all,
        grad_inner_bias,
        grad_outer_all,
        whole[3],
        whole[4],
        whole[5],
    )


def solution(mesh):
    row = P("seq", None)
    vector = P("seq")
    placed = P("seq", "ctx", None)
    return jax.shard_map(
        per_device,
        mesh=mesh,
        in_specs=(
            placed,
            placed,
            row,
            vector,
            row,
            row,
            vector,
            row,
            vector,
            vector,
            vector,
            row,
            vector,
            row,
            vector,
            vector,
            vector,
        ),
        out_specs=(
            placed,
            placed,
            row,
            vector,
            row,
            row,
            vector,
            row,
            vector,
            vector,
            vector,
            row,
            vector,
            row,
            vector,
            vector,
            vector,
        ),
        check_vma=False,
    )
```

```python
import functools
import math

import jax
import jax.numpy as jnp
from jax import lax
from jax.experimental import pallas as pl
from jax.experimental.pallas import tpu as pltpu
from jax.sharding import PartitionSpec as P

D = 1024
HEADS = 16
HD = 64
FF = 4096
SEQ = 8
CHIPS = 8
ROWS = 192
PAIR = 2 * ROWS
LENGTH = CHIPS * PAIR
SCALE2 = HD ** (-0.5) * math.log2(math.e)
BLOCK = 512
BF = jnp.bfloat16
F32 = jnp.float32
ANY = pl.BlockSpec(memory_space=pl.ANY)
VMEM = pl.BlockSpec(memory_space=pltpu.VMEM)


def dot(left, right, dims=((1,), (0,))):
    return lax.dot_general(left, right, (dims, ((), ())), preferred_element_type=F32)


SIZES = {"seq": 8, "chip": 8, "z": 4, "half": 2, "core": 2}


def group_size(group):
    return SIZES[group]


def group_me(group):
    if group == "seq":
        return lax.axis_index("seq")
    ctx = lax.axis_index("ctx")
    if group == "core":
        return lax.rem(ctx, 2)
    if group == "half":
        return lax.div(ctx, 8)
    if group == "z":
        return lax.rem(lax.div(ctx, 2), 4)
    return lax.div(ctx, 2)


def group_device(group, index):
    seq, ctx = lax.axis_index("seq"), lax.axis_index("ctx")
    if group == "seq":
        return (index, ctx)
    if group == "core":
        return (seq, lax.div(ctx, 2) * 2 + index)
    if group == "half":
        return (seq, index * 8 + lax.rem(ctx, 8))
    if group == "z":
        return (seq, lax.div(ctx, 8) * 8 + index * 2 + lax.rem(ctx, 2))
    return (seq, index * 2 + lax.rem(ctx, 2))


def group_peer(group, step):
    return lax.rem(group_me(group) + step, group_size(group))


def enter(groups):
    barrier = pltpu.get_barrier_semaphore()
    count = 0
    for group in groups:
        for step in range(1, group_size(group)):
            pl.semaphore_signal(
                barrier,
                inc=1,
                device_id=group_device(group, group_peer(group, step)),
                device_id_type=pl.DeviceIdType.MESH,
            )
            count += 1
    pl.semaphore_wait(barrier, count)


def remote(source, target, send, recv, group, peer):
    return pltpu.make_async_remote_copy(
        src_ref=source,
        dst_ref=target,
        send_sem=send,
        recv_sem=recv,
        device_id=group_device(group, peer),
        device_id_type=pl.DeviceIdType.MESH,
    )


def dma(*shape):
    return pltpu.SemaphoreType.DMA(shape)


class Exchange:
    def __init__(self, kind, group, source, target, refs, rows=None):
        self.kind, self.group = kind, group
        self.source, self.target, self.rows = source, target, rows
        self.send, self.recv = refs[:2]
        if rows is None:
            self.own, self.own_held = refs[2:]

    @staticmethod
    def scratch(kind, group, value, rows=None):
        count = group_size(group) - 1
        if rows is not None:
            return [dma(count), dma(count)]
        piece = value.shape if kind == "ag" else value.shape[1:]
        return [dma(count), dma(count), dma(2), pltpu.VMEM(piece, value.dtype)]

    def copies(self):
        me = group_me(self.group)
        made = []
        for step in range(1, group_size(self.group)):
            peer = group_peer(self.group, step)
            piece = self.source if self.kind == "ag" else self.source.at[peer]
            target = self.target.at[me]
            if self.rows is not None:
                piece, target = piece.at[pl.ds(*self.rows)], target.at[pl.ds(*self.rows)]
            made.append(
                remote(piece, target, self.send.at[step - 1], self.recv.at[step - 1], self.group, peer)
            )
        return made

    def own_copies(self):
        me = group_me(self.group)
        piece = self.source if self.kind == "ag" else self.source.at[me]
        return (
            pltpu.make_async_copy(piece, self.own_held, self.own.at[0]),
            pltpu.make_async_copy(self.own_held, self.target.at[me], self.own.at[1]),
        )

    def start(self):
        for copy in self.copies():
            copy.start()
        if self.rows is None:
            self.own_copies()[0].start()

    def wait(self):
        if self.rows is None:
            own_in, own_out = self.own_copies()
            own_in.wait()
            own_out.start()
            own_out.wait()
        for copy in self.copies():
            copy.wait()


class Own:
    def __init__(self, source, target, refs):
        self.source, self.target = source, target.at[group_me("seq")]
        self.sems, self.held = refs

    @staticmethod
    def scratch(value):
        return [dma(2), pltpu.VMEM(value.shape, value.dtype)]

    def start(self):
        pltpu.make_async_copy(self.source, self.held, self.sems.at[0]).start()

    def wait(self):
        pltpu.make_async_copy(self.source, self.held, self.sems.at[0]).wait()
        copy = pltpu.make_async_copy(self.held, self.target, self.sems.at[1])
        copy.start()
        copy.wait()


class SplitGather:
    def __init__(self, source, target, rows, refs):
        self.source, self.target, self.base = source, target, rows[0]
        self.quarter = rows[1] // 4
        self.send, self.recv, self.send_z, self.recv_z = refs

    @staticmethod
    def scratch():
        return [dma(7), dma(7), dma(21), dma(21)]

    def span(self):
        start = pl.multiple_of(self.base + group_me("z") * self.quarter, 16)
        return pl.ds(start, self.quarter)

    def first(self, step):
        span = self.span()
        return remote(
            self.source.at[span],
            self.target.at[group_me("seq"), span],
            self.send.at[step - 1],
            self.recv.at[step - 1],
            "seq",
            group_peer("seq", step),
        )

    def second(self, step, hop):
        owner, span, at = group_peer("seq", 8 - step), self.span(), (step - 1) * 3 + hop - 1
        piece = self.target.at[owner, span]
        return remote(
            piece, piece, self.send_z.at[at], self.recv_z.at[at], "z", group_peer("z", hop)
        )

    def start(self):
        for step in range(1, 8):
            self.first(step).start()

    def forward(self):
        for step in range(1, 8):
            self.first(step).wait_recv()
            for hop in range(1, 4):
                self.second(step, hop).start()

    def wait(self):
        for step in range(1, 8):
            self.first(step).wait_send()
            for hop in range(1, 4):
                self.second(step, hop).wait()


class Reduce:
    def __init__(self, source, rows, refs):
        self.source, self.span = source, pl.ds(*rows)
        self.send, self.recv, self.local, self.got, self.own = refs

    @staticmethod
    def scratch(value, rows):
        piece = (rows[1], value.shape[2])
        return [dma(7), dma(7), dma(), pltpu.VMEM((7,) + piece, BF), pltpu.VMEM(piece, BF)]

    def copies(self):
        return [
            remote(
                self.source.at[group_peer("seq", step), self.span],
                self.got.at[step - 1],
                self.send.at[step - 1],
                self.recv.at[step - 1],
                "seq",
                group_peer("seq", step),
            )
            for step in range(1, 8)
        ]

    def own_copy(self):
        return pltpu.make_async_copy(
            self.source.at[group_me("seq"), self.span], self.own, self.local
        )

    def start(self):
        for copy in self.copies():
            copy.start()
        self.own_copy().start()

    def wait(self, out):
        self.own_copy().wait()
        for copy in self.copies():
            copy.wait()
        value = sum((self.got[at].astype(F32) for at in range(7)), self.own[...].astype(F32))
        out[...] = value.astype(out.dtype).reshape(out.shape)


class SplitReduce:
    def __init__(self, source, rows, refs):
        self.source, self.base, self.quarter = source, rows[0], rows[1] // 4
        self.send_z, self.recv_z, self.send, self.recv, self.local = refs[:5]
        self.got_z, self.total, self.got = refs[5:]

    @staticmethod
    def scratch(value, rows):
        piece = (rows[1] // 4, value.shape[2])
        return [dma(3), dma(3), dma(7), dma(7), dma()] + [
            pltpu.VMEM(lead + piece, BF) for lead in ((3, 8), (8,), (7,))
        ]

    def part(self, index):
        start = pl.multiple_of(self.base + index * self.quarter, 16)
        return self.source.at[:, pl.ds(start, self.quarter)]

    def first(self, hop):
        peer = group_peer("z", hop)
        return remote(
            self.part(peer), self.got_z.at[hop - 1], self.send_z.at[hop - 1], self.recv_z.at[hop - 1], "z", peer
        )

    def own_copy(self):
        return pltpu.make_async_copy(self.part(group_me("z")), self.total, self.local)

    def second(self, step):
        peer = group_peer("seq", step)
        return remote(
            self.total.at[peer], self.got.at[step - 1], self.send.at[step - 1], self.recv.at[step - 1], "seq", peer
        )

    def start(self):
        for hop in range(1, 4):
            self.first(hop).start()
        self.own_copy().start()

    def forward(self):
        self.own_copy().wait()
        for hop in range(1, 4):
            self.first(hop).wait()

        def add(at, carry):
            value = self.total[at].astype(F32)
            for hop in range(3):
                value += self.got_z[hop, at].astype(F32)
            self.total[at] = value.astype(BF)
            return carry

        lax.fori_loop(0, 8, add, 0)
        for step in range(1, 8):
            self.second(step).start()

    def wait(self, out):
        for step in range(1, 8):
            self.second(step).wait()
        out[...] = sum(
            (self.got[at].astype(F32) for at in range(7)), self.total[group_me("seq")].astype(F32)
        ).astype(BF)


class Refs:
    def __init__(self, refs):
        self.refs, self.at = refs, 0

    def take(self, count):
        self.at += count
        return self.refs[self.at - count : self.at]

    def left(self):
        return self.refs[self.at :]


def target_shape(kind, group, value):
    shape = value.shape if kind == "a2a" else (group_size(group),) + value.shape
    return jax.ShapeDtypeStruct(shape, value.dtype)


def params(identifier, mebibytes):
    return pltpu.CompilerParams(
        collective_id=identifier,
        has_side_effects=True,
        vmem_limit_bytes=mebibytes * 1024 * 1024,
    )


def exchange(identifier, *items):
    number = len(items)

    def kernel(*refs):
        refs = Refs(refs)
        sources, targets = refs.take(number), refs.take(number)
        enter(sorted({item[1] for item in items}))
        made = [
            Exchange(item[0], item[1], source, target, refs.take(4))
            for item, source, target in zip(items, sources, targets)
        ]
        for one in made:
            one.start()
        for one in made:
            one.wait()

    return pl.pallas_call(
        kernel,
        out_shape=[target_shape(*item) for item in items],
        in_specs=[ANY] * number,
        out_specs=[ANY] * number,
        scratch_shapes=[ref for item in items for ref in Exchange.scratch(*item)],
        compiler_params=params(identifier, 16),
        name="exchange%d" % identifier,
    )(*[item[2] for item in items])


def gather_first(identifier, qkv, small, rows):
    half = qkv.shape[0] // 2

    def kernel(*refs):
        refs = Refs(refs)
        qkv_ref, small_ref, rows_ref = refs.take(3)
        qkv_out, small_out, rows_out = refs.take(3)
        enter(["seq", "z", "core"])
        split = SplitGather(qkv_ref, qkv_out, (0, half), refs.take(4))
        direct = Exchange("ag", "seq", qkv_ref, qkv_out, refs.take(2), rows=(half, half))
        own = Own(qkv_ref, qkv_out, refs.take(2))
        smalls = Exchange("ag", "seq", small_ref, small_out, refs.take(4))
        pair = Exchange("ag", "core", rows_ref, rows_out, refs.take(4))
        split.start()
        for one in (direct, own, smalls, pair):
            one.start()
        split.forward()
        for one in (pair, own, smalls, direct, split):
            one.wait()

    return pl.pallas_call(
        kernel,
        out_shape=[
            target_shape("ag", "seq", qkv),
            target_shape("ag", "seq", small),
            target_shape("ag", "core", rows),
        ],
        in_specs=[ANY] * 3,
        out_specs=[ANY] * 3,
        scratch_shapes=SplitGather.scratch()
        + Exchange.scratch("ag", "seq", qkv, (half, half))
        + Own.scratch(qkv)
        + Exchange.scratch("ag", "seq", small)
        + Exchange.scratch("ag", "core", rows),
        compiler_params=params(identifier, 16),
        name="gather_first",
    )(qkv, small, rows)


def attend_forward(identifier, qkv, output_part, inner_part, outer_part):
    low_shape = jax.ShapeDtypeStruct((CHIPS, HD, PAIR), BF)

    def kernel(*refs):
        refs = Refs(refs)
        qkv_ref, output_ref, inner_ref, outer_ref = refs.take(4)
        qkv_got, summed_ref, back_ref, stat_ref = refs.take(4)
        output_out, inner_out, outer_out = refs.take(3)
        query_t, keys, value_t, low = refs.take(4)
        enter(["seq", "chip"])
        first = Exchange("a2a", "chip", qkv_ref, qkv_got, refs.take(4))
        last = Exchange("a2a", "chip", low, back_ref, refs.take(4))
        inner = SplitGather(inner_ref, inner_out, (0, inner_part.shape[0]), refs.take(4))
        inner_own = Own(inner_ref, inner_out, refs.take(2))
        output = Exchange("ag", "seq", output_ref, output_out, refs.take(4))
        outer = Exchange("ag", "seq", outer_ref, outer_out, refs.take(4))
        first.start()
        inner.start()
        inner_own.start()
        output.start()
        first.wait()
        inner.forward()
        outer.start()
        for chip in range(CHIPS):
            at = pl.ds(chip * PAIR, PAIR)
            query_t[:, at] = qkv_got[chip, 0:HD, :]
            keys[at, :] = qkv_got[chip, HD : 2 * HD, :].astype(F32).T.astype(BF)
            value_t[:, at] = qkv_got[chip, 2 * HD : 3 * HD, :]

        def one_block(block, carry):
            at = pl.ds(pl.multiple_of(block * BLOCK, BLOCK), BLOCK)
            query = query_t[:, at]
            top = jnp.full((1, BLOCK), -1e30, F32)
            total = jnp.zeros((1, BLOCK), F32)
            summed = jnp.zeros((HD, BLOCK), F32)
            for part in range(LENGTH // BLOCK):
                here = slice(part * BLOCK, (part + 1) * BLOCK)
                scores = dot(keys[here, :], query) * SCALE2
                new_top = jnp.maximum(top, jnp.max(scores, axis=0, keepdims=True))
                factor = jnp.exp2(top - new_top)
                weights = jnp.exp2(scores - new_top)
                total = total * factor + jnp.sum(weights, axis=0, keepdims=True)
                summed = summed * factor + dot(value_t[:, here], weights.astype(BF))
                top = new_top
            summed_ref[:, at] = summed / total
            stat_ref[:, at] = top + jnp.log2(total)
            return carry

        lax.fori_loop(0, LENGTH // BLOCK, one_block, 0)
        for chip in range(CHIPS):
            low[chip] = summed_ref[:, chip * PAIR : (chip + 1) * PAIR].astype(BF)
        last.start()
        for one in (last, output, inner_own, inner, outer):
            one.wait()

    return pl.pallas_call(
        kernel,
        out_shape=[
            jax.ShapeDtypeStruct(qkv.shape, BF),
            jax.ShapeDtypeStruct((HD, LENGTH), F32),
            low_shape,
            jax.ShapeDtypeStruct((1, LENGTH), F32),
        ]
        + [target_shape("ag", "seq", part) for part in (output_part, inner_part, outer_part)],
        in_specs=[VMEM] + [ANY] * 3,
        out_specs=[VMEM] * 4 + [ANY] * 3,
        scratch_shapes=[
            pltpu.VMEM((HD, LENGTH), BF),
            pltpu.VMEM((LENGTH, HD), BF),
            pltpu.VMEM((HD, LENGTH), BF),
            pltpu.VMEM((CHIPS, HD, PAIR), BF),
        ]
        + Exchange.scratch("a2a", "chip", qkv)
        + Exchange.scratch("a2a", "chip", low_shape)
        + SplitGather.scratch()
        + Own.scratch(inner_part)
        + Exchange.scratch("ag", "seq", output_part)
        + Exchange.scratch("ag", "seq", outer_part),
        compiler_params=params(identifier, 40),
        name="attend_forward",
    )(qkv, output_part, inner_part, outer_part)


def attend_backward(identifier, qkv_got, summed, stat, grad, output_grad, inner_grad, outer_grad):
    def kernel(*refs):
        refs = Refs(refs)
        qkv_ref, summed_ref, stat_ref, grad_ref = refs.take(4)
        output_ref, inner_ref, outer_ref = refs.take(3)
        grad_got, back_ref, output_out, inner_out, outer_out = refs.take(5)
        query_t, queries, key_t, keys, values, up_t, ups, delta_ref = refs.take(8)
        grad_query, grad_key, grad_value, low = refs.take(4)
        enter(["seq", "chip"])
        first = Exchange("a2a", "chip", grad_ref, grad_got, refs.take(4))
        last = Exchange("a2a", "chip", low, back_ref, refs.take(4))
        inner = SplitReduce(inner_ref, (0, 128), refs.take(8))
        output = Reduce(output_ref, (0, HD), refs.take(5))
        outer = Reduce(outer_ref, (0, 256), refs.take(5))
        first.start()
        inner.start()
        output.start()
        outer.start()
        for chip in range(CHIPS):
            at = pl.ds(chip * PAIR, PAIR)
            query_t[:, at] = qkv_ref[chip, 0:HD, :]
            queries[at, :] = qkv_ref[chip, 0:HD, :].astype(F32).T.astype(BF)
            key_t[:, at] = qkv_ref[chip, HD : 2 * HD, :]
            keys[at, :] = qkv_ref[chip, HD : 2 * HD, :].astype(F32).T.astype(BF)
            values[at, :] = qkv_ref[chip, 2 * HD : 3 * HD, :].astype(F32).T.astype(BF)
        grad_key[...] = jnp.zeros_like(grad_key)
        grad_value[...] = jnp.zeros_like(grad_value)
        first.wait()
        for chip in range(CHIPS):
            at = pl.ds(chip * PAIR, PAIR)
            up = grad_got[chip].astype(F32)
            up_t[:, at] = grad_got[chip]
            ups[at, :] = up.T.astype(BF)
            delta_ref[:, at] = jnp.sum(up * summed_ref[:, at], axis=0, keepdims=True)

        def one_block(block, carry):
            at = pl.ds(pl.multiple_of(block * BLOCK, BLOCK), BLOCK)
            query, up = query_t[:, at], up_t[:, at]
            query_rows, up_rows = queries[at, :], ups[at, :]
            stat, delta = stat_ref[:, at], delta_ref[:, at]
            gathered = jnp.zeros((HD, BLOCK), F32)
            for part in range(LENGTH // BLOCK):
                here = slice(part * BLOCK, (part + 1) * BLOCK)
                scores = dot(keys[here, :], query) * SCALE2
                probs = jnp.exp2(scores - stat)
                grad_value[here, :] += dot(probs.astype(BF), up_rows)
                slope = dot(values[here, :], up) - delta
                grad_scores = (probs * slope).astype(BF)
                grad_key[here, :] += dot(grad_scores, query_rows)
                gathered += dot(key_t[:, here], grad_scores)
            grad_query[:, at] = gathered
            return carry

        lax.fori_loop(0, LENGTH // BLOCK, one_block, 0)
        scale = HD ** (-0.5)
        for chip in range(CHIPS):
            at = slice(chip * PAIR, (chip + 1) * PAIR)
            low[chip, 0:HD, :] = (grad_query[:, at] * scale).astype(BF)
            low[chip, HD : 2 * HD, :] = (grad_key[at, :] * scale).T.astype(BF)
            low[chip, 2 * HD : 3 * HD, :] = grad_value[at, :].T.astype(BF)
        last.start()
        inner.forward()
        last.wait()
        output.wait(output_out)
        outer.wait(outer_out)
        inner.wait(inner_out)

    return pl.pallas_call(
        kernel,
        out_shape=[
            jax.ShapeDtypeStruct(grad.shape, BF),
            jax.ShapeDtypeStruct(qkv_got.shape, BF),
            jax.ShapeDtypeStruct(output_grad.shape[1:], F32),
            jax.ShapeDtypeStruct((32, FF // 2), BF),
            jax.ShapeDtypeStruct(outer_grad.shape[1:], BF),
        ],
        in_specs=[VMEM] * 4 + [ANY] * 3,
        out_specs=[VMEM] * 5,
        scratch_shapes=[
            pltpu.VMEM((HD, LENGTH), BF),
            pltpu.VMEM((LENGTH, HD), BF),
            pltpu.VMEM((HD, LENGTH), BF),
            pltpu.VMEM((LENGTH, HD), BF),
            pltpu.VMEM((LENGTH, HD), BF),
            pltpu.VMEM((HD, LENGTH), BF),
            pltpu.VMEM((LENGTH, HD), BF),
            pltpu.VMEM((1, LENGTH), F32),
            pltpu.VMEM((HD, LENGTH), F32),
            pltpu.VMEM((LENGTH, HD), F32),
            pltpu.VMEM((LENGTH, HD), F32),
            pltpu.VMEM((CHIPS, 3 * HD, PAIR), BF),
        ]
        + Exchange.scratch("a2a", "chip", grad)
        + Exchange.scratch("a2a", "chip", qkv_got)
        + SplitReduce.scratch(inner_grad, (0, 128))
        + Reduce.scratch(output_grad, (0, HD))
        + Reduce.scratch(outer_grad, (0, 256)),
        compiler_params=params(identifier, 48),
        name="attend_backward",
    )(qkv_got, summed, stat, grad, output_grad, inner_grad, outer_grad)


class Scatter:
    def __init__(self, group, source, refs):
        self.group, self.source = group, source
        send, recv, self.got = refs
        self.copies = [
            remote(
                source.at[group_peer(group, step)],
                self.got.at[step - 1],
                send.at[step - 1],
                recv.at[step - 1],
                group,
                group_peer(group, step),
            )
            for step in range(1, group_size(group))
        ]

    @staticmethod
    def scratch(group, piece, kind):
        count = group_size(group) - 1
        return [dma(count), dma(count), pltpu.VMEM((count,) + piece, kind)]

    def start(self):
        for copy in self.copies:
            copy.start()

    def sum(self):
        for copy in self.copies:
            copy.wait()
        own = self.source[group_me(self.group)].astype(F32)
        return sum((self.got[at].astype(F32) for at in range(group_size(self.group) - 1)), own)


class Swap:
    def __init__(self, group, source, refs):
        send, recv, self.got = refs
        self.source = source
        self.copy = remote(source, self.got, send, recv, group, group_peer(group, 1))

    @staticmethod
    def scratch(piece, kind):
        return [dma(), dma(), pltpu.VMEM(piece, kind)]

    def start(self):
        self.copy.start()

    def sum(self):
        self.copy.wait()
        return self.source[...].astype(F32) + self.got[...].astype(F32)


class Spread:
    def __init__(self, group, held, refs):
        send, recv, send_core, recv_core = refs
        self.group, self.held = group, held
        mine = held.at[group_me("core")]
        self.mine = mine
        piece = mine.at[group_me(group)]
        self.copies = [
            remote(piece, piece, send.at[step - 1], recv.at[step - 1], group, group_peer(group, step))
            for step in range(1, group_size(group))
        ]
        self.last = remote(mine, mine, send_core, recv_core, "core", group_peer("core", 1))

    @staticmethod
    def scratch(group):
        count = group_size(group) - 1
        return [dma(count), dma(count), dma(), dma()]

    def start(self, value):
        self.mine[group_me(self.group)] = value.astype(self.held.dtype)
        for copy in self.copies:
            copy.start()

    def forward(self):
        for copy in self.copies:
            copy.wait()
        self.last.start()

    def wait(self):
        self.last.wait()


def reduce_last(identifier, rows_t, qkv_weight, grad_qkv, vectors, output_share, inner_share, outer_share):
    columns = SEQ * 3 * HD
    half, low = 64, 16
    chip_piece, quarter = (8, columns), (low, columns)
    vector = vectors.shape[1:]

    def kernel(*refs):
        refs = Refs(refs)
        rows_ref, weight_ref, grad_ref, vectors_ref, output_ref, inner_ref, outer_ref = refs.take(7)
        token_out, split_out, direct_out, output_out, inner_out, outer_out, vector_out, bias_out = refs.take(8)
        grads, bias, partial, token_got, token_send, token_recv = refs.take(6)
        direct_sum, split_sum = refs.take(2)
        split = SplitReduce(grads, (0, half), refs.take(8))
        direct = Reduce(grads, (half, half), refs.take(5))
        vector_seq = Scatter("seq", vectors_ref, refs.take(3))
        bias_seq = Scatter("seq", bias, refs.take(3))
        output_chip = Scatter("chip", output_ref, refs.take(3))
        outer_chip = Scatter("chip", outer_ref, refs.take(3))
        inner_half = Swap("half", inner_ref, refs.take(3))
        direct_chip = Scatter("chip", direct_sum, refs.take(3))
        split_half = Swap("half", split_sum, refs.take(3))
        output_all = Spread("chip", output_out, refs.take(4))
        outer_all = Spread("chip", outer_out, refs.take(4))
        inner_all = Spread("z", inner_out, refs.take(4))
        direct_all = Spread("chip", direct_out, refs.take(4))
        split_all = Spread("z", split_out, refs.take(4))
        vector_all = Spread("chip", vector_out, refs.take(4))
        bias_all = Spread("chip", bias_out, refs.take(4))
        other = group_peer("core", 1)
        token = remote(partial.at[other], token_got, token_send, token_recv, "core", other)

        enter(["seq", "chip", "core"])
        for one in (inner_half, outer_chip, output_chip, vector_seq):
            one.start()

        def weight_rows(owner, carry):
            at = pl.ds(pl.multiple_of(owner * 128, 128), 128)
            grads[owner] = dot(rows_ref[at, :], grad_ref[...], ((1,), (1,))).astype(BF)
            part = pl.ds(pl.multiple_of(owner * 192, 64), 192)
            bias[owner] = dot(jnp.ones((8, PAIR), BF), grad_ref[part, :], ((1,), (1,)))
            return carry

        lax.fori_loop(0, SEQ, weight_rows, 0)
        split.start()
        direct.start()
        bias_seq.start()
        turned = dot(weight_ref[...], grad_ref[...]).T
        partial[0] = turned[:ROWS]
        partial[1] = turned[ROWS:]
        token.start()
        inner_all.start(inner_half.sum())
        outer_all.start(outer_chip.sum())
        output_all.start(output_chip.sum())
        vector_all.start(vector_seq.sum())
        split.forward()
        inner_all.forward()
        outer_all.forward()
        output_all.forward()
        direct.wait(direct_sum)
        direct_chip.start()
        bias_all.start(bias_seq.sum())
        split.wait(split_sum)
        split_half.start()
        token.wait()
        token_out[...] = partial[group_me("core")] + token_got[...]
        vector_all.forward()
        direct_all.start(direct_chip.sum())
        split_all.start(split_half.sum())
        bias_all.forward()
        direct_all.forward()
        split_all.forward()
        for one in (inner_all, outer_all, output_all, vector_all, bias_all, direct_all, split_all):
            one.wait()

    return pl.pallas_call(
        kernel,
        out_shape=[
            jax.ShapeDtypeStruct((ROWS, D), F32),
            jax.ShapeDtypeStruct((2, 4) + quarter, BF),
            jax.ShapeDtypeStruct((2, CHIPS) + chip_piece, F32),
            jax.ShapeDtypeStruct((2, CHIPS, 8, D), F32),
            jax.ShapeDtypeStruct((2, 4, 32, FF // 2), BF),
            jax.ShapeDtypeStruct((2, CHIPS, 32, D), BF),
            jax.ShapeDtypeStruct((2, CHIPS) + vector, F32),
            jax.ShapeDtypeStruct((2, CHIPS, 8, 3 * HD), F32),
        ],
        in_specs=[VMEM] * 7,
        out_specs=[VMEM] * 8,
        scratch_shapes=[
            pltpu.VMEM((SEQ, 128, columns), BF),
            pltpu.VMEM((SEQ, 8, 3 * HD), F32),
            pltpu.VMEM((2, ROWS, D), F32),
            pltpu.VMEM((ROWS, D), F32),
            dma(),
            dma(),
            pltpu.VMEM((CHIPS,) + chip_piece, F32),
            pltpu.VMEM(quarter, BF),
        ]
        + SplitReduce.scratch(jax.ShapeDtypeStruct((SEQ, 128, columns), BF), (0, half))
        + Reduce.scratch(jax.ShapeDtypeStruct((SEQ, 128, columns), BF), (half, half))
        + Scatter.scratch("seq", vector, F32)
        + Scatter.scratch("seq", (8, 3 * HD), F32)
        + Scatter.scratch("chip", (8, D), F32)
        + Scatter.scratch("chip", (32, D), BF)
        + Swap.scratch((32, FF // 2), BF)
        + Scatter.scratch("chip", chip_piece, F32)
        + Swap.scratch(quarter, BF)
        + Spread.scratch("chip")
        + Spread.scratch("chip")
        + Spread.scratch("z")
        + Spread.scratch("chip")
        + Spread.scratch("z")
        + Spread.scratch("chip")
        + Spread.scratch("chip"),
        compiler_params=params(identifier, 48),
        name="reduce_last",
    )(rows_t, qkv_weight, grad_qkv, vectors, output_share, inner_share, outer_share)


def unpack(split, direct, output, inner, outer):
    def kernel(split_ref, direct_ref, output_ref, inner_ref, outer_ref, query, key, value, output_out, inner_out, outer_out):
        def place(pair, rows):
            for kind, out in enumerate((query, key, value)):
                for head in range(SEQ):
                    at = head * 3 * HD + kind * HD
                    out[rows, head * 128 : (head + 1) * 128] = jnp.concatenate(
                        [part[:, at : at + HD] for part in pair], axis=1
                    )

        for quarter in range(4):
            place(
                [split_ref[core, quarter].astype(F32) for core in range(2)],
                slice(quarter * 16, (quarter + 1) * 16),
            )
        for chip in range(CHIPS):
            place(
                [direct_ref[core, chip] for core in range(2)],
                slice(64 + chip * 8, 64 + (chip + 1) * 8),
            )
        for core in range(2):
            for chip in range(CHIPS):
                output_out[core * HD + chip * 8 : core * HD + (chip + 1) * 8] = output_ref[core, chip]
                start = core * 256 + chip * 32
                outer_out[start : start + 32] = outer_ref[core, chip].astype(F32)
            for quarter in range(4):
                for owner in range(SEQ):
                    start = owner * 512 + core * 256
                    inner_out[quarter * 32 : (quarter + 1) * 32, start : start + 256] = inner_ref[
                        core, quarter, :, owner * 256 : (owner + 1) * 256
                    ].astype(F32)

    shapes = [(128, D)] * 4 + [(128, FF), (512, D)]
    return pl.pallas_call(
        kernel,
        out_shape=[jax.ShapeDtypeStruct(shape, F32) for shape in shapes],
        in_specs=[VMEM] * 5,
        out_specs=[VMEM] * 6,
        compiler_params=pltpu.CompilerParams(vmem_limit_bytes=32 * 1024 * 1024),
        name="unpack",
    )(split, direct, output, inner, outer)


def normalize(hidden, gain, shift):
    centered = hidden - jnp.mean(hidden, axis=-1, keepdims=True)
    inverse = lax.rsqrt(jnp.mean(centered * centered, axis=-1, keepdims=True) + 1e-05)
    normed = centered * inverse
    return (normed * gain + shift, normed, inverse)


def normalize_back(upstream, normed, inverse, gain):
    scaled = upstream * gain
    inner = (
        scaled
        - jnp.mean(scaled, axis=-1, keepdims=True)
        - normed * jnp.mean(scaled * normed, axis=-1, keepdims=True)
    )
    return (inverse * inner, jnp.sum(upstream * normed, axis=0), jnp.sum(upstream, axis=0))


def gelu_exact(value):
    return jax.nn.gelu(value, approximate=False)


def per_device(
    tokens,
    cotangent,
    w_query,
    b_query,
    w_key,
    w_value,
    b_value,
    w_output,
    b_output,
    first_gain,
    first_shift,
    w_inner,
    b_inner,
    w_outer,
    b_outer,
    second_gain,
    second_shift,
):
    core = lax.rem(lax.axis_index("ctx"), 2)
    rows = tokens[0]

    def pick(value, axis):
        return lax.dynamic_index_in_dim(value, core, axis, keepdims=False)

    qkv_part = pick(
        jnp.stack([w_query, w_key, w_value]).reshape(3, 128, SEQ, 2, HD), 3
    )
    qkv_part = jnp.transpose(qkv_part, (1, 2, 0, 3)).reshape(128, SEQ * 3 * HD)
    output_part = pick(w_output.reshape(2, HD, D), 0)
    inner_part = pick(w_inner.reshape(128, SEQ, 2, 256), 2).reshape(128, FF // 2)
    outer_part = pick(w_outer.reshape(2, 256, D), 0)
    small_part = jnp.concatenate(
        [
            jnp.stack(
                [b_query, b_value, b_output, first_gain, first_shift, b_outer, second_gain, second_shift]
            ),
            b_inner.reshape(4, 128),
            jnp.zeros((4, 128), BF),
        ]
    )
    qkv_weight, small, rows_pair = gather_first(0, qkv_part, small_part, rows)
    qkv_weight = qkv_weight.reshape(D, SEQ * 3 * HD)
    rows_pair = rows_pair.reshape(PAIR, D)
    small = small.astype(F32)
    query_bias = pick(small[:, 0].reshape(SEQ, 2, HD), 1)
    value_bias = pick(small[:, 1].reshape(SEQ, 2, HD), 1)
    qkv_bias = jnp.stack([query_bias, jnp.zeros_like(query_bias), value_bias], axis=1)
    output_bias, norm_gain, norm_shift, outer_bias, final_gain, final_shift = (
        small[:, at].reshape(D) for at in range(2, 8)
    )
    inner_bias = pick(small[:, 8:12].reshape(SEQ, 2, 256), 1).reshape(FF // 2)

    qkv = (dot(qkv_weight, rows_pair, ((0,), (1,))) + qkv_bias.reshape(-1, 1)).astype(BF)
    qkv_got, summed, attended, stat, output_weight, inner_weight, outer_weight = attend_forward(
        1,
        qkv.reshape(CHIPS, 3 * HD, PAIR),
        output_part,
        inner_part,
        outer_part,
    )
    attended = attended.reshape(D // 2, PAIR)
    output_weight = output_weight.reshape(D // 2, D)
    inner_weight = inner_weight.reshape(D, FF // 2)
    outer_weight = outer_weight.reshape(FF // 2, D)

    def core_sum(identifier, partial):
        (got,) = exchange(identifier, ("a2a", "core", partial.reshape(2, ROWS, D)))
        return got[0] + got[1]

    def core_pair(identifier, value):
        (got,) = exchange(identifier, ("ag", "core", value))
        return got.reshape(PAIR, D)

    branch = core_sum(2, dot(attended, output_weight, ((0,), (0,)))) + output_bias
    middle, unit_one, inverse_one = normalize(rows.astype(F32) + branch, norm_gain, norm_shift)
    middle_pair = core_pair(3, middle.astype(BF))
    inner = dot(middle_pair, inner_weight) + inner_bias
    active, gelu_pull = jax.vjp(gelu_exact, inner)
    active_low = active.astype(BF)
    outer = core_sum(4, dot(active_low, outer_weight)) + outer_bias
    result, unit_two, inverse_two = normalize(middle + outer, final_gain, final_shift)
    upstream = cotangent[0].astype(F32)
    grad_mid, grad_final_gain, grad_final_shift = normalize_back(
        upstream, unit_two, inverse_two, final_gain
    )
    grad_outer_low = grad_mid.astype(BF)
    grad_outer_bias = jnp.sum(grad_outer_low.astype(F32), axis=0)
    grad_outer_pair = core_pair(5, grad_outer_low)
    grad_outer_weight = dot(active_low, grad_outer_pair, ((0,), (0,))).astype(BF)
    grad_active = dot(grad_outer_pair, outer_weight, ((1,), (1,)))
    grad_inner_low = gelu_pull(grad_active)[0].astype(BF)
    grad_inner_weight = dot(middle_pair, grad_inner_low, ((0,), (0,))).astype(BF)
    grad_inner_bias = jnp.sum(grad_inner_low.astype(F32), axis=0)
    grad_middle = core_sum(6, dot(grad_inner_low, inner_weight, ((1,), (1,)))) + grad_mid
    grad_residual, grad_norm_gain, grad_norm_shift = normalize_back(
        grad_middle, unit_one, inverse_one, norm_gain
    )
    grad_branch_low = grad_residual.astype(BF)
    grad_output_bias = jnp.sum(grad_branch_low.astype(F32), axis=0)
    grad_branch_pair = core_pair(7, grad_branch_low)
    grad_output_weight = dot(attended, grad_branch_pair).astype(BF)
    grad_attended = dot(output_weight, grad_branch_pair, ((1,), (1,))).astype(BF)

    ignored, grad_qkv, output_share, inner_share, outer_share = attend_backward(
        8,
        qkv_got,
        summed,
        stat,
        grad_attended.reshape(CHIPS, HD, PAIR),
        grad_output_weight.reshape(SEQ, HD, D),
        grad_inner_weight.reshape(SEQ, 128, FF // 2),
        grad_outer_weight.reshape(SEQ, 256, D),
    )
    vectors = jnp.concatenate(
        [
            jnp.stack(
                [
                    grad_output_bias,
                    grad_norm_gain,
                    grad_norm_shift,
                    grad_outer_bias,
                    grad_final_gain,
                    grad_final_shift,
                ]
            )
            .reshape(6, SEQ, 128)
            .transpose(1, 0, 2),
            grad_inner_bias.reshape(SEQ, 2, 128),
        ],
        axis=1,
    )
    token_part, split, direct, output_share, inner_share, outer_share, vectors, biases = reduce_last(
        9,
        rows_pair.T,
        qkv_weight,
        grad_qkv.reshape(SEQ * 3 * HD, PAIR),
        vectors,
        output_share.reshape(CHIPS, 8, D),
        inner_share,
        outer_share.reshape(CHIPS, 32, D),
    )
    grad_tokens = grad_residual + token_part
    grad_query, grad_key, grad_value, grad_output, grad_inner, grad_outer = unpack(
        split, direct, output_share, inner_share, outer_share
    )
    vectors, biases = jnp.sum(vectors, axis=1), jnp.sum(biases[:, :, 0], axis=1)
    whole = vectors[0, :6] + vectors[1, :6]
    grad_query_bias = biases[:, :HD].reshape(128)
    grad_value_bias = biases[:, 2 * HD :].reshape(128)
    grad_inner_bias = vectors[:, 6:].reshape(512)
    return (
        result.astype(BF)[None],
        grad_tokens[None],
        grad_query,
        grad_query_bias,
        grad_key,
        grad_value,
        grad_value_bias,
        grad_output,
        whole[0],
        whole[1],
        whole[2],
        grad_inner,
        grad_inner_bias,
        grad_outer,
        whole[3],
        whole[4],
        whole[5],
    )


def solution(mesh):
    row = P("seq", None)
    vector = P("seq")
    placed = P("seq", "ctx", None)
    return jax.shard_map(
        per_device,
        mesh=mesh,
        in_specs=(
            placed,
            placed,
            row,
            vector,
            row,
            row,
            vector,
            row,
            vector,
            vector,
            vector,
            row,
            vector,
            row,
            vector,
            vector,
            vector,
        ),
        out_specs=(
            placed,
            placed,
            row,
            vector,
            row,
            row,
            vector,
            row,
            vector,
            vector,
            vector,
            row,
            vector,
            row,
            vector,
            vector,
            vector,
        ),
        check_vma=False,
    )
```

```python
import functools
import math

import jax
import jax.numpy as jnp
from jax import lax
from jax.experimental import pallas as pl
from jax.experimental.pallas import tpu as pltpu
from jax.sharding import PartitionSpec as P

D = 1024
HEADS = 16
HD = 64
FF = 4096
SEQ = 8
CHIPS = 8
ROWS = 192
PAIR = 2 * ROWS
LENGTH = CHIPS * PAIR
SCALE2 = HD ** (-0.5) * math.log2(math.e)
BLOCK = 512
BF = jnp.bfloat16
F32 = jnp.float32
ANY = pl.BlockSpec(memory_space=pl.ANY)
VMEM = pl.BlockSpec(memory_space=pltpu.VMEM)


def dot(left, right, dims=((1,), (0,))):
    return lax.dot_general(left, right, (dims, ((), ())), preferred_element_type=F32)


SIZES = {"seq": 8, "chip": 8, "x": 4, "y": 2, "z": 4, "half": 2, "core": 2}


def group_size(group):
    return SIZES[group]


def group_me(group):
    seq, ctx = lax.axis_index("seq"), lax.axis_index("ctx")
    if group == "seq":
        return seq
    if group == "x":
        return lax.rem(seq, 4)
    if group == "y":
        return lax.div(seq, 4)
    if group == "core":
        return lax.rem(ctx, 2)
    if group == "half":
        return lax.div(ctx, 8)
    if group == "z":
        return lax.rem(lax.div(ctx, 2), 4)
    return lax.div(ctx, 2)


def group_device(group, index):
    seq, ctx = lax.axis_index("seq"), lax.axis_index("ctx")
    if group == "seq":
        return (index, ctx)
    if group == "x":
        return (lax.div(seq, 4) * 4 + index, ctx)
    if group == "y":
        return (index * 4 + lax.rem(seq, 4), ctx)
    if group == "core":
        return (seq, lax.div(ctx, 2) * 2 + index)
    if group == "half":
        return (seq, index * 8 + lax.rem(ctx, 8))
    if group == "z":
        return (seq, lax.div(ctx, 8) * 8 + index * 2 + lax.rem(ctx, 2))
    return (seq, index * 2 + lax.rem(ctx, 2))


def group_peer(group, step):
    return lax.rem(group_me(group) + step, group_size(group))


def enter(groups):
    barrier = pltpu.get_barrier_semaphore()
    count = 0
    for group in groups:
        for step in range(1, group_size(group)):
            pl.semaphore_signal(
                barrier,
                inc=1,
                device_id=group_device(group, group_peer(group, step)),
                device_id_type=pl.DeviceIdType.MESH,
            )
            count += 1
    pl.semaphore_wait(barrier, count)


def remote(source, target, send, recv, group, peer):
    return pltpu.make_async_remote_copy(
        src_ref=source,
        dst_ref=target,
        send_sem=send,
        recv_sem=recv,
        device_id=group_device(group, peer),
        device_id_type=pl.DeviceIdType.MESH,
    )


def dma(*shape):
    return pltpu.SemaphoreType.DMA(shape)


class Exchange:
    def __init__(self, kind, group, source, target, refs, rows=None):
        self.kind, self.group = kind, group
        self.source, self.target, self.rows = source, target, rows
        self.send, self.recv = refs[:2]
        if rows is None:
            self.own, self.own_held = refs[2:]

    @staticmethod
    def scratch(kind, group, value, rows=None):
        count = group_size(group) - 1
        if rows is not None:
            return [dma(count), dma(count)]
        piece = value.shape if kind == "ag" else value.shape[1:]
        return [dma(count), dma(count), dma(2), pltpu.VMEM(piece, value.dtype)]

    def copies(self):
        me = group_me(self.group)
        made = []
        for step in range(1, group_size(self.group)):
            peer = group_peer(self.group, step)
            piece = self.source if self.kind == "ag" else self.source.at[peer]
            target = self.target.at[me]
            if self.rows is not None:
                piece, target = piece.at[pl.ds(*self.rows)], target.at[pl.ds(*self.rows)]
            made.append(
                remote(piece, target, self.send.at[step - 1], self.recv.at[step - 1], self.group, peer)
            )
        return made

    def own_copies(self):
        me = group_me(self.group)
        piece = self.source if self.kind == "ag" else self.source.at[me]
        return (
            pltpu.make_async_copy(piece, self.own_held, self.own.at[0]),
            pltpu.make_async_copy(self.own_held, self.target.at[me], self.own.at[1]),
        )

    def start(self):
        for copy in self.copies():
            copy.start()
        if self.rows is None:
            self.own_copies()[0].start()

    def wait(self):
        if self.rows is None:
            own_in, own_out = self.own_copies()
            own_in.wait()
            own_out.start()
            own_out.wait()
        for copy in self.copies():
            copy.wait()


class Own:
    def __init__(self, source, target, refs):
        self.source, self.target = source, target.at[group_me("seq")]
        self.sems, self.held = refs

    @staticmethod
    def scratch(value):
        return [dma(2), pltpu.VMEM(value.shape, value.dtype)]

    def start(self):
        pltpu.make_async_copy(self.source, self.held, self.sems.at[0]).start()

    def wait(self):
        pltpu.make_async_copy(self.source, self.held, self.sems.at[0]).wait()
        copy = pltpu.make_async_copy(self.held, self.target, self.sems.at[1])
        copy.start()
        copy.wait()


class RelayGather:
    def __init__(self, source, target, span, order, refs):
        self.source, self.target, self.span, self.order = source, target, span, order
        self.send, self.recv = refs
        x, y = group_me("x"), group_me("y")
        back = [lax.rem(x + 4 - step, 4) for step in range(1, 4)]
        if order == "yx":
            self.owners = [(1 - y) * 4 + x] + [y * 4 + at for at in back] + [(1 - y) * 4 + at for at in back]
        else:
            self.owners = [y * 4 + at for at in back] + [(1 - y) * 4 + x] + [(1 - y) * 4 + at for at in back]

    @staticmethod
    def scratch():
        return [dma(7), dma(7)]

    def slot(self, at):
        x, y = group_me("x"), group_me("y")
        piece = self.source.at[self.span]
        place = self.target.at[y * 4 + x, self.span]
        if self.order == "yx":
            group, step = ("y", 1) if at == 0 else ("x", (at - 1) % 3 + 1)
            if at >= 4:
                piece = place = self.target.at[self.owners[0], self.span]
        else:
            group, step = ("x", at + 1) if at < 3 else ("y", 1)
            if at >= 4:
                piece = place = self.target.at[self.owners[at - 4], self.span]
        return remote(piece, place, self.send.at[at], self.recv.at[at], group, group_peer(group, step))

    def start(self):
        for at in range(4):
            self.slot(at).start()

    def forward(self):
        if self.order == "yx":
            self.slot(0).wait_recv()
            for at in range(4, 7):
                self.slot(at).start()
        else:
            for at in range(3):
                self.slot(at).wait_recv()
                self.slot(at + 4).start()

    def waited(self):
        return (0,) if self.order == "yx" else (0, 1, 2)

    def wait_recv(self):
        for at in range(7):
            if at not in self.waited():
                self.slot(at).wait_recv()

    def wait_send(self):
        for at in range(7):
            self.slot(at).wait_send()

    def wait(self):
        self.wait_recv()
        self.wait_send()


class SplitGather:
    def __init__(self, source, target, refs):
        rows = source.shape[0] // 4
        self.span = pl.ds(pl.multiple_of(group_me("z") * rows, 16), rows)
        self.target = target
        self.relay = RelayGather(source, target, self.span, "yx", refs[:2])
        self.send, self.recv = refs[2:]

    @staticmethod
    def scratch():
        return RelayGather.scratch() + [dma(21), dma(21)]

    def second(self, slot, hop):
        at = slot * 3 + hop - 1
        piece = self.target.at[self.relay.owners[slot], self.span]
        return remote(piece, piece, self.send.at[at], self.recv.at[at], "z", group_peer("z", hop))

    def start(self):
        self.relay.start()

    def forward_x(self):
        self.relay.forward()
        for hop in range(1, 4):
            self.second(0, hop).start()

    def forward_z(self):
        for slot in range(1, 7):
            self.relay.slot(slot).wait_recv()
            for hop in range(1, 4):
                self.second(slot, hop).start()

    def wait(self):
        self.relay.wait_send()
        for slot in range(7):
            for hop in range(1, 4):
                self.second(slot, hop).wait()


class RelayReduce:
    def __init__(self, source, rows, order, refs):
        self.source, self.span, self.order = source, pl.ds(*rows), order
        self.group, self.group_two = order
        self.size, self.size_two = group_size(order[0]), group_size(order[1])
        self.send, self.recv, self.local, self.got, self.total, self.send_two, self.recv_two, self.got_two = refs

    @staticmethod
    def scratch(value, rows, order):
        piece, kind = (rows[1], value.shape[2]), value.dtype
        one, two = group_size(order[0]), group_size(order[1])
        pieces = (one - 1) * two
        return [
            dma(pieces),
            dma(pieces),
            dma(two),
            pltpu.VMEM((pieces,) + piece, kind),
            pltpu.VMEM((two,) + piece, kind),
            dma(two - 1),
            dma(two - 1),
            pltpu.VMEM((two - 1,) + piece, kind),
        ]

    def piece(self, one, two):
        return self.source.at[one * 4 + two if self.order == "yx" else two * 4 + one, self.span]

    def first(self):
        made = []
        for step in range(1, self.size):
            peer = group_peer(self.group, step)
            for two in range(self.size_two):
                at = (step - 1) * self.size_two + two
                made.append(
                    remote(
                        self.piece(peer, two), self.got.at[at], self.send.at[at], self.recv.at[at], self.group, peer
                    )
                )
        return made

    def own(self):
        return [
            pltpu.make_async_copy(
                self.piece(group_me(self.group), two), self.total.at[two], self.local.at[two]
            )
            for two in range(self.size_two)
        ]

    def second(self):
        made = []
        for step in range(1, self.size_two):
            peer = group_peer(self.group_two, step)
            made.append(
                remote(
                    self.total.at[peer],
                    self.got_two.at[step - 1],
                    self.send_two.at[step - 1],
                    self.recv_two.at[step - 1],
                    self.group_two,
                    peer,
                )
            )
        return made

    def start(self):
        for copy in self.first() + self.own():
            copy.start()

    def forward(self):
        for copy in self.own() + self.first():
            copy.wait()
        for two in range(self.size_two):
            value = self.total[two].astype(F32)
            for step in range(self.size - 1):
                value += self.got[step * self.size_two + two].astype(F32)
            self.total[two] = value.astype(self.total.dtype)
        for copy in self.second():
            copy.start()

    def sum(self):
        for copy in self.second():
            copy.wait()
        value = self.total[group_me(self.group_two)].astype(F32)
        for step in range(self.size_two - 1):
            value += self.got_two[step].astype(F32)
        return value


class SplitReduce:
    def __init__(self, source, refs):
        self.source, self.quarter = source, source.shape[1] // 4
        self.send, self.recv, self.local, self.got, self.total = refs[:5]
        self.relay = RelayReduce(self.total, (0, self.quarter), "xy", refs[5:])

    @staticmethod
    def scratch(value):
        quarter, columns = value.shape[1] // 4, value.shape[2]
        return [dma(3), dma(3), dma()] + [
            pltpu.VMEM((3, 8, quarter, columns), BF),
            pltpu.VMEM((8, quarter, columns), BF),
        ] + RelayReduce.scratch(value, (0, quarter), "xy")

    def part(self, index):
        return self.source.at[:, pl.ds(pl.multiple_of(index * self.quarter, 16), self.quarter)]

    def first(self, hop):
        peer = group_peer("z", hop)
        return remote(
            self.part(peer), self.got.at[hop - 1], self.send.at[hop - 1], self.recv.at[hop - 1], "z", peer
        )

    def own_copy(self):
        return pltpu.make_async_copy(self.part(group_me("z")), self.total, self.local)

    def start(self):
        for hop in range(1, 4):
            self.first(hop).start()
        self.own_copy().start()

    def forward_z(self):
        self.own_copy().wait()
        for hop in range(1, 4):
            self.first(hop).wait()

        def add(at, carry):
            value = self.total[at].astype(F32)
            for hop in range(3):
                value += self.got[hop, at].astype(F32)
            self.total[at] = value.astype(BF)
            return carry

        lax.fori_loop(0, 8, add, 0)
        self.relay.start()

    def forward(self):
        self.relay.forward()

    def sum(self):
        return self.relay.sum()


class Refs:
    def __init__(self, refs):
        self.refs, self.at = refs, 0

    def take(self, count):
        self.at += count
        return self.refs[self.at - count : self.at]

    def left(self):
        return self.refs[self.at :]


def target_shape(kind, group, value):
    shape = value.shape if kind == "a2a" else (group_size(group),) + value.shape
    return jax.ShapeDtypeStruct(shape, value.dtype)


def params(identifier, mebibytes):
    return pltpu.CompilerParams(
        collective_id=identifier,
        has_side_effects=True,
        vmem_limit_bytes=mebibytes * 1024 * 1024,
    )


def exchange(identifier, *items):
    number = len(items)

    def kernel(*refs):
        refs = Refs(refs)
        sources, targets = refs.take(number), refs.take(number)
        enter(sorted({item[1] for item in items}))
        made = [
            Exchange(item[0], item[1], source, target, refs.take(4))
            for item, source, target in zip(items, sources, targets)
        ]
        for one in made:
            one.start()
        for one in made:
            one.wait()

    return pl.pallas_call(
        kernel,
        out_shape=[target_shape(*item) for item in items],
        in_specs=[ANY] * number,
        out_specs=[ANY] * number,
        scratch_shapes=[ref for item in items for ref in Exchange.scratch(*item)],
        compiler_params=params(identifier, 16),
        name="exchange%d" % identifier,
    )(*[item[2] for item in items])


def gather_first(identifier, qkv, small, rows):
    def kernel(*refs):
        refs = Refs(refs)
        qkv_ref, small_ref, rows_ref = refs.take(3)
        qkv_out, small_out, rows_out = refs.take(3)
        enter(["seq", "z", "core"])
        split = SplitGather(qkv_ref.at[pl.ds(0, 64)], qkv_out, refs.take(4))
        one_way = RelayGather(qkv_ref, qkv_out, pl.ds(64, 32), "yx", refs.take(2))
        other_way = RelayGather(qkv_ref, qkv_out, pl.ds(96, 32), "xy", refs.take(2))
        own = Own(qkv_ref, qkv_out, refs.take(2))
        smalls = Exchange("ag", "seq", small_ref, small_out, refs.take(4))
        pair = Exchange("ag", "core", rows_ref, rows_out, refs.take(4))
        for one in (split, one_way, other_way, own, smalls, pair):
            one.start()
        split.forward_x()
        one_way.forward()
        split.forward_z()
        other_way.forward()
        for one in (pair, own, smalls, one_way, other_way, split):
            one.wait()

    return pl.pallas_call(
        kernel,
        out_shape=[
            target_shape("ag", "seq", qkv),
            target_shape("ag", "seq", small),
            target_shape("ag", "core", rows),
        ],
        in_specs=[ANY] * 3,
        out_specs=[ANY] * 3,
        scratch_shapes=SplitGather.scratch()
        + RelayGather.scratch()
        + RelayGather.scratch()
        + Own.scratch(qkv)
        + Exchange.scratch("ag", "seq", small)
        + Exchange.scratch("ag", "core", rows),
        compiler_params=params(identifier, 16),
        name="gather_first",
    )(qkv, small, rows)


def attend_forward(identifier, qkv, output_part, inner_part, outer_part):
    low_shape = jax.ShapeDtypeStruct((CHIPS, HD, PAIR), BF)

    def kernel(*refs):
        refs = Refs(refs)
        qkv_ref, output_ref, inner_ref, outer_ref = refs.take(4)
        qkv_got, summed_ref, back_ref, stat_ref = refs.take(4)
        output_out, inner_out, outer_out = refs.take(3)
        query_t, keys, value_t, low = refs.take(4)
        enter(["seq", "chip"])
        first = Exchange("a2a", "chip", qkv_ref, qkv_got, refs.take(4))
        last = Exchange("a2a", "chip", low, back_ref, refs.take(4))
        inner = SplitGather(inner_ref, inner_out, refs.take(4))
        output = RelayGather(output_ref, output_out, pl.ds(0, HD), "yx", refs.take(2))
        outer_one = RelayGather(outer_ref, outer_out, pl.ds(0, 128), "yx", refs.take(2))
        outer_two = RelayGather(outer_ref, outer_out, pl.ds(128, 128), "xy", refs.take(2))
        owns = [
            Own(source, target, refs.take(2))
            for source, target in (
                (output_ref, output_out),
                (inner_ref, inner_out),
                (outer_ref, outer_out),
            )
        ]
        inner.start()
        first.start()
        output.start()
        for own in owns:
            own.start()
        inner.forward_x()
        output.forward()
        first.wait()
        inner.forward_z()
        outer_two.start()
        outer_one.start()
        for chip in range(CHIPS):
            at = pl.ds(chip * PAIR, PAIR)
            query_t[:, at] = qkv_got[chip, 0:HD, :]
            keys[at, :] = qkv_got[chip, HD : 2 * HD, :].astype(F32).T.astype(BF)
            value_t[:, at] = qkv_got[chip, 2 * HD : 3 * HD, :]
        outer_one.forward()

        def one_block(block, carry):
            at = pl.ds(pl.multiple_of(block * BLOCK, BLOCK), BLOCK)
            query = query_t[:, at]
            top = jnp.full((1, BLOCK), -1e30, F32)
            total = jnp.zeros((1, BLOCK), F32)
            summed = jnp.zeros((HD, BLOCK), F32)
            for part in range(LENGTH // BLOCK):
                here = slice(part * BLOCK, (part + 1) * BLOCK)
                scores = dot(keys[here, :], query) * SCALE2
                new_top = jnp.maximum(top, jnp.max(scores, axis=0, keepdims=True))
                factor = jnp.exp2(top - new_top)
                weights = jnp.exp2(scores - new_top)
                total = total * factor + jnp.sum(weights, axis=0, keepdims=True)
                summed = summed * factor + dot(value_t[:, here], weights.astype(BF))
                top = new_top
            summed_ref[:, at] = summed / total
            stat_ref[:, at] = top + jnp.log2(total)
            return carry

        lax.fori_loop(0, LENGTH // BLOCK, one_block, 0)
        for chip in range(CHIPS):
            low[chip] = summed_ref[:, chip * PAIR : (chip + 1) * PAIR].astype(BF)
        last.start()
        outer_two.forward()
        for one in [last, output, inner, outer_one, outer_two] + owns:
            one.wait()

    return pl.pallas_call(
        kernel,
        out_shape=[
            jax.ShapeDtypeStruct(qkv.shape, BF),
            jax.ShapeDtypeStruct((HD, LENGTH), F32),
            low_shape,
            jax.ShapeDtypeStruct((1, LENGTH), F32),
        ]
        + [target_shape("ag", "seq", part) for part in (output_part, inner_part, outer_part)],
        in_specs=[VMEM] + [ANY] * 3,
        out_specs=[VMEM] * 4 + [ANY] * 3,
        scratch_shapes=[
            pltpu.VMEM((HD, LENGTH), BF),
            pltpu.VMEM((LENGTH, HD), BF),
            pltpu.VMEM((HD, LENGTH), BF),
            pltpu.VMEM((CHIPS, HD, PAIR), BF),
        ]
        + Exchange.scratch("a2a", "chip", qkv)
        + Exchange.scratch("a2a", "chip", low_shape)
        + SplitGather.scratch()
        + RelayGather.scratch()
        + RelayGather.scratch()
        + RelayGather.scratch()
        + Own.scratch(output_part)
        + Own.scratch(inner_part)
        + Own.scratch(outer_part),
        compiler_params=params(identifier, 40),
        name="attend_forward",
    )(qkv, output_part, inner_part, outer_part)


def attend_backward(identifier, qkv_got, summed, stat, grad, output_grad, inner_grad, outer_grad):
    def kernel(*refs):
        refs = Refs(refs)
        qkv_ref, summed_ref, stat_ref, grad_ref = refs.take(4)
        output_ref, inner_ref, outer_ref = refs.take(3)
        grad_got, back_ref, output_out, inner_out, outer_out = refs.take(5)
        query_t, queries, key_t, keys, values, up_t, ups, delta_ref = refs.take(8)
        grad_query, grad_key, grad_value, low = refs.take(4)
        enter(["seq", "chip"])
        first = Exchange("a2a", "chip", grad_ref, grad_got, refs.take(4))
        last = Exchange("a2a", "chip", low, back_ref, refs.take(4))
        inner = SplitReduce(inner_ref, refs.take(13))
        output = RelayReduce(output_ref, (0, HD), "xy", refs.take(8))
        outer_one = RelayReduce(outer_ref, (0, 128), "xy", refs.take(8))
        outer_two = RelayReduce(outer_ref, (128, 128), "yx", refs.take(8))
        first.start()
        for one in (inner, outer_two, output, outer_one):
            one.start()
        for chip in range(CHIPS):
            at = pl.ds(chip * PAIR, PAIR)
            query_t[:, at] = qkv_ref[chip, 0:HD, :]
            queries[at, :] = qkv_ref[chip, 0:HD, :].astype(F32).T.astype(BF)
            key_t[:, at] = qkv_ref[chip, HD : 2 * HD, :]
            keys[at, :] = qkv_ref[chip, HD : 2 * HD, :].astype(F32).T.astype(BF)
            values[at, :] = qkv_ref[chip, 2 * HD : 3 * HD, :].astype(F32).T.astype(BF)
        grad_key[...] = jnp.zeros_like(grad_key)
        grad_value[...] = jnp.zeros_like(grad_value)
        first.wait()
        for chip in range(CHIPS):
            at = pl.ds(chip * PAIR, PAIR)
            up = grad_got[chip].astype(F32)
            up_t[:, at] = grad_got[chip]
            ups[at, :] = up.T.astype(BF)
            delta_ref[:, at] = jnp.sum(up * summed_ref[:, at], axis=0, keepdims=True)
        outer_two.forward()

        def one_block(block, carry):
            at = pl.ds(pl.multiple_of(block * BLOCK, BLOCK), BLOCK)
            query, up = query_t[:, at], up_t[:, at]
            query_rows, up_rows = queries[at, :], ups[at, :]
            stat, delta = stat_ref[:, at], delta_ref[:, at]
            gathered = jnp.zeros((HD, BLOCK), F32)
            for part in range(LENGTH // BLOCK):
                here = slice(part * BLOCK, (part + 1) * BLOCK)
                scores = dot(keys[here, :], query) * SCALE2
                probs = jnp.exp2(scores - stat)
                grad_value[here, :] += dot(probs.astype(BF), up_rows)
                slope = dot(values[here, :], up) - delta
                grad_scores = (probs * slope).astype(BF)
                grad_key[here, :] += dot(grad_scores, query_rows)
                gathered += dot(key_t[:, here], grad_scores)
            grad_query[:, at] = gathered
            return carry

        lax.fori_loop(0, LENGTH // BLOCK, one_block, 0)
        scale = HD ** (-0.5)
        for chip in range(CHIPS):
            at = slice(chip * PAIR, (chip + 1) * PAIR)
            low[chip, 0:HD, :] = (grad_query[:, at] * scale).astype(BF)
            low[chip, HD : 2 * HD, :] = (grad_key[at, :] * scale).T.astype(BF)
            low[chip, 2 * HD : 3 * HD, :] = grad_value[at, :].T.astype(BF)
        output.forward()
        inner.forward_z()
        last.start()
        outer_one.forward()
        output_out[...] = output.sum()
        outer_out[128:] = outer_two.sum().astype(BF)
        outer_out[:128] = outer_one.sum().astype(BF)
        inner.forward()
        inner_out[...] = inner.sum().astype(BF)
        last.wait()

    return pl.pallas_call(
        kernel,
        out_shape=[
            jax.ShapeDtypeStruct(grad.shape, BF),
            jax.ShapeDtypeStruct(qkv_got.shape, BF),
            jax.ShapeDtypeStruct(output_grad.shape[1:], F32),
            jax.ShapeDtypeStruct((32, FF // 2), BF),
            jax.ShapeDtypeStruct(outer_grad.shape[1:], BF),
        ],
        in_specs=[VMEM] * 4 + [ANY] * 3,
        out_specs=[VMEM] * 5,
        scratch_shapes=[
            pltpu.VMEM((HD, LENGTH), BF),
            pltpu.VMEM((LENGTH, HD), BF),
            pltpu.VMEM((HD, LENGTH), BF),
            pltpu.VMEM((LENGTH, HD), BF),
            pltpu.VMEM((LENGTH, HD), BF),
            pltpu.VMEM((HD, LENGTH), BF),
            pltpu.VMEM((LENGTH, HD), BF),
            pltpu.VMEM((1, LENGTH), F32),
            pltpu.VMEM((HD, LENGTH), F32),
            pltpu.VMEM((LENGTH, HD), F32),
            pltpu.VMEM((LENGTH, HD), F32),
            pltpu.VMEM((CHIPS, 3 * HD, PAIR), BF),
        ]
        + Exchange.scratch("a2a", "chip", grad)
        + Exchange.scratch("a2a", "chip", qkv_got)
        + SplitReduce.scratch(inner_grad)
        + RelayReduce.scratch(output_grad, (0, HD), "xy")
        + RelayReduce.scratch(outer_grad, (0, 128), "xy")
        + RelayReduce.scratch(outer_grad, (128, 128), "yx"),
        compiler_params=params(identifier, 48),
        name="attend_backward",
    )(qkv_got, summed, stat, grad, output_grad, inner_grad, outer_grad)


class Scatter:
    def __init__(self, group, source, refs):
        self.group, self.source = group, source
        send, recv, self.got = refs
        self.copies = [
            remote(
                source.at[group_peer(group, step)],
                self.got.at[step - 1],
                send.at[step - 1],
                recv.at[step - 1],
                group,
                group_peer(group, step),
            )
            for step in range(1, group_size(group))
        ]

    @staticmethod
    def scratch(group, piece, kind):
        count = group_size(group) - 1
        return [dma(count), dma(count), pltpu.VMEM((count,) + piece, kind)]

    def start(self):
        for copy in self.copies:
            copy.start()

    def sum(self):
        for copy in self.copies:
            copy.wait()
        own = self.source[group_me(self.group)].astype(F32)
        return sum((self.got[at].astype(F32) for at in range(group_size(self.group) - 1)), own)


class Swap:
    def __init__(self, group, source, refs):
        send, recv, self.got = refs
        self.source = source
        self.copy = remote(source, self.got, send, recv, group, group_peer(group, 1))

    @staticmethod
    def scratch(piece, kind):
        return [dma(), dma(), pltpu.VMEM(piece, kind)]

    def start(self):
        self.copy.start()

    def sum(self):
        self.copy.wait()
        return self.source[...].astype(F32) + self.got[...].astype(F32)


class Spread:
    def __init__(self, group, held, refs):
        send, recv, send_core, recv_core = refs
        self.group, self.held = group, held
        mine = held.at[group_me("core")]
        self.mine = mine
        piece = mine.at[group_me(group)]
        self.copies = [
            remote(piece, piece, send.at[step - 1], recv.at[step - 1], group, group_peer(group, step))
            for step in range(1, group_size(group))
        ]
        self.last = remote(mine, mine, send_core, recv_core, "core", group_peer("core", 1))

    @staticmethod
    def scratch(group):
        count = group_size(group) - 1
        return [dma(count), dma(count), dma(), dma()]

    def start(self, value):
        self.mine[group_me(self.group)] = value.astype(self.held.dtype)
        for copy in self.copies:
            copy.start()

    def forward(self):
        for copy in self.copies:
            copy.wait()
        self.last.start()

    def wait(self):
        self.last.wait()


def reduce_last(identifier, rows_t, qkv_weight, grad_qkv, vectors, output_share, inner_share, outer_share):
    columns = SEQ * 3 * HD
    half = 64
    chip_piece = (16, columns)
    vector = vectors.shape[1:]

    def kernel(*refs):
        refs = Refs(refs)
        rows_ref, weight_ref, grad_ref, vectors_ref, output_ref, inner_ref, outer_ref = refs.take(7)
        token_out, qkv_out, output_out, inner_out, outer_out, vector_out, bias_out = refs.take(7)
        grads, bias, partial, token_got, token_send, token_recv = refs.take(6)
        (qkv_sum,) = refs.take(1)
        qkv_one = RelayReduce(grads, (0, half), "xy", refs.take(8))
        qkv_two = RelayReduce(grads, (half, half), "yx", refs.take(8))
        vector_seq = Scatter("seq", vectors_ref, refs.take(3))
        bias_seq = Scatter("seq", bias, refs.take(3))
        output_chip = Scatter("chip", output_ref, refs.take(3))
        outer_chip = Scatter("chip", outer_ref, refs.take(3))
        inner_half = Swap("half", inner_ref, refs.take(3))
        qkv_chip = Scatter("chip", qkv_sum, refs.take(3))
        output_all = Spread("chip", output_out, refs.take(4))
        outer_all = Spread("chip", outer_out, refs.take(4))
        inner_all = Spread("z", inner_out, refs.take(4))
        qkv_all = Spread("chip", qkv_out, refs.take(4))
        vector_all = Spread("chip", vector_out, refs.take(4))
        bias_all = Spread("chip", bias_out, refs.take(4))
        other = group_peer("core", 1)
        token = remote(partial.at[other], token_got, token_send, token_recv, "core", other)

        enter(["seq", "chip", "core"])
        for one in (inner_half, outer_chip, output_chip, vector_seq):
            one.start()

        def weight_rows(owner, carry):
            at = pl.ds(pl.multiple_of(owner * 128, 128), 128)
            grads[owner] = dot(rows_ref[at, :], grad_ref[...], ((1,), (1,))).astype(BF)
            part = pl.ds(pl.multiple_of(owner * 192, 64), 192)
            bias[owner] = dot(jnp.ones((8, PAIR), BF), grad_ref[part, :], ((1,), (1,)))
            return carry

        lax.fori_loop(0, SEQ, weight_rows, 0)
        qkv_one.start()
        qkv_two.start()
        bias_seq.start()
        turned = dot(weight_ref[...], grad_ref[...]).T
        partial[0] = turned[:ROWS]
        partial[1] = turned[ROWS:]
        token.start()
        inner_all.start(inner_half.sum())
        outer_all.start(outer_chip.sum())
        output_all.start(output_chip.sum())
        vector_all.start(vector_seq.sum())
        bias_all.start(bias_seq.sum())
        qkv_two.forward()
        qkv_one.forward()
        inner_all.forward()
        outer_all.forward()
        output_all.forward()
        token.wait()
        token_out[...] = partial[group_me("core")] + token_got[...]
        vector_all.forward()
        bias_all.forward()
        upper = qkv_one.sum().reshape(CHIPS, 8, columns)
        lower = qkv_two.sum().reshape(CHIPS, 8, columns)
        qkv_sum[...] = jnp.concatenate([upper, lower], axis=1).astype(BF)
        qkv_chip.start()
        qkv_all.start(qkv_chip.sum())
        qkv_all.forward()
        for one in (inner_all, outer_all, output_all, vector_all, bias_all, qkv_all):
            one.wait()

    return pl.pallas_call(
        kernel,
        out_shape=[
            jax.ShapeDtypeStruct((ROWS, D), F32),
            jax.ShapeDtypeStruct((2, CHIPS) + chip_piece, BF),
            jax.ShapeDtypeStruct((2, CHIPS, 8, D), F32),
            jax.ShapeDtypeStruct((2, 4, 32, FF // 2), BF),
            jax.ShapeDtypeStruct((2, CHIPS, 32, D), BF),
            jax.ShapeDtypeStruct((2, CHIPS) + vector, F32),
            jax.ShapeDtypeStruct((2, CHIPS, 8, 3 * HD), F32),
        ],
        in_specs=[VMEM] * 7,
        out_specs=[VMEM] * 7,
        scratch_shapes=[
            pltpu.VMEM((SEQ, 128, columns), BF),
            pltpu.VMEM((SEQ, 8, 3 * HD), F32),
            pltpu.VMEM((2, ROWS, D), F32),
            pltpu.VMEM((ROWS, D), F32),
            dma(),
            dma(),
            pltpu.VMEM((CHIPS,) + chip_piece, BF),
        ]
        + RelayReduce.scratch(jax.ShapeDtypeStruct((SEQ, 128, columns), BF), (0, half), "xy")
        + RelayReduce.scratch(jax.ShapeDtypeStruct((SEQ, 128, columns), BF), (half, half), "yx")
        + Scatter.scratch("seq", vector, F32)
        + Scatter.scratch("seq", (8, 3 * HD), F32)
        + Scatter.scratch("chip", (8, D), F32)
        + Scatter.scratch("chip", (32, D), BF)
        + Swap.scratch((32, FF // 2), BF)
        + Scatter.scratch("chip", chip_piece, BF)
        + Spread.scratch("chip")
        + Spread.scratch("chip")
        + Spread.scratch("z")
        + Spread.scratch("chip")
        + Spread.scratch("chip")
        + Spread.scratch("chip"),
        compiler_params=params(identifier, 48),
        name="reduce_last",
    )(rows_t, qkv_weight, grad_qkv, vectors, output_share, inner_share, outer_share)


def unpack(qkv, output, inner, outer):
    def kernel(qkv_ref, output_ref, inner_ref, outer_ref, query, key, value, output_out, inner_out, outer_out):
        def place(pair, rows):
            for kind, out in enumerate((query, key, value)):
                for head in range(SEQ):
                    at = head * 3 * HD + kind * HD
                    out[rows, head * 128 : (head + 1) * 128] = jnp.concatenate(
                        [part[:, at : at + HD] for part in pair], axis=1
                    )

        for chip in range(CHIPS):
            pair = [qkv_ref[core, chip].astype(F32) for core in range(2)]
            place([part[:8] for part in pair], slice(chip * 8, (chip + 1) * 8))
            place([part[8:] for part in pair], slice(64 + chip * 8, 64 + (chip + 1) * 8))
        for core in range(2):
            for chip in range(CHIPS):
                output_out[core * HD + chip * 8 : core * HD + (chip + 1) * 8] = output_ref[core, chip]
                start = core * 256 + chip * 32
                outer_out[start : start + 32] = outer_ref[core, chip].astype(F32)
            for quarter in range(4):
                for owner in range(SEQ):
                    start = owner * 512 + core * 256
                    inner_out[quarter * 32 : (quarter + 1) * 32, start : start + 256] = inner_ref[
                        core, quarter, :, owner * 256 : (owner + 1) * 256
                    ].astype(F32)

    shapes = [(128, D)] * 4 + [(128, FF), (512, D)]
    return pl.pallas_call(
        kernel,
        out_shape=[jax.ShapeDtypeStruct(shape, F32) for shape in shapes],
        in_specs=[VMEM] * 4,
        out_specs=[VMEM] * 6,
        compiler_params=pltpu.CompilerParams(vmem_limit_bytes=32 * 1024 * 1024),
        name="unpack",
    )(qkv, output, inner, outer)


def normalize(hidden, gain, shift):
    centered = hidden - jnp.mean(hidden, axis=-1, keepdims=True)
    inverse = lax.rsqrt(jnp.mean(centered * centered, axis=-1, keepdims=True) + 1e-05)
    normed = centered * inverse
    return (normed * gain + shift, normed, inverse)


def normalize_back(upstream, normed, inverse, gain):
    scaled = upstream * gain
    inner = (
        scaled
        - jnp.mean(scaled, axis=-1, keepdims=True)
        - normed * jnp.mean(scaled * normed, axis=-1, keepdims=True)
    )
    return (inverse * inner, jnp.sum(upstream * normed, axis=0), jnp.sum(upstream, axis=0))


def gelu_exact(value):
    return jax.nn.gelu(value, approximate=False)


def per_device(
    tokens,
    cotangent,
    w_query,
    b_query,
    w_key,
    w_value,
    b_value,
    w_output,
    b_output,
    first_gain,
    first_shift,
    w_inner,
    b_inner,
    w_outer,
    b_outer,
    second_gain,
    second_shift,
):
    core = lax.rem(lax.axis_index("ctx"), 2)
    rows = tokens[0]

    def pick(value, axis):
        return lax.dynamic_index_in_dim(value, core, axis, keepdims=False)

    qkv_part = pick(
        jnp.stack([w_query, w_key, w_value]).reshape(3, 128, SEQ, 2, HD), 3
    )
    qkv_part = jnp.transpose(qkv_part, (1, 2, 0, 3)).reshape(128, SEQ * 3 * HD)
    output_part = pick(w_output.reshape(2, HD, D), 0)
    inner_part = pick(w_inner.reshape(128, SEQ, 2, 256), 2).reshape(128, FF // 2)
    outer_part = pick(w_outer.reshape(2, 256, D), 0)
    small_part = jnp.concatenate(
        [
            jnp.stack(
                [b_query, b_value, b_output, first_gain, first_shift, b_outer, second_gain, second_shift]
            ),
            b_inner.reshape(4, 128),
            jnp.zeros((4, 128), BF),
        ]
    )
    qkv_weight, small, rows_pair = gather_first(0, qkv_part, small_part, rows)
    qkv_weight = qkv_weight.reshape(D, SEQ * 3 * HD)
    rows_pair = rows_pair.reshape(PAIR, D)
    small = small.astype(F32)
    query_bias = pick(small[:, 0].reshape(SEQ, 2, HD), 1)
    value_bias = pick(small[:, 1].reshape(SEQ, 2, HD), 1)
    qkv_bias = jnp.stack([query_bias, jnp.zeros_like(query_bias), value_bias], axis=1)
    output_bias, norm_gain, norm_shift, outer_bias, final_gain, final_shift = (
        small[:, at].reshape(D) for at in range(2, 8)
    )
    inner_bias = pick(small[:, 8:12].reshape(SEQ, 2, 256), 1).reshape(FF // 2)

    qkv = (dot(qkv_weight, rows_pair, ((0,), (1,))) + qkv_bias.reshape(-1, 1)).astype(BF)
    qkv_got, summed, attended, stat, output_weight, inner_weight, outer_weight = attend_forward(
        1,
        qkv.reshape(CHIPS, 3 * HD, PAIR),
        output_part,
        inner_part,
        outer_part,
    )
    attended = attended.reshape(D // 2, PAIR)
    output_weight = output_weight.reshape(D // 2, D)
    inner_weight = inner_weight.reshape(D, FF // 2)
    outer_weight = outer_weight.reshape(FF // 2, D)

    def core_sum(identifier, partial):
        (got,) = exchange(identifier, ("a2a", "core", partial.reshape(2, ROWS, D)))
        return got[0] + got[1]

    def core_pair(identifier, value):
        (got,) = exchange(identifier, ("ag", "core", value))
        return got.reshape(PAIR, D)

    branch = core_sum(2, dot(attended, output_weight, ((0,), (0,)))) + output_bias
    middle, unit_one, inverse_one = normalize(rows.astype(F32) + branch, norm_gain, norm_shift)
    middle_pair = core_pair(3, middle.astype(BF))
    inner = dot(middle_pair, inner_weight) + inner_bias
    active, gelu_pull = jax.vjp(gelu_exact, inner)
    active_low = active.astype(BF)
    outer = core_sum(4, dot(active_low, outer_weight)) + outer_bias
    result, unit_two, inverse_two = normalize(middle + outer, final_gain, final_shift)
    upstream = cotangent[0].astype(F32)
    grad_mid, grad_final_gain, grad_final_shift = normalize_back(
        upstream, unit_two, inverse_two, final_gain
    )
    grad_outer_low = grad_mid.astype(BF)
    grad_outer_bias = jnp.sum(grad_outer_low.astype(F32), axis=0)
    grad_outer_pair = core_pair(5, grad_outer_low)
    grad_outer_weight = dot(active_low, grad_outer_pair, ((0,), (0,))).astype(BF)
    grad_active = dot(grad_outer_pair, outer_weight, ((1,), (1,)))
    grad_inner_low = gelu_pull(grad_active)[0].astype(BF)
    grad_inner_weight = dot(middle_pair, grad_inner_low, ((0,), (0,))).astype(BF)
    grad_inner_bias = jnp.sum(grad_inner_low.astype(F32), axis=0)
    grad_middle = core_sum(6, dot(grad_inner_low, inner_weight, ((1,), (1,)))) + grad_mid
    grad_residual, grad_norm_gain, grad_norm_shift = normalize_back(
        grad_middle, unit_one, inverse_one, norm_gain
    )
    grad_branch_low = grad_residual.astype(BF)
    grad_output_bias = jnp.sum(grad_branch_low.astype(F32), axis=0)
    grad_branch_pair = core_pair(7, grad_branch_low)
    grad_output_weight = dot(attended, grad_branch_pair).astype(BF)
    grad_attended = dot(output_weight, grad_branch_pair, ((1,), (1,))).astype(BF)

    ignored, grad_qkv, output_share, inner_share, outer_share = attend_backward(
        8,
        qkv_got,
        summed,
        stat,
        grad_attended.reshape(CHIPS, HD, PAIR),
        grad_output_weight.reshape(SEQ, HD, D),
        grad_inner_weight.reshape(SEQ, 128, FF // 2),
        grad_outer_weight.reshape(SEQ, 256, D),
    )
    vectors = jnp.concatenate(
        [
            jnp.stack(
                [
                    grad_output_bias,
                    grad_norm_gain,
                    grad_norm_shift,
                    grad_outer_bias,
                    grad_final_gain,
                    grad_final_shift,
                ]
            )
            .reshape(6, SEQ, 128)
            .transpose(1, 0, 2),
            grad_inner_bias.reshape(SEQ, 2, 128),
        ],
        axis=1,
    )
    token_part, qkv_share, output_share, inner_share, outer_share, vectors, biases = reduce_last(
        9,
        rows_pair.T,
        qkv_weight,
        grad_qkv.reshape(SEQ * 3 * HD, PAIR),
        vectors,
        output_share.reshape(CHIPS, 8, D),
        inner_share,
        outer_share.reshape(CHIPS, 32, D),
    )
    grad_tokens = grad_residual + token_part
    grad_query, grad_key, grad_value, grad_output, grad_inner, grad_outer = unpack(
        qkv_share, output_share, inner_share, outer_share
    )
    vectors, biases = jnp.sum(vectors, axis=1), jnp.sum(biases[:, :, 0], axis=1)
    whole = vectors[0, :6] + vectors[1, :6]
    grad_query_bias = biases[:, :HD].reshape(128)
    grad_value_bias = biases[:, 2 * HD :].reshape(128)
    grad_inner_bias = vectors[:, 6:].reshape(512)
    return (
        result.astype(BF)[None],
        grad_tokens[None],
        grad_query,
        grad_query_bias,
        grad_key,
        grad_value,
        grad_value_bias,
        grad_output,
        whole[0],
        whole[1],
        whole[2],
        grad_inner,
        grad_inner_bias,
        grad_outer,
        whole[3],
        whole[4],
        whole[5],
    )


def solution(mesh):
    row = P("seq", None)
    vector = P("seq")
    placed = P("seq", "ctx", None)
    return jax.shard_map(
        per_device,
        mesh=mesh,
        in_specs=(
            placed,
            placed,
            row,
            vector,
            row,
            row,
            vector,
            row,
            vector,
            vector,
            vector,
            row,
            vector,
            row,
            vector,
            vector,
            vector,
        ),
        out_specs=(
            placed,
            placed,
            row,
            vector,
            row,
            row,
            vector,
            row,
            vector,
            vector,
            vector,
            row,
            vector,
            row,
            vector,
            vector,
            vector,
        ),
        check_vma=False,
    )
```

```python
import functools
import math

import jax
import jax.numpy as jnp
from jax import lax
from jax.experimental import pallas as pl
from jax.experimental.pallas import tpu as pltpu
from jax.sharding import PartitionSpec as P

D = 1024
HEADS = 16
HD = 64
FF = 4096
SEQ = 8
CHIPS = 8
ROWS = 192
PAIR = 2 * ROWS
LENGTH = CHIPS * PAIR
SCALE2 = HD ** (-0.5) * math.log2(math.e)
BLOCK = 512
BF = jnp.bfloat16
F32 = jnp.float32
ANY = pl.BlockSpec(memory_space=pl.ANY)
VMEM = pl.BlockSpec(memory_space=pltpu.VMEM)


def dot(left, right, dims=((1,), (0,))):
    return lax.dot_general(left, right, (dims, ((), ())), preferred_element_type=F32)


SIZES = {"seq": 8, "chip": 8, "x": 4, "y": 2, "z": 4, "half": 2, "core": 2}


def group_size(group):
    return SIZES[group]


def group_me(group):
    seq, ctx = lax.axis_index("seq"), lax.axis_index("ctx")
    if group == "seq":
        return seq
    if group == "x":
        return lax.rem(seq, 4)
    if group == "y":
        return lax.div(seq, 4)
    if group == "core":
        return lax.rem(ctx, 2)
    if group == "half":
        return lax.div(ctx, 8)
    if group == "z":
        return lax.rem(lax.div(ctx, 2), 4)
    return lax.div(ctx, 2)


def group_device(group, index):
    seq, ctx = lax.axis_index("seq"), lax.axis_index("ctx")
    if group == "seq":
        return (index, ctx)
    if group == "x":
        return (lax.div(seq, 4) * 4 + index, ctx)
    if group == "y":
        return (index * 4 + lax.rem(seq, 4), ctx)
    if group == "core":
        return (seq, lax.div(ctx, 2) * 2 + index)
    if group == "half":
        return (seq, index * 8 + lax.rem(ctx, 8))
    if group == "z":
        return (seq, lax.div(ctx, 8) * 8 + index * 2 + lax.rem(ctx, 2))
    return (seq, index * 2 + lax.rem(ctx, 2))


def group_peer(group, step):
    return lax.rem(group_me(group) + step, group_size(group))


def enter(groups):
    barrier = pltpu.get_barrier_semaphore()
    count = 0
    for group in groups:
        for step in range(1, group_size(group)):
            pl.semaphore_signal(
                barrier,
                inc=1,
                device_id=group_device(group, group_peer(group, step)),
                device_id_type=pl.DeviceIdType.MESH,
            )
            count += 1
    pl.semaphore_wait(barrier, count)


def remote(source, target, send, recv, group, peer):
    return pltpu.make_async_remote_copy(
        src_ref=source,
        dst_ref=target,
        send_sem=send,
        recv_sem=recv,
        device_id=group_device(group, peer),
        device_id_type=pl.DeviceIdType.MESH,
    )


def dma(*shape):
    return pltpu.SemaphoreType.DMA(shape)


class Exchange:
    def __init__(self, kind, group, source, target, refs, rows=None):
        self.kind, self.group = kind, group
        self.source, self.target, self.rows = source, target, rows
        self.send, self.recv = refs[:2]
        if rows is None:
            self.own, self.own_held = refs[2:]

    @staticmethod
    def scratch(kind, group, value, rows=None):
        count = group_size(group) - 1
        if rows is not None:
            return [dma(count), dma(count)]
        piece = value.shape if kind == "ag" else value.shape[1:]
        return [dma(count), dma(count), dma(2), pltpu.VMEM(piece, value.dtype)]

    def copies(self):
        me = group_me(self.group)
        made = []
        for step in range(1, group_size(self.group)):
            peer = group_peer(self.group, step)
            piece = self.source if self.kind == "ag" else self.source.at[peer]
            target = self.target.at[me]
            if self.rows is not None:
                piece, target = piece.at[pl.ds(*self.rows)], target.at[pl.ds(*self.rows)]
            made.append(
                remote(piece, target, self.send.at[step - 1], self.recv.at[step - 1], self.group, peer)
            )
        return made

    def own_copies(self):
        me = group_me(self.group)
        piece = self.source if self.kind == "ag" else self.source.at[me]
        return (
            pltpu.make_async_copy(piece, self.own_held, self.own.at[0]),
            pltpu.make_async_copy(self.own_held, self.target.at[me], self.own.at[1]),
        )

    def start(self):
        for copy in self.copies():
            copy.start()
        if self.rows is None:
            self.own_copies()[0].start()

    def wait(self):
        if self.rows is None:
            own_in, own_out = self.own_copies()
            own_in.wait()
            own_out.start()
            own_out.wait()
        for copy in self.copies():
            copy.wait()


class Own:
    def __init__(self, source, target, refs):
        self.source, self.target = source, target.at[group_me("seq")]
        self.sems, self.held = refs

    @staticmethod
    def scratch(value):
        return [dma(2), pltpu.VMEM(value.shape, value.dtype)]

    def start(self):
        pltpu.make_async_copy(self.source, self.held, self.sems.at[0]).start()

    def wait(self):
        pltpu.make_async_copy(self.source, self.held, self.sems.at[0]).wait()
        copy = pltpu.make_async_copy(self.held, self.target, self.sems.at[1])
        copy.start()
        copy.wait()


class RelayGather:
    def __init__(self, source, target, span, order, refs):
        self.source, self.target, self.span, self.order = source, target, span, order
        self.send, self.recv = refs
        x, y = group_me("x"), group_me("y")
        back = [lax.rem(x + 4 - step, 4) for step in range(1, 4)]
        if order == "yx":
            self.owners = [(1 - y) * 4 + x] + [y * 4 + at for at in back] + [(1 - y) * 4 + at for at in back]
        else:
            self.owners = [y * 4 + at for at in back] + [(1 - y) * 4 + x] + [(1 - y) * 4 + at for at in back]

    @staticmethod
    def scratch():
        return [dma(7), dma(7)]

    def slot(self, at):
        x, y = group_me("x"), group_me("y")
        piece = self.source.at[self.span]
        place = self.target.at[y * 4 + x, self.span]
        if self.order == "yx":
            group, step = ("y", 1) if at == 0 else ("x", (at - 1) % 3 + 1)
            if at >= 4:
                piece = place = self.target.at[self.owners[0], self.span]
        else:
            group, step = ("x", at + 1) if at < 3 else ("y", 1)
            if at >= 4:
                piece = place = self.target.at[self.owners[at - 4], self.span]
        return remote(piece, place, self.send.at[at], self.recv.at[at], group, group_peer(group, step))

    def start(self):
        for at in range(4):
            self.slot(at).start()

    def forward(self):
        if self.order == "yx":
            self.slot(0).wait_recv()
            for at in range(4, 7):
                self.slot(at).start()
        else:
            for at in range(3):
                self.slot(at).wait_recv()
                self.slot(at + 4).start()

    def waited(self):
        return (0,) if self.order == "yx" else (0, 1, 2)

    def wait_recv(self):
        for at in range(7):
            if at not in self.waited():
                self.slot(at).wait_recv()

    def wait_send(self):
        for at in range(7):
            self.slot(at).wait_send()

    def wait(self):
        self.wait_recv()
        self.wait_send()


class SplitGather:
    def __init__(self, source, target, refs):
        rows = source.shape[0] // 4
        self.span = pl.ds(pl.multiple_of(group_me("z") * rows, 16), rows)
        self.target = target
        self.relay = RelayGather(source, target, self.span, "yx", refs[:2])
        self.send, self.recv = refs[2:]

    @staticmethod
    def scratch():
        return RelayGather.scratch() + [dma(21), dma(21)]

    def second(self, slot, hop):
        at = slot * 3 + hop - 1
        piece = self.target.at[self.relay.owners[slot], self.span]
        return remote(piece, piece, self.send.at[at], self.recv.at[at], "z", group_peer("z", hop))

    def start(self):
        self.relay.start()

    def forward_x(self):
        self.relay.forward()
        for hop in range(1, 4):
            self.second(0, hop).start()

    def forward_z(self):
        for slot in range(1, 7):
            self.relay.slot(slot).wait_recv()
            for hop in range(1, 4):
                self.second(slot, hop).start()

    def wait(self):
        self.relay.wait_send()
        for slot in range(7):
            for hop in range(1, 4):
                self.second(slot, hop).wait()


class RelayReduce:
    def __init__(self, source, rows, order, refs):
        self.source, self.span, self.order = source, pl.ds(*rows), order
        self.group, self.group_two = order
        self.size, self.size_two = group_size(order[0]), group_size(order[1])
        self.send, self.recv, self.local, self.got, self.total, self.send_two, self.recv_two, self.got_two = refs

    @staticmethod
    def scratch(value, rows, order):
        piece, kind = (rows[1], value.shape[2]), value.dtype
        one, two = group_size(order[0]), group_size(order[1])
        pieces = (one - 1) * two
        return [
            dma(pieces),
            dma(pieces),
            dma(two),
            pltpu.VMEM((pieces,) + piece, kind),
            pltpu.VMEM((two,) + piece, kind),
            dma(two - 1),
            dma(two - 1),
            pltpu.VMEM((two - 1,) + piece, kind),
        ]

    def piece(self, one, two):
        return self.source.at[one * 4 + two if self.order == "yx" else two * 4 + one, self.span]

    def first(self):
        made = []
        for step in range(1, self.size):
            peer = group_peer(self.group, step)
            for two in range(self.size_two):
                at = (step - 1) * self.size_two + two
                made.append(
                    remote(
                        self.piece(peer, two), self.got.at[at], self.send.at[at], self.recv.at[at], self.group, peer
                    )
                )
        return made

    def own(self):
        return [
            pltpu.make_async_copy(
                self.piece(group_me(self.group), two), self.total.at[two], self.local.at[two]
            )
            for two in range(self.size_two)
        ]

    def second(self):
        made = []
        for step in range(1, self.size_two):
            peer = group_peer(self.group_two, step)
            made.append(
                remote(
                    self.total.at[peer],
                    self.got_two.at[step - 1],
                    self.send_two.at[step - 1],
                    self.recv_two.at[step - 1],
                    self.group_two,
                    peer,
                )
            )
        return made

    def start(self):
        for copy in self.first() + self.own():
            copy.start()

    def forward(self):
        for copy in self.own() + self.first():
            copy.wait()
        for two in range(self.size_two):
            value = self.total[two].astype(F32)
            for step in range(self.size - 1):
                value += self.got[step * self.size_two + two].astype(F32)
            self.total[two] = value.astype(self.total.dtype)
        for copy in self.second():
            copy.start()

    def sum(self):
        for copy in self.second():
            copy.wait()
        value = self.total[group_me(self.group_two)].astype(F32)
        for step in range(self.size_two - 1):
            value += self.got_two[step].astype(F32)
        return value


class SplitReduce:
    def __init__(self, source, refs):
        self.source, self.quarter = source, source.shape[1] // 4
        self.send, self.recv, self.local, self.got, self.total = refs[:5]
        self.relay = RelayReduce(self.total, (0, self.quarter), "xy", refs[5:])

    @staticmethod
    def scratch(value):
        quarter, columns = value.shape[1] // 4, value.shape[2]
        return [dma(3), dma(3), dma()] + [
            pltpu.VMEM((3, 8, quarter, columns), BF),
            pltpu.VMEM((8, quarter, columns), BF),
        ] + RelayReduce.scratch(value, (0, quarter), "xy")

    def part(self, index):
        return self.source.at[:, pl.ds(pl.multiple_of(index * self.quarter, 16), self.quarter)]

    def first(self, hop):
        peer = group_peer("z", hop)
        return remote(
            self.part(peer), self.got.at[hop - 1], self.send.at[hop - 1], self.recv.at[hop - 1], "z", peer
        )

    def own_copy(self):
        return pltpu.make_async_copy(self.part(group_me("z")), self.total, self.local)

    def start(self):
        for hop in range(1, 4):
            self.first(hop).start()
        self.own_copy().start()

    def forward_z(self):
        self.own_copy().wait()
        for hop in range(1, 4):
            self.first(hop).wait()

        def add(at, carry):
            value = self.total[at].astype(F32)
            for hop in range(3):
                value += self.got[hop, at].astype(F32)
            self.total[at] = value.astype(BF)
            return carry

        lax.fori_loop(0, 8, add, 0)
        self.relay.start()

    def forward(self):
        self.relay.forward()

    def sum(self):
        return self.relay.sum()


class Refs:
    def __init__(self, refs):
        self.refs, self.at = refs, 0

    def take(self, count):
        self.at += count
        return self.refs[self.at - count : self.at]

    def left(self):
        return self.refs[self.at :]


def target_shape(kind, group, value):
    shape = value.shape if kind == "a2a" else (group_size(group),) + value.shape
    return jax.ShapeDtypeStruct(shape, value.dtype)


def params(identifier, mebibytes):
    return pltpu.CompilerParams(
        collective_id=identifier,
        has_side_effects=True,
        vmem_limit_bytes=mebibytes * 1024 * 1024,
    )


def exchange(identifier, *items):
    number = len(items)

    def kernel(*refs):
        refs = Refs(refs)
        sources, targets = refs.take(number), refs.take(number)
        enter(sorted({item[1] for item in items}))
        made = [
            Exchange(item[0], item[1], source, target, refs.take(4))
            for item, source, target in zip(items, sources, targets)
        ]
        for one in made:
            one.start()
        for one in made:
            one.wait()

    return pl.pallas_call(
        kernel,
        out_shape=[target_shape(*item) for item in items],
        in_specs=[ANY] * number,
        out_specs=[ANY] * number,
        scratch_shapes=[ref for item in items for ref in Exchange.scratch(*item)],
        compiler_params=params(identifier, 16),
        name="exchange%d" % identifier,
    )(*[item[2] for item in items])


def forward(identifier, rows, qkv_part, bias_part, small_part, w_output, w_inner, w_outer):
    columns = SEQ * 3 * HD
    heads_shape = jax.ShapeDtypeStruct((CHIPS, 3 * HD, PAIR), BF)
    low_shape = jax.ShapeDtypeStruct((CHIPS, HD, PAIR), BF)
    output_part = jax.ShapeDtypeStruct((HD, D), BF)
    inner_part = jax.ShapeDtypeStruct((128, FF // 2), BF)
    outer_part = jax.ShapeDtypeStruct((256, D), BF)

    def kernel(*refs):
        refs = Refs(refs)
        rows_ref, qkv_ref, bias_ref, small_ref, output_ref, inner_ref, outer_ref = refs.take(7)
        rows_out, qkv_out, small_out, output_out, inner_out, outer_out = refs.take(6)
        qkv_got, summed_ref, back_ref, stat_ref = refs.take(4)
        inner_held, bias_got, heads, query_t, keys, value_t, low = refs.take(7)
        core = group_me("core")
        output_ref = output_ref.at[pl.ds(pl.multiple_of(core * HD, HD), HD)]
        outer_ref = outer_ref.at[pl.ds(pl.multiple_of(core * 256, 256), 256)]
        split = SplitGather(qkv_ref.at[pl.ds(0, 64)], qkv_out, refs.take(4))
        one_way = RelayGather(qkv_ref, qkv_out, pl.ds(64, 32), "yx", refs.take(2))
        other_way = RelayGather(qkv_ref, qkv_out, pl.ds(96, 32), "xy", refs.take(2))
        qkv_own = Own(qkv_ref, qkv_out, refs.take(2))
        bias = Exchange("ag", "seq", bias_ref, bias_got, refs.take(4))
        small = Exchange("ag", "seq", small_ref, small_out, refs.take(4))
        pair = Exchange("ag", "core", rows_ref, rows_out, refs.take(4))
        first = Exchange("a2a", "chip", heads, qkv_got, refs.take(4))
        last = Exchange("a2a", "chip", low, back_ref, refs.take(4))
        inner = SplitGather(inner_held, inner_out, refs.take(4))
        output = RelayGather(output_ref, output_out, pl.ds(0, HD), "yx", refs.take(2))
        outer_one = RelayGather(outer_ref, outer_out, pl.ds(0, 128), "yx", refs.take(2))
        outer_two = RelayGather(outer_ref, outer_out, pl.ds(128, 128), "xy", refs.take(2))
        owns = [
            Own(source, target, refs.take(2))
            for source, target in (
                (output_ref, output_out),
                (inner_held, inner_out),
                (outer_ref, outer_out),
            )
        ]
        enter(["seq", "chip", "core"])
        for one in (split, one_way, other_way, qkv_own, bias, pair, small):
            one.start()
        for owner in range(SEQ):
            here = pl.ds(pl.multiple_of(owner * 512 + core * 256, 256), 256)
            inner_held[:, owner * 256 : (owner + 1) * 256] = inner_ref[:, here]
        for own in owns:
            own.start()
        split.forward_x()
        one_way.forward()
        split.forward_z()
        inner.start()
        outer_two.start()
        other_way.forward()
        for one in (pair, bias, qkv_own, one_way, other_way, split):
            one.wait()
        inner.forward_x()
        weight = qkv_out[...].reshape(D, columns)
        turned = dot(rows_out[...].reshape(PAIR, D), weight).T
        for chip in range(CHIPS):
            shift = bias_got[chip].T[: 3 * HD, 0:1]
            heads[chip] = (turned[chip * 3 * HD : (chip + 1) * 3 * HD] + shift).astype(BF)
        first.start()
        output.start()
        outer_one.start()
        inner.forward_z()
        output.forward()
        first.wait()
        for chip in range(CHIPS):
            at = pl.ds(chip * PAIR, PAIR)
            query_t[:, at] = qkv_got[chip, 0:HD, :]
            keys[at, :] = qkv_got[chip, HD : 2 * HD, :].astype(F32).T.astype(BF)
            value_t[:, at] = qkv_got[chip, 2 * HD : 3 * HD, :]
        outer_one.forward()

        def one_block(block, carry):
            at = pl.ds(pl.multiple_of(block * BLOCK, BLOCK), BLOCK)
            query = query_t[:, at]
            top = jnp.full((1, BLOCK), -1e30, F32)
            total = jnp.zeros((1, BLOCK), F32)
            summed = jnp.zeros((HD, BLOCK), F32)
            for part in range(LENGTH // BLOCK):
                here = slice(part * BLOCK, (part + 1) * BLOCK)
                scores = dot(keys[here, :], query) * SCALE2
                new_top = jnp.maximum(top, jnp.max(scores, axis=0, keepdims=True))
                factor = jnp.exp2(top - new_top)
                weights = jnp.exp2(scores - new_top)
                total = total * factor + jnp.sum(weights, axis=0, keepdims=True)
                summed = summed * factor + dot(value_t[:, here], weights.astype(BF))
                top = new_top
            summed_ref[:, at] = summed / total
            stat_ref[:, at] = top + jnp.log2(total)
            return carry

        lax.fori_loop(0, 2, one_block, 0)
        outer_two.forward()
        lax.fori_loop(2, LENGTH // BLOCK, one_block, 0)
        for chip in range(CHIPS):
            low[chip] = summed_ref[:, chip * PAIR : (chip + 1) * PAIR].astype(BF)
        last.start()
        for one in [last, small, output, inner, outer_one, outer_two] + owns:
            one.wait()

    return pl.pallas_call(
        kernel,
        out_shape=[
            target_shape("ag", "core", rows),
            target_shape("ag", "seq", qkv_part),
            target_shape("ag", "seq", small_part),
            target_shape("ag", "seq", output_part),
            target_shape("ag", "seq", inner_part),
            target_shape("ag", "seq", outer_part),
            heads_shape,
            jax.ShapeDtypeStruct((HD, LENGTH), F32),
            low_shape,
            jax.ShapeDtypeStruct((1, LENGTH), F32),
        ],
        in_specs=[ANY] * 5 + [VMEM, ANY],
        out_specs=[VMEM, VMEM] + [ANY] * 4 + [VMEM] * 4,
        scratch_shapes=[
            pltpu.VMEM(inner_part.shape, BF),
            pltpu.VMEM((SEQ,) + bias_part.shape, F32),
            pltpu.VMEM(heads_shape.shape, BF),
            pltpu.VMEM((HD, LENGTH), BF),
            pltpu.VMEM((LENGTH, HD), BF),
            pltpu.VMEM((HD, LENGTH), BF),
            pltpu.VMEM(low_shape.shape, BF),
        ]
        + SplitGather.scratch()
        + RelayGather.scratch()
        + RelayGather.scratch()
        + Own.scratch(qkv_part)
        + Exchange.scratch("ag", "seq", bias_part)
        + Exchange.scratch("ag", "seq", small_part)
        + Exchange.scratch("ag", "core", rows)
        + Exchange.scratch("a2a", "chip", heads_shape)
        + Exchange.scratch("a2a", "chip", low_shape)
        + SplitGather.scratch()
        + RelayGather.scratch()
        + RelayGather.scratch()
        + RelayGather.scratch()
        + Own.scratch(output_part)
        + Own.scratch(inner_part)
        + Own.scratch(outer_part),
        compiler_params=params(identifier, 48),
        name="forward",
    )(rows, qkv_part, bias_part, small_part, w_output, w_inner, w_outer)


class Scatter:
    def __init__(self, group, source, refs):
        self.group, self.source = group, source
        send, recv, self.got = refs
        self.copies = [
            remote(
                source.at[group_peer(group, step)],
                self.got.at[step - 1],
                send.at[step - 1],
                recv.at[step - 1],
                group,
                group_peer(group, step),
            )
            for step in range(1, group_size(group))
        ]

    @staticmethod
    def scratch(group, piece, kind):
        count = group_size(group) - 1
        return [dma(count), dma(count), pltpu.VMEM((count,) + piece, kind)]

    def start(self):
        for copy in self.copies:
            copy.start()

    def sum(self):
        for copy in self.copies:
            copy.wait()
        own = self.source[group_me(self.group)].astype(F32)
        return sum((self.got[at].astype(F32) for at in range(group_size(self.group) - 1)), own)


class Swap:
    def __init__(self, group, source, refs):
        send, recv, self.got = refs
        self.source = source
        self.copy = remote(source, self.got, send, recv, group, group_peer(group, 1))

    @staticmethod
    def scratch(piece, kind):
        return [dma(), dma(), pltpu.VMEM(piece, kind)]

    def start(self):
        self.copy.start()

    def sum(self):
        self.copy.wait()
        return self.source[...].astype(F32) + self.got[...].astype(F32)


class Spread:
    def __init__(self, group, held, refs):
        send, recv, send_core, recv_core = refs
        self.group, self.held = group, held
        mine = held.at[group_me("core")]
        self.mine = mine
        piece = mine.at[group_me(group)]
        self.copies = [
            remote(piece, piece, send.at[step - 1], recv.at[step - 1], group, group_peer(group, step))
            for step in range(1, group_size(group))
        ]
        self.last = remote(mine, mine, send_core, recv_core, "core", group_peer("core", 1))

    @staticmethod
    def scratch(group):
        count = group_size(group) - 1
        return [dma(count), dma(count), dma(), dma()]

    def start(self, value):
        self.mine[group_me(self.group)] = value.astype(self.held.dtype)
        for copy in self.copies:
            copy.start()

    def forward(self):
        for copy in self.copies:
            copy.wait()
        self.last.start()

    def wait(self):
        self.last.wait()


def backward(
    identifier, qkv_got, summed, stat, grad, rows_t, qkv_weight, vectors, output_grad, inner_grad, outer_grad
):
    columns = SEQ * 3 * HD
    half = 64
    chip_piece = (16, columns)
    vector = vectors.shape[1:]
    grads_shape = jax.ShapeDtypeStruct((SEQ, 128, columns), BF)
    inner_half_shape = jax.ShapeDtypeStruct((SEQ, 64, FF // 2), BF)

    def kernel(*refs):
        refs = Refs(refs)
        qkv_ref, summed_ref, stat_ref, grad_ref, rows_ref, weight_ref, vectors_ref = refs.take(7)
        output_ref, inner_ref, outer_ref = refs.take(3)
        token_out, qkv_out, output_out, inner_out, outer_out, vector_out, bias_out = refs.take(7)
        grad_got, heads_got, query_t, queries, key_t, keys, values, up_t, ups, delta_ref = refs.take(10)
        grad_query, grad_key, grad_value, low = refs.take(4)
        grads, bias, partial, token_got, token_send, token_recv = refs.take(6)
        output_sum, outer_sum, output_mine, inner_mine, outer_mine, qkv_sum = refs.take(6)
        first = Exchange("a2a", "chip", grad_ref, grad_got, refs.take(4))
        last = Exchange("a2a", "chip", low, heads_got, refs.take(4))
        inner_one = SplitReduce(inner_ref.at[:, pl.ds(0, 64)], refs.take(13))
        inner_two = SplitReduce(inner_ref.at[:, pl.ds(64, 64)], refs.take(13))
        output = RelayReduce(output_ref, (0, HD), "xy", refs.take(8))
        outer_one = RelayReduce(outer_ref, (0, 128), "xy", refs.take(8))
        outer_two = RelayReduce(outer_ref, (128, 128), "yx", refs.take(8))
        qkv_one = RelayReduce(grads, (0, half), "xy", refs.take(8))
        qkv_two = RelayReduce(grads, (half, half), "yx", refs.take(8))
        vector_seq = Scatter("seq", vectors_ref, refs.take(3))
        bias_seq = Scatter("seq", bias, refs.take(3))
        output_z = Scatter("z", output_sum, refs.take(3))
        outer_z = Scatter("z", outer_sum, refs.take(3))
        output_half = Swap("half", output_mine, refs.take(3))
        outer_half = Swap("half", outer_mine, refs.take(3))
        inner_half = Swap("half", inner_mine, refs.take(3))
        qkv_chip = Scatter("chip", qkv_sum, refs.take(3))
        output_all = Spread("z", output_out, refs.take(4))
        outer_all = Spread("z", outer_out, refs.take(4))
        inner_all = Spread("z", inner_out, refs.take(4))
        qkv_all = Spread("chip", qkv_out, refs.take(4))
        vector_all = Spread("chip", vector_out, refs.take(4))
        bias_all = Spread("chip", bias_out, refs.take(4))
        other = group_peer("core", 1)
        token = remote(partial.at[other], token_got, token_send, token_recv, "core", other)

        enter(["seq", "chip", "core"])
        for one in (first, inner_one, outer_two, output, outer_one, vector_seq):
            one.start()
        for chip in range(CHIPS):
            at = pl.ds(chip * PAIR, PAIR)
            query_t[:, at] = qkv_ref[chip, 0:HD, :]
            queries[at, :] = qkv_ref[chip, 0:HD, :].astype(F32).T.astype(BF)
            key_t[:, at] = qkv_ref[chip, HD : 2 * HD, :]
            keys[at, :] = qkv_ref[chip, HD : 2 * HD, :].astype(F32).T.astype(BF)
            values[at, :] = qkv_ref[chip, 2 * HD : 3 * HD, :].astype(F32).T.astype(BF)
        grad_key[...] = jnp.zeros_like(grad_key)
        grad_value[...] = jnp.zeros_like(grad_value)
        first.wait()
        for chip in range(CHIPS):
            at = pl.ds(chip * PAIR, PAIR)
            up = grad_got[chip].astype(F32)
            up_t[:, at] = grad_got[chip]
            ups[at, :] = up.T.astype(BF)
            delta_ref[:, at] = jnp.sum(up * summed_ref[:, at], axis=0, keepdims=True)

        def one_block(block, carry):
            at = pl.ds(pl.multiple_of(block * BLOCK, BLOCK), BLOCK)
            query, up = query_t[:, at], up_t[:, at]
            query_rows, up_rows = queries[at, :], ups[at, :]
            stat, delta = stat_ref[:, at], delta_ref[:, at]
            gathered = jnp.zeros((HD, BLOCK), F32)
            for part in range(LENGTH // BLOCK):
                here = slice(part * BLOCK, (part + 1) * BLOCK)
                scores = dot(keys[here, :], query) * SCALE2
                probs = jnp.exp2(scores - stat)
                grad_value[here, :] += dot(probs.astype(BF), up_rows)
                slope = dot(values[here, :], up) - delta
                grad_scores = (probs * slope).astype(BF)
                grad_key[here, :] += dot(grad_scores, query_rows)
                gathered += dot(key_t[:, here], grad_scores)
            grad_query[:, at] = gathered
            return carry

        lax.fori_loop(0, LENGTH // BLOCK, one_block, 0)
        scale = HD ** (-0.5)
        for chip in range(CHIPS):
            at = slice(chip * PAIR, (chip + 1) * PAIR)
            low[chip, 0:HD, :] = (grad_query[:, at] * scale).astype(BF)
            low[chip, HD : 2 * HD, :] = (grad_key[at, :] * scale).T.astype(BF)
            low[chip, 2 * HD : 3 * HD, :] = grad_value[at, :].T.astype(BF)
        last.start()
        output.forward()
        outer_two.forward()
        outer_one.forward()
        vector_all.start(vector_seq.sum())
        last.wait()

        heads = heads_got[...].reshape(columns, PAIR)

        def weight_rows(owner, carry):
            at = pl.ds(pl.multiple_of(owner * 128, 128), 128)
            grads[owner] = dot(rows_ref[at, :], heads, ((1,), (1,))).astype(BF)
            bias[owner] = dot(jnp.ones((8, PAIR), BF), heads_got[owner], ((1,), (1,)))
            return carry

        lax.fori_loop(0, SEQ, weight_rows, 0)
        qkv_two.start()
        qkv_one.start()
        bias_seq.start()
        inner_one.forward_z()
        inner_two.start()
        output_sum[...] = output.sum().astype(BF).reshape(output_sum.shape)
        output_z.start()
        outer_sum[2:] = outer_two.sum().astype(BF).reshape(2, 64, D)
        outer_sum[:2] = outer_one.sum().astype(BF).reshape(2, 64, D)
        outer_z.start()
        turned = dot(weight_ref[...].reshape(D, columns), heads).T
        partial[0] = turned[:ROWS]
        partial[1] = turned[ROWS:]
        token.start()
        qkv_two.forward()
        qkv_one.forward()
        inner_one.forward()
        output_mine[...] = output_z.sum().astype(BF)
        output_half.start()
        outer_mine[...] = outer_z.sum().astype(BF)
        outer_half.start()
        bias_all.start(bias_seq.sum())
        upper = qkv_one.sum().reshape(CHIPS, 8, columns)
        lower = qkv_two.sum().reshape(CHIPS, 8, columns)
        qkv_sum[...] = jnp.concatenate([upper, lower], axis=1).astype(BF)
        qkv_chip.start()
        inner_two.forward_z()
        output_all.start(output_half.sum())
        outer_all.start(outer_half.sum())
        inner_mine[:16] = inner_one.sum().astype(BF)
        token.wait()
        token_out[...] = partial[group_me("core")] + token_got[...]
        qkv_all.start(qkv_chip.sum())
        inner_two.forward()
        vector_all.forward()
        bias_all.forward()
        inner_mine[16:] = inner_two.sum().astype(BF)
        inner_half.start()
        output_all.forward()
        outer_all.forward()
        qkv_all.forward()
        inner_all.start(inner_half.sum())
        inner_all.forward()
        for one in (vector_all, bias_all, output_all, outer_all, qkv_all, inner_all):
            one.wait()

    return pl.pallas_call(
        kernel,
        out_shape=[
            jax.ShapeDtypeStruct((ROWS, D), F32),
            jax.ShapeDtypeStruct((2, CHIPS) + chip_piece, BF),
            jax.ShapeDtypeStruct((2, 4, 16, D), BF),
            jax.ShapeDtypeStruct((2, 4, 32, FF // 2), BF),
            jax.ShapeDtypeStruct((2, 4, 64, D), BF),
            jax.ShapeDtypeStruct((2, CHIPS) + vector, F32),
            jax.ShapeDtypeStruct((2, CHIPS, 8, 3 * HD), F32),
        ],
        in_specs=[VMEM] * 7 + [ANY] * 3,
        out_specs=[VMEM] * 7,
        scratch_shapes=[
            pltpu.VMEM(grad.shape, BF),
            pltpu.VMEM(qkv_got.shape, BF),
            pltpu.VMEM((HD, LENGTH), BF),
            pltpu.VMEM((LENGTH, HD), BF),
            pltpu.VMEM((HD, LENGTH), BF),
            pltpu.VMEM((LENGTH, HD), BF),
            pltpu.VMEM((LENGTH, HD), BF),
            pltpu.VMEM((HD, LENGTH), BF),
            pltpu.VMEM((LENGTH, HD), BF),
            pltpu.VMEM((1, LENGTH), F32),
            pltpu.VMEM((HD, LENGTH), F32),
            pltpu.VMEM((LENGTH, HD), F32),
            pltpu.VMEM((LENGTH, HD), F32),
            pltpu.VMEM((CHIPS, 3 * HD, PAIR), BF),
            pltpu.VMEM((SEQ, 128, columns), BF),
            pltpu.VMEM((SEQ, 8, 3 * HD), F32),
            pltpu.VMEM((2, ROWS, D), F32),
            pltpu.VMEM((ROWS, D), F32),
            dma(),
            dma(),
            pltpu.VMEM((4, 16, D), BF),
            pltpu.VMEM((4, 64, D), BF),
            pltpu.VMEM((16, D), BF),
            pltpu.VMEM((32, FF // 2), BF),
            pltpu.VMEM((64, D), BF),
            pltpu.VMEM((CHIPS,) + chip_piece, BF),
        ]
        + Exchange.scratch("a2a", "chip", grad)
        + Exchange.scratch("a2a", "chip", qkv_got)
        + SplitReduce.scratch(inner_half_shape)
        + SplitReduce.scratch(inner_half_shape)
        + RelayReduce.scratch(output_grad, (0, HD), "xy")
        + RelayReduce.scratch(outer_grad, (0, 128), "xy")
        + RelayReduce.scratch(outer_grad, (128, 128), "yx")
        + RelayReduce.scratch(grads_shape, (0, half), "xy")
        + RelayReduce.scratch(grads_shape, (half, half), "yx")
        + Scatter.scratch("seq", vector, F32)
        + Scatter.scratch("seq", (8, 3 * HD), F32)
        + Scatter.scratch("z", (16, D), BF)
        + Scatter.scratch("z", (64, D), BF)
        + Swap.scratch((16, D), BF)
        + Swap.scratch((64, D), BF)
        + Swap.scratch((32, FF // 2), BF)
        + Scatter.scratch("chip", chip_piece, BF)
        + Spread.scratch("z")
        + Spread.scratch("z")
        + Spread.scratch("z")
        + Spread.scratch("chip")
        + Spread.scratch("chip")
        + Spread.scratch("chip"),
        compiler_params=params(identifier, 56),
        name="backward",
    )(qkv_got, summed, stat, grad, rows_t, qkv_weight, vectors, output_grad, inner_grad, outer_grad)


def unpack(qkv, output, inner, outer):
    def kernel(qkv_ref, output_ref, inner_ref, outer_ref, query, key, value, output_out, inner_out, outer_out):
        def place(pair, rows):
            for kind, out in enumerate((query, key, value)):
                for head in range(SEQ):
                    at = head * 3 * HD + kind * HD
                    out[rows, head * 128 : (head + 1) * 128] = jnp.concatenate(
                        [part[:, at : at + HD] for part in pair], axis=1
                    )

        for chip in range(CHIPS):
            pair = [qkv_ref[core, chip].astype(F32) for core in range(2)]
            place([part[:8] for part in pair], slice(chip * 8, (chip + 1) * 8))
            place([part[8:] for part in pair], slice(64 + chip * 8, 64 + (chip + 1) * 8))
        for core in range(2):
            for quarter in range(4):
                start = core * HD + quarter * 16
                output_out[start : start + 16] = output_ref[core, quarter].astype(F32)
                start = core * 256 + quarter * 64
                outer_out[start : start + 64] = outer_ref[core, quarter].astype(F32)
                for half in range(2):
                    rows = slice(half * 64 + quarter * 16, half * 64 + (quarter + 1) * 16)
                    for owner in range(SEQ):
                        start = owner * 512 + core * 256
                        inner_out[rows, start : start + 256] = inner_ref[
                            core, quarter, half * 16 : (half + 1) * 16, owner * 256 : (owner + 1) * 256
                        ].astype(F32)

    shapes = [(128, D)] * 4 + [(128, FF), (512, D)]
    return pl.pallas_call(
        kernel,
        out_shape=[jax.ShapeDtypeStruct(shape, F32) for shape in shapes],
        in_specs=[VMEM] * 4,
        out_specs=[VMEM] * 6,
        compiler_params=pltpu.CompilerParams(vmem_limit_bytes=32 * 1024 * 1024),
        name="unpack",
    )(qkv, output, inner, outer)


def normalize(hidden, gain, shift):
    centered = hidden - jnp.mean(hidden, axis=-1, keepdims=True)
    inverse = lax.rsqrt(jnp.mean(centered * centered, axis=-1, keepdims=True) + 1e-05)
    normed = centered * inverse
    return (normed * gain + shift, normed, inverse)


def normalize_back(upstream, normed, inverse, gain):
    scaled = upstream * gain
    inner = (
        scaled
        - jnp.mean(scaled, axis=-1, keepdims=True)
        - normed * jnp.mean(scaled * normed, axis=-1, keepdims=True)
    )
    return (inverse * inner, jnp.sum(upstream * normed, axis=0), jnp.sum(upstream, axis=0))


def gelu_exact(value):
    return jax.nn.gelu(value, approximate=False)


def per_device(
    tokens,
    cotangent,
    w_query,
    b_query,
    w_key,
    w_value,
    b_value,
    w_output,
    b_output,
    first_gain,
    first_shift,
    w_inner,
    b_inner,
    w_outer,
    b_outer,
    second_gain,
    second_shift,
):
    core = lax.rem(lax.axis_index("ctx"), 2)
    rows = tokens[0]

    def pick(value, axis):
        return lax.dynamic_index_in_dim(value, core, axis, keepdims=False)

    qkv_part = pick(
        jnp.stack([w_query, w_key, w_value]).reshape(3, 128, SEQ, 2, HD), 3
    )
    qkv_part = jnp.transpose(qkv_part, (1, 2, 0, 3)).reshape(128, SEQ * 3 * HD)
    bias_part = jnp.concatenate(
        [
            pick(b_query.reshape(2, HD), 0),
            jnp.zeros((HD,), BF),
            pick(b_value.reshape(2, HD), 0),
            jnp.zeros((HD,), BF),
        ]
    )
    bias_part = jnp.broadcast_to(bias_part.astype(F32), (8, 4 * HD))
    small_part = jnp.concatenate(
        [
            jnp.stack(
                [b_query, b_value, b_output, first_gain, first_shift, b_outer, second_gain, second_shift]
            ),
            b_inner.reshape(4, 128),
            jnp.zeros((4, 128), BF),
        ]
    )
    (
        rows_pair,
        qkv_weight,
        small,
        output_weight,
        inner_weight,
        outer_weight,
        qkv_got,
        summed,
        attended,
        stat,
    ) = forward(0, rows, qkv_part, bias_part, small_part, w_output, w_inner, w_outer)
    rows_pair = rows_pair.reshape(PAIR, D)
    small = small.astype(F32)
    output_bias, norm_gain, norm_shift, outer_bias, final_gain, final_shift = (
        small[:, at].reshape(D) for at in range(2, 8)
    )
    inner_bias = pick(small[:, 8:12].reshape(SEQ, 2, 256), 1).reshape(FF // 2)

    attended = attended.reshape(D // 2, PAIR)
    output_weight = output_weight.reshape(D // 2, D)
    inner_weight = inner_weight.reshape(D, FF // 2)
    outer_weight = outer_weight.reshape(FF // 2, D)

    def core_sum(identifier, partial):
        (got,) = exchange(identifier, ("a2a", "core", partial.reshape(2, ROWS, D)))
        return got[0] + got[1]

    def core_pair(identifier, value):
        (got,) = exchange(identifier, ("ag", "core", value))
        return got.reshape(PAIR, D)

    branch = core_sum(2, dot(attended, output_weight, ((0,), (0,)))) + output_bias
    middle, unit_one, inverse_one = normalize(rows.astype(F32) + branch, norm_gain, norm_shift)
    middle_pair = core_pair(3, middle.astype(BF))
    inner = dot(middle_pair, inner_weight) + inner_bias
    active, gelu_pull = jax.vjp(gelu_exact, inner)
    active_low = active.astype(BF)
    outer = core_sum(4, dot(active_low, outer_weight)) + outer_bias
    result, unit_two, inverse_two = normalize(middle + outer, final_gain, final_shift)
    upstream = cotangent[0].astype(F32)
    grad_mid, grad_final_gain, grad_final_shift = normalize_back(
        upstream, unit_two, inverse_two, final_gain
    )
    grad_outer_low = grad_mid.astype(BF)
    grad_outer_bias = jnp.sum(grad_outer_low.astype(F32), axis=0)
    grad_outer_pair = core_pair(5, grad_outer_low)
    grad_outer_weight = dot(active_low, grad_outer_pair, ((0,), (0,))).astype(BF)
    grad_active = dot(grad_outer_pair, outer_weight, ((1,), (1,)))
    grad_inner_low = gelu_pull(grad_active)[0].astype(BF)
    grad_inner_weight = dot(middle_pair, grad_inner_low, ((0,), (0,))).astype(BF)
    grad_inner_bias = jnp.sum(grad_inner_low.astype(F32), axis=0)
    grad_middle = core_sum(6, dot(grad_inner_low, inner_weight, ((1,), (1,)))) + grad_mid
    grad_residual, grad_norm_gain, grad_norm_shift = normalize_back(
        grad_middle, unit_one, inverse_one, norm_gain
    )
    grad_branch_low = grad_residual.astype(BF)
    grad_output_bias = jnp.sum(grad_branch_low.astype(F32), axis=0)
    grad_branch_pair = core_pair(7, grad_branch_low)
    grad_output_weight = dot(attended, grad_branch_pair).astype(BF)
    grad_attended = dot(output_weight, grad_branch_pair, ((1,), (1,))).astype(BF)

    vectors = jnp.concatenate(
        [
            jnp.stack(
                [
                    grad_output_bias,
                    grad_norm_gain,
                    grad_norm_shift,
                    grad_outer_bias,
                    grad_final_gain,
                    grad_final_shift,
                ]
            )
            .reshape(6, SEQ, 128)
            .transpose(1, 0, 2),
            grad_inner_bias.reshape(SEQ, 2, 128),
        ],
        axis=1,
    )
    token_part, qkv_share, output_share, inner_share, outer_share, vectors, biases = backward(
        8,
        qkv_got,
        summed,
        stat,
        grad_attended.reshape(CHIPS, HD, PAIR),
        rows_pair.T,
        qkv_weight,
        vectors,
        grad_output_weight.reshape(SEQ, HD, D),
        grad_inner_weight.reshape(SEQ, 128, FF // 2),
        grad_outer_weight.reshape(SEQ, 256, D),
    )
    grad_tokens = grad_residual + token_part
    grad_query, grad_key, grad_value, grad_output, grad_inner, grad_outer = unpack(
        qkv_share, output_share, inner_share, outer_share
    )
    vectors, biases = jnp.sum(vectors, axis=1), jnp.sum(biases[:, :, 0], axis=1)
    whole = vectors[0, :6] + vectors[1, :6]
    grad_query_bias = biases[:, :HD].reshape(128)
    grad_value_bias = biases[:, 2 * HD :].reshape(128)
    grad_inner_bias = vectors[:, 6:].reshape(512)
    return (
        result.astype(BF)[None],
        grad_tokens[None],
        grad_query,
        grad_query_bias,
        grad_key,
        grad_value,
        grad_value_bias,
        grad_output,
        whole[0],
        whole[1],
        whole[2],
        grad_inner,
        grad_inner_bias,
        grad_outer,
        whole[3],
        whole[4],
        whole[5],
    )


def solution(mesh):
    row = P("seq", None)
    vector = P("seq")
    placed = P("seq", "ctx", None)
    return jax.shard_map(
        per_device,
        mesh=mesh,
        in_specs=(
            placed,
            placed,
            row,
            vector,
            row,
            row,
            vector,
            row,
            vector,
            vector,
            vector,
            row,
            vector,
            row,
            vector,
            vector,
            vector,
        ),
        out_specs=(
            placed,
            placed,
            row,
            vector,
            row,
            row,
            vector,
            row,
            vector,
            vector,
            vector,
            row,
            vector,
            row,
            vector,
            vector,
            vector,
        ),
        check_vma=False,
    )
```

```python
import functools
import math

import jax
import jax.numpy as jnp
from jax import lax
from jax.experimental import pallas as pl
from jax.experimental.pallas import tpu as pltpu
from jax.sharding import PartitionSpec as P

D = 1024
HEADS = 16
HD = 64
FF = 4096
SEQ = 8
CHIPS = 8
ROWS = 192
PAIR = 2 * ROWS
LENGTH = CHIPS * PAIR
SCALE2 = HD ** (-0.5) * math.log2(math.e)
BLOCK = 512
BF = jnp.bfloat16
F32 = jnp.float32
ANY = pl.BlockSpec(memory_space=pl.ANY)
VMEM = pl.BlockSpec(memory_space=pltpu.VMEM)


def dot(left, right, dims=((1,), (0,))):
    return lax.dot_general(left, right, (dims, ((), ())), preferred_element_type=F32)


SIZES = {"seq": 8, "chip": 8, "x": 4, "y": 2, "z": 4, "half": 2, "core": 2}


def group_size(group):
    return SIZES[group]


def group_me(group):
    seq, ctx = lax.axis_index("seq"), lax.axis_index("ctx")
    if group == "seq":
        return seq
    if group == "x":
        return lax.rem(seq, 4)
    if group == "y":
        return lax.div(seq, 4)
    if group == "core":
        return lax.rem(ctx, 2)
    if group == "half":
        return lax.div(ctx, 8)
    if group == "z":
        return lax.rem(lax.div(ctx, 2), 4)
    return lax.div(ctx, 2)


def group_device(group, index):
    seq, ctx = lax.axis_index("seq"), lax.axis_index("ctx")
    if group == "seq":
        return (index, ctx)
    if group == "x":
        return (lax.div(seq, 4) * 4 + index, ctx)
    if group == "y":
        return (index * 4 + lax.rem(seq, 4), ctx)
    if group == "core":
        return (seq, lax.div(ctx, 2) * 2 + index)
    if group == "half":
        return (seq, index * 8 + lax.rem(ctx, 8))
    if group == "z":
        return (seq, lax.div(ctx, 8) * 8 + index * 2 + lax.rem(ctx, 2))
    return (seq, index * 2 + lax.rem(ctx, 2))


def group_peer(group, step):
    return lax.rem(group_me(group) + step, group_size(group))


def enter(groups):
    barrier = pltpu.get_barrier_semaphore()
    count = 0
    for group in groups:
        for step in range(1, group_size(group)):
            pl.semaphore_signal(
                barrier,
                inc=1,
                device_id=group_device(group, group_peer(group, step)),
                device_id_type=pl.DeviceIdType.MESH,
            )
            count += 1
    pl.semaphore_wait(barrier, count)


def remote(source, target, send, recv, group, peer):
    return pltpu.make_async_remote_copy(
        src_ref=source,
        dst_ref=target,
        send_sem=send,
        recv_sem=recv,
        device_id=group_device(group, peer),
        device_id_type=pl.DeviceIdType.MESH,
    )


def dma(*shape):
    return pltpu.SemaphoreType.DMA(shape)


class Exchange:
    def __init__(self, kind, group, source, target, refs, rows=None):
        self.kind, self.group = kind, group
        self.source, self.target, self.rows = source, target, rows
        self.send, self.recv = refs[:2]
        if rows is None:
            self.own, self.own_held = refs[2:]

    @staticmethod
    def scratch(kind, group, value, rows=None):
        count = group_size(group) - 1
        if rows is not None:
            return [dma(count), dma(count)]
        piece = value.shape if kind == "ag" else value.shape[1:]
        return [dma(count), dma(count), dma(2), pltpu.VMEM(piece, value.dtype)]

    def copies(self):
        me = group_me(self.group)
        made = []
        for step in range(1, group_size(self.group)):
            peer = group_peer(self.group, step)
            piece = self.source if self.kind == "ag" else self.source.at[peer]
            target = self.target.at[me]
            if self.rows is not None:
                piece, target = piece.at[pl.ds(*self.rows)], target.at[pl.ds(*self.rows)]
            made.append(
                remote(piece, target, self.send.at[step - 1], self.recv.at[step - 1], self.group, peer)
            )
        return made

    def own_copies(self):
        me = group_me(self.group)
        piece = self.source if self.kind == "ag" else self.source.at[me]
        return (
            pltpu.make_async_copy(piece, self.own_held, self.own.at[0]),
            pltpu.make_async_copy(self.own_held, self.target.at[me], self.own.at[1]),
        )

    def start(self):
        for copy in self.copies():
            copy.start()
        if self.rows is None:
            self.own_copies()[0].start()

    def wait(self):
        if self.rows is None:
            own_in, own_out = self.own_copies()
            own_in.wait()
            own_out.start()
            own_out.wait()
        for copy in self.copies():
            copy.wait()


class Own:
    def __init__(self, source, target, refs):
        self.source, self.target = source, target.at[group_me("seq")]
        self.sems, self.held = refs

    @staticmethod
    def scratch(value):
        return [dma(2), pltpu.VMEM(value.shape, value.dtype)]

    def start(self):
        pltpu.make_async_copy(self.source, self.held, self.sems.at[0]).start()

    def wait(self):
        pltpu.make_async_copy(self.source, self.held, self.sems.at[0]).wait()
        copy = pltpu.make_async_copy(self.held, self.target, self.sems.at[1])
        copy.start()
        copy.wait()


class RelayGather:
    def __init__(self, source, target, span, order, refs):
        self.source, self.target, self.span, self.order = source, target, span, order
        self.send, self.recv = refs
        x, y = group_me("x"), group_me("y")
        back = [lax.rem(x + 4 - step, 4) for step in range(1, 4)]
        if order == "yx":
            self.owners = [(1 - y) * 4 + x] + [y * 4 + at for at in back] + [(1 - y) * 4 + at for at in back]
        else:
            self.owners = [y * 4 + at for at in back] + [(1 - y) * 4 + x] + [(1 - y) * 4 + at for at in back]

    @staticmethod
    def scratch():
        return [dma(7), dma(7)]

    def slot(self, at):
        x, y = group_me("x"), group_me("y")
        piece = self.source.at[self.span]
        place = self.target.at[y * 4 + x, self.span]
        if self.order == "yx":
            group, step = ("y", 1) if at == 0 else ("x", (at - 1) % 3 + 1)
            if at >= 4:
                piece = place = self.target.at[self.owners[0], self.span]
        else:
            group, step = ("x", at + 1) if at < 3 else ("y", 1)
            if at >= 4:
                piece = place = self.target.at[self.owners[at - 4], self.span]
        return remote(piece, place, self.send.at[at], self.recv.at[at], group, group_peer(group, step))

    def start(self):
        for at in range(4):
            self.slot(at).start()

    def forward(self):
        if self.order == "yx":
            self.slot(0).wait_recv()
            for at in range(4, 7):
                self.slot(at).start()
        else:
            for at in range(3):
                self.slot(at).wait_recv()
                self.slot(at + 4).start()

    def waited(self):
        return (0,) if self.order == "yx" else (0, 1, 2)

    def wait_recv(self):
        for at in range(7):
            if at not in self.waited():
                self.slot(at).wait_recv()

    def wait_send(self):
        for at in range(7):
            self.slot(at).wait_send()

    def wait(self):
        self.wait_recv()
        self.wait_send()


class SplitGather:
    def __init__(self, source, target, refs):
        rows = source.shape[0] // 4
        self.span = pl.ds(pl.multiple_of(group_me("z") * rows, 16), rows)
        self.target = target
        self.relay = RelayGather(source, target, self.span, "yx", refs[:2])
        self.send, self.recv = refs[2:]

    @staticmethod
    def scratch():
        return RelayGather.scratch() + [dma(21), dma(21)]

    def second(self, slot, hop):
        at = slot * 3 + hop - 1
        piece = self.target.at[self.relay.owners[slot], self.span]
        return remote(piece, piece, self.send.at[at], self.recv.at[at], "z", group_peer("z", hop))

    def start(self):
        self.relay.start()

    def forward_x(self):
        self.relay.forward()
        for hop in range(1, 4):
            self.second(0, hop).start()

    def forward_z(self):
        for slot in range(1, 7):
            self.relay.slot(slot).wait_recv()
            for hop in range(1, 4):
                self.second(slot, hop).start()

    def wait(self):
        self.relay.wait_send()
        for slot in range(7):
            for hop in range(1, 4):
                self.second(slot, hop).wait()


class RelayReduce:
    def __init__(self, source, rows, order, refs):
        self.source, self.span, self.order = source, pl.ds(*rows), order
        self.group, self.group_two = order
        self.size, self.size_two = group_size(order[0]), group_size(order[1])
        self.send, self.recv, self.local, self.got, self.total, self.send_two, self.recv_two, self.got_two = refs

    @staticmethod
    def scratch(value, rows, order):
        piece, kind = (rows[1], value.shape[2]), value.dtype
        one, two = group_size(order[0]), group_size(order[1])
        pieces = (one - 1) * two
        return [
            dma(pieces),
            dma(pieces),
            dma(two),
            pltpu.VMEM((pieces,) + piece, kind),
            pltpu.VMEM((two,) + piece, kind),
            dma(two - 1),
            dma(two - 1),
            pltpu.VMEM((two - 1,) + piece, kind),
        ]

    def piece(self, one, two):
        return self.source.at[one * 4 + two if self.order == "yx" else two * 4 + one, self.span]

    def first(self):
        made = []
        for step in range(1, self.size):
            peer = group_peer(self.group, step)
            for two in range(self.size_two):
                at = (step - 1) * self.size_two + two
                made.append(
                    remote(
                        self.piece(peer, two), self.got.at[at], self.send.at[at], self.recv.at[at], self.group, peer
                    )
                )
        return made

    def own(self):
        return [
            pltpu.make_async_copy(
                self.piece(group_me(self.group), two), self.total.at[two], self.local.at[two]
            )
            for two in range(self.size_two)
        ]

    def second(self):
        made = []
        for step in range(1, self.size_two):
            peer = group_peer(self.group_two, step)
            made.append(
                remote(
                    self.total.at[peer],
                    self.got_two.at[step - 1],
                    self.send_two.at[step - 1],
                    self.recv_two.at[step - 1],
                    self.group_two,
                    peer,
                )
            )
        return made

    def start(self):
        for copy in self.first() + self.own():
            copy.start()

    def forward(self):
        for copy in self.own() + self.first():
            copy.wait()
        for two in range(self.size_two):
            value = self.total[two].astype(F32)
            for step in range(self.size - 1):
                value += self.got[step * self.size_two + two].astype(F32)
            self.total[two] = value.astype(self.total.dtype)
        for copy in self.second():
            copy.start()

    def sum(self):
        for copy in self.second():
            copy.wait()
        value = self.total[group_me(self.group_two)].astype(F32)
        for step in range(self.size_two - 1):
            value += self.got_two[step].astype(F32)
        return value


class SplitReduce:
    def __init__(self, source, refs):
        self.source, self.quarter = source, source.shape[1] // 4
        self.send, self.recv, self.local, self.got, self.total = refs[:5]
        self.relay = RelayReduce(self.total, (0, self.quarter), "xy", refs[5:])

    @staticmethod
    def scratch(value):
        quarter, columns = value.shape[1] // 4, value.shape[2]
        return [dma(3), dma(3), dma()] + [
            pltpu.VMEM((3, 8, quarter, columns), BF),
            pltpu.VMEM((8, quarter, columns), BF),
        ] + RelayReduce.scratch(value, (0, quarter), "xy")

    def part(self, index):
        return self.source.at[:, pl.ds(pl.multiple_of(index * self.quarter, 16), self.quarter)]

    def first(self, hop):
        peer = group_peer("z", hop)
        return remote(
            self.part(peer), self.got.at[hop - 1], self.send.at[hop - 1], self.recv.at[hop - 1], "z", peer
        )

    def own_copy(self):
        return pltpu.make_async_copy(self.part(group_me("z")), self.total, self.local)

    def start(self):
        for hop in range(1, 4):
            self.first(hop).start()
        self.own_copy().start()

    def forward_z(self):
        self.own_copy().wait()
        for hop in range(1, 4):
            self.first(hop).wait()

        def add(at, carry):
            value = self.total[at].astype(F32)
            for hop in range(3):
                value += self.got[hop, at].astype(F32)
            self.total[at] = value.astype(BF)
            return carry

        lax.fori_loop(0, 8, add, 0)
        self.relay.start()

    def forward(self):
        self.relay.forward()

    def sum(self):
        return self.relay.sum()


class Refs:
    def __init__(self, refs):
        self.refs, self.at = refs, 0

    def take(self, count):
        self.at += count
        return self.refs[self.at - count : self.at]

    def left(self):
        return self.refs[self.at :]


def target_shape(kind, group, value):
    shape = value.shape if kind == "a2a" else (group_size(group),) + value.shape
    return jax.ShapeDtypeStruct(shape, value.dtype)


def params(identifier, mebibytes):
    return pltpu.CompilerParams(
        collective_id=identifier,
        has_side_effects=True,
        vmem_limit_bytes=mebibytes * 1024 * 1024,
    )


def forward(identifier, rows, w_query, w_key, w_value, small_part, w_output, w_inner, w_outer):
    columns = SEQ * 3 * HD
    qkv_part = jax.ShapeDtypeStruct((128, columns), BF)
    heads_shape = jax.ShapeDtypeStruct((CHIPS, 3 * HD, PAIR), BF)
    low_shape = jax.ShapeDtypeStruct((CHIPS, HD, PAIR), BF)
    output_part = jax.ShapeDtypeStruct((HD, D), BF)
    inner_part = jax.ShapeDtypeStruct((128, FF // 2), BF)
    outer_part = jax.ShapeDtypeStruct((256, D), BF)

    def kernel(*refs):
        refs = Refs(refs)
        rows_ref, query_ref, key_ref, value_ref, small_ref, output_ref, inner_ref, outer_ref = refs.take(8)
        turned_out, qkv_out, small_out, bias_out, output_out, inner_out, outer_out = refs.take(7)
        qkv_got, summed_ref, back_ref, stat_ref = refs.take(4)
        qkv_ref, inner_held, rows_out, small_got, heads, query_t, keys, value_t, low = refs.take(9)
        core = group_me("core")

        def mine(value, axis):
            half = value.shape[axis] // 2
            low_half = lax.slice_in_dim(value, 0, half, axis=axis)
            return jnp.where(core == 0, low_half, lax.slice_in_dim(value, half, 2 * half, axis=axis))

        output_ref = output_ref.at[pl.ds(pl.multiple_of(core * HD, HD), HD)]
        outer_ref = outer_ref.at[pl.ds(pl.multiple_of(core * 256, 256), 256)]
        split = SplitGather(qkv_ref.at[pl.ds(0, 64)], qkv_out, refs.take(4))
        one_way = RelayGather(qkv_ref, qkv_out, pl.ds(64, 32), "yx", refs.take(2))
        other_way = RelayGather(qkv_ref, qkv_out, pl.ds(96, 32), "xy", refs.take(2))
        qkv_own = Own(qkv_ref, qkv_out, refs.take(2))
        small = Exchange("ag", "seq", small_ref, small_got, refs.take(4))
        pair = Exchange("ag", "core", rows_ref, rows_out, refs.take(4))
        first = Exchange("a2a", "chip", heads, qkv_got, refs.take(4))
        last = Exchange("a2a", "chip", low, back_ref, refs.take(4))
        inner = SplitGather(inner_held, inner_out, refs.take(4))
        output = RelayGather(output_ref, output_out, pl.ds(0, HD), "yx", refs.take(2))
        outer_one = RelayGather(outer_ref, outer_out, pl.ds(0, 128), "yx", refs.take(2))
        outer_two = RelayGather(outer_ref, outer_out, pl.ds(128, 128), "xy", refs.take(2))
        owns = [
            Own(source, target, refs.take(2))
            for source, target in (
                (output_ref, output_out),
                (inner_held, inner_out),
                (outer_ref, outer_out),
            )
        ]
        for owner in range(0, SEQ, 2):
            parts = []
            for head in (owner, owner + 1):
                for ref in (query_ref, key_ref, value_ref):
                    parts.append(mine(ref[:, head * 128 : (head + 1) * 128].astype(F32), 1))
            qkv_ref[:, owner * 192 : (owner + 2) * 192] = jnp.concatenate(parts, axis=1).astype(BF)
        enter(["seq", "chip", "core"])
        for one in (split, one_way, other_way, qkv_own, small, pair):
            one.start()
        for owner in range(SEQ):
            here = pl.ds(pl.multiple_of(owner * 512 + core * 256, 256), 256)
            inner_held[:, owner * 256 : (owner + 1) * 256] = inner_ref[:, here]
        for own in owns:
            own.start()
        split.forward_x()
        one_way.forward()
        split.forward_z()
        inner.start()
        outer_two.start()
        other_way.forward()
        for one in (pair, small, qkv_own, one_way, other_way, split):
            one.wait()
        inner.forward_x()
        weight = qkv_out[...].reshape(D, columns)
        turned = dot(rows_out[...].reshape(PAIR, D), weight).T
        for chip in range(CHIPS):
            shift = mine(small_got[chip].astype(F32).T, 0)
            part = turned[chip * 3 * HD : (chip + 1) * 3 * HD]
            heads[chip, 0:HD, :] = (part[:HD] + shift[:, 0:1]).astype(BF)
            heads[chip, HD : 2 * HD, :] = part[HD : 2 * HD].astype(BF)
            heads[chip, 2 * HD :, :] = (part[2 * HD :] + shift[:, 1:2]).astype(BF)
        first.start()
        output.start()
        outer_one.start()
        inner.forward_z()
        output.forward()
        turned_out[...] = rows_out[...].reshape(PAIR, D).astype(F32).T.astype(BF)
        for owner in range(SEQ):
            at = slice(owner * 128, (owner + 1) * 128)
            values = small_got[owner].astype(F32)
            small_out[:, at] = values[2:10]
            for row in range(2):
                at = slice(owner * 256 + row * 128, owner * 256 + (row + 1) * 128)
                bias_out[:, at] = jnp.where(core == 0, values[8 + row : 9 + row], values[10 + row : 11 + row])
        first.wait()
        for chip in range(CHIPS):
            at = pl.ds(chip * PAIR, PAIR)
            query_t[:, at] = qkv_got[chip, 0:HD, :]
            keys[at, :] = qkv_got[chip, HD : 2 * HD, :].astype(F32).T.astype(BF)
            value_t[:, at] = qkv_got[chip, 2 * HD : 3 * HD, :]
        outer_one.forward()

        def one_block(block, carry):
            at = pl.ds(pl.multiple_of(block * BLOCK, BLOCK), BLOCK)
            query = query_t[:, at]
            top = jnp.full((1, BLOCK), -1e30, F32)
            total = jnp.zeros((1, BLOCK), F32)
            summed = jnp.zeros((HD, BLOCK), F32)
            for part in range(LENGTH // BLOCK):
                here = slice(part * BLOCK, (part + 1) * BLOCK)
                scores = dot(keys[here, :], query) * SCALE2
                new_top = jnp.maximum(top, jnp.max(scores, axis=0, keepdims=True))
                factor = jnp.exp2(top - new_top)
                weights = jnp.exp2(scores - new_top)
                total = total * factor + jnp.sum(weights, axis=0, keepdims=True)
                summed = summed * factor + dot(value_t[:, here], weights.astype(BF))
                top = new_top
            summed_ref[:, at] = summed / total
            stat_ref[:, at] = top + jnp.log2(total)
            return carry

        lax.fori_loop(0, 2, one_block, 0)
        outer_two.forward()
        lax.fori_loop(2, LENGTH // BLOCK, one_block, 0)
        for chip in range(CHIPS):
            low[chip] = summed_ref[:, chip * PAIR : (chip + 1) * PAIR].astype(BF)
        last.start()
        for one in [last, output, inner, outer_one, outer_two] + owns:
            one.wait()

    return pl.pallas_call(
        kernel,
        out_shape=[
            jax.ShapeDtypeStruct((D, PAIR), BF),
            target_shape("ag", "seq", qkv_part),
            jax.ShapeDtypeStruct((8, D), F32),
            jax.ShapeDtypeStruct((1, FF // 2), F32),
            target_shape("ag", "seq", output_part),
            target_shape("ag", "seq", inner_part),
            target_shape("ag", "seq", outer_part),
            heads_shape,
            jax.ShapeDtypeStruct((HD, LENGTH), F32),
            low_shape,
            jax.ShapeDtypeStruct((1, LENGTH), F32),
        ],
        in_specs=[ANY] + [VMEM] * 3 + [ANY] * 2 + [VMEM, ANY],
        out_specs=[VMEM] * 4 + [ANY] * 3 + [VMEM] * 4,
        scratch_shapes=[
            pltpu.VMEM(qkv_part.shape, BF),
            pltpu.VMEM(inner_part.shape, BF),
            pltpu.VMEM((2, ROWS, D), BF),
            pltpu.VMEM((SEQ, 16, 128), BF),
            pltpu.VMEM(heads_shape.shape, BF),
            pltpu.VMEM((HD, LENGTH), BF),
            pltpu.VMEM((LENGTH, HD), BF),
            pltpu.VMEM((HD, LENGTH), BF),
            pltpu.VMEM(low_shape.shape, BF),
        ]
        + SplitGather.scratch()
        + RelayGather.scratch()
        + RelayGather.scratch()
        + Own.scratch(qkv_part)
        + Exchange.scratch("ag", "seq", small_part)
        + Exchange.scratch("ag", "core", rows)
        + Exchange.scratch("a2a", "chip", heads_shape)
        + Exchange.scratch("a2a", "chip", low_shape)
        + SplitGather.scratch()
        + RelayGather.scratch()
        + RelayGather.scratch()
        + RelayGather.scratch()
        + Own.scratch(output_part)
        + Own.scratch(inner_part)
        + Own.scratch(outer_part),
        compiler_params=params(identifier, 48),
        name="forward",
    )(rows, w_query, w_key, w_value, small_part, w_output, w_inner, w_outer)


class Scatter:
    def __init__(self, group, source, refs):
        self.group, self.source = group, source
        send, recv, self.got = refs
        self.copies = [
            remote(
                source.at[group_peer(group, step)],
                self.got.at[step - 1],
                send.at[step - 1],
                recv.at[step - 1],
                group,
                group_peer(group, step),
            )
            for step in range(1, group_size(group))
        ]

    @staticmethod
    def scratch(group, piece, kind):
        count = group_size(group) - 1
        return [dma(count), dma(count), pltpu.VMEM((count,) + piece, kind)]

    def start(self):
        for copy in self.copies:
            copy.start()

    def sum(self):
        for copy in self.copies:
            copy.wait()
        own = self.source[group_me(self.group)].astype(F32)
        return sum((self.got[at].astype(F32) for at in range(group_size(self.group) - 1)), own)


class Swap:
    def __init__(self, group, source, refs):
        send, recv, self.got = refs
        self.source = source
        self.copy = remote(source, self.got, send, recv, group, group_peer(group, 1))

    @staticmethod
    def scratch(piece, kind):
        return [dma(), dma(), pltpu.VMEM(piece, kind)]

    def start(self):
        self.copy.start()

    def sum(self):
        self.copy.wait()
        return self.source[...].astype(F32) + self.got[...].astype(F32)


class Spread:
    def __init__(self, group, held, refs):
        send, recv, send_core, recv_core = refs
        self.group, self.held = group, held
        mine = held.at[group_me("core")]
        self.mine = mine
        piece = mine.at[group_me(group)]
        self.copies = [
            remote(piece, piece, send.at[step - 1], recv.at[step - 1], group, group_peer(group, step))
            for step in range(1, group_size(group))
        ]
        self.last = remote(mine, mine, send_core, recv_core, "core", group_peer("core", 1))

    @staticmethod
    def scratch(group):
        count = group_size(group) - 1
        return [dma(count), dma(count), dma(), dma()]

    def start(self, value):
        self.mine[group_me(self.group)] = value.astype(self.held.dtype)
        for copy in self.copies:
            copy.start()

    def forward(self):
        for copy in self.copies:
            copy.wait()
        self.last.start()

    def wait(self):
        self.last.wait()


def backward(
    identifier,
    qkv_got,
    summed,
    stat,
    grad,
    rows_t,
    qkv_weight,
    residual,
    row_sums,
    bias_sums,
    output_grad,
    inner_grad,
    outer_grad,
):
    columns = SEQ * 3 * HD
    half = 64
    chip_piece = (16, columns)
    vector = (8, 128)
    grads_shape = jax.ShapeDtypeStruct((SEQ, 128, columns), BF)
    inner_half_shape = jax.ShapeDtypeStruct((SEQ, 64, FF // 2), BF)

    def kernel(*refs):
        refs = Refs(refs)
        qkv_ref, summed_ref, stat_ref, grad_ref, rows_ref, weight_ref = refs.take(6)
        residual_ref, row_sums_ref, bias_sums_ref = refs.take(3)
        output_ref, inner_ref, outer_ref = refs.take(3)
        token_out, qkv_out, output_out, inner_out, outer_out, vector_out, bias_out = refs.take(7)
        grad_got, heads_got, query_t, queries, key_t, keys, values, up_t, ups, delta_ref = refs.take(10)
        grad_query, grad_key, grad_value, low = refs.take(4)
        vectors_ref, grads, bias, partial, token_got, token_send, token_recv = refs.take(7)
        output_sum, outer_sum, output_mine, inner_mine, outer_mine, qkv_sum = refs.take(6)
        first = Exchange("a2a", "chip", grad_ref, grad_got, refs.take(4))
        last = Exchange("a2a", "chip", low, heads_got, refs.take(4))
        inner_one = SplitReduce(inner_ref.at[:, pl.ds(0, 64)], refs.take(13))
        inner_two = SplitReduce(inner_ref.at[:, pl.ds(64, 64)], refs.take(13))
        output = RelayReduce(output_ref, (0, HD), "xy", refs.take(8))
        outer_one = RelayReduce(outer_ref, (0, 128), "xy", refs.take(8))
        outer_two = RelayReduce(outer_ref, (128, 128), "yx", refs.take(8))
        qkv_one = RelayReduce(grads, (0, half), "xy", refs.take(8))
        qkv_two = RelayReduce(grads, (half, half), "yx", refs.take(8))
        vector_seq = Scatter("seq", vectors_ref, refs.take(3))
        bias_seq = Scatter("seq", bias, refs.take(3))
        output_z = Scatter("z", output_sum, refs.take(3))
        outer_z = Scatter("z", outer_sum, refs.take(3))
        output_half = Swap("half", output_mine, refs.take(3))
        outer_half = Swap("half", outer_mine, refs.take(3))
        inner_half = Swap("half", inner_mine, refs.take(3))
        qkv_chip = Scatter("chip", qkv_sum, refs.take(3))
        output_all = Spread("z", output_out, refs.take(4))
        outer_all = Spread("z", outer_out, refs.take(4))
        inner_all = Spread("z", inner_out, refs.take(4))
        qkv_all = Spread("chip", qkv_out, refs.take(4))
        vector_all = Spread("chip", vector_out, refs.take(4))
        bias_all = Spread("chip", bias_out, refs.take(4))
        other = group_peer("core", 1)
        token = remote(partial.at[other], token_got, token_send, token_recv, "core", other)

        for owner in range(SEQ):
            vectors_ref[owner, 0:6, :] = row_sums_ref[0:6, owner * 128 : (owner + 1) * 128]
            for row in range(2):
                at = slice(owner * 256 + row * 128, owner * 256 + (row + 1) * 128)
                vectors_ref[owner, 6 + row : 7 + row, :] = bias_sums_ref[:, at]
        enter(["seq", "chip", "core"])
        for one in (first, inner_one, outer_two, output, outer_one, vector_seq):
            one.start()
        for chip in range(CHIPS):
            at = pl.ds(chip * PAIR, PAIR)
            query_t[:, at] = qkv_ref[chip, 0:HD, :]
            queries[at, :] = qkv_ref[chip, 0:HD, :].astype(F32).T.astype(BF)
            key_t[:, at] = qkv_ref[chip, HD : 2 * HD, :]
            keys[at, :] = qkv_ref[chip, HD : 2 * HD, :].astype(F32).T.astype(BF)
            values[at, :] = qkv_ref[chip, 2 * HD : 3 * HD, :].astype(F32).T.astype(BF)
        grad_key[...] = jnp.zeros_like(grad_key)
        grad_value[...] = jnp.zeros_like(grad_value)
        first.wait()
        for chip in range(CHIPS):
            at = pl.ds(chip * PAIR, PAIR)
            up = grad_got[chip].astype(F32)
            up_t[:, at] = grad_got[chip]
            ups[at, :] = up.T.astype(BF)
            delta_ref[:, at] = jnp.sum(up * summed_ref[:, at], axis=0, keepdims=True)

        def one_block(block, carry):
            at = pl.ds(pl.multiple_of(block * BLOCK, BLOCK), BLOCK)
            query, up = query_t[:, at], up_t[:, at]
            query_rows, up_rows = queries[at, :], ups[at, :]
            stat, delta = stat_ref[:, at], delta_ref[:, at]
            gathered = jnp.zeros((HD, BLOCK), F32)
            for part in range(LENGTH // BLOCK):
                here = slice(part * BLOCK, (part + 1) * BLOCK)
                scores = dot(keys[here, :], query) * SCALE2
                probs = jnp.exp2(scores - stat)
                grad_value[here, :] += dot(probs.astype(BF), up_rows)
                slope = dot(values[here, :], up) - delta
                grad_scores = (probs * slope).astype(BF)
                grad_key[here, :] += dot(grad_scores, query_rows)
                gathered += dot(key_t[:, here], grad_scores)
            grad_query[:, at] = gathered
            return carry

        lax.fori_loop(0, LENGTH // BLOCK, one_block, 0)
        scale = HD ** (-0.5)
        for chip in range(CHIPS):
            at = slice(chip * PAIR, (chip + 1) * PAIR)
            low[chip, 0:HD, :] = (grad_query[:, at] * scale).astype(BF)
            low[chip, HD : 2 * HD, :] = (grad_key[at, :] * scale).T.astype(BF)
            low[chip, 2 * HD : 3 * HD, :] = grad_value[at, :].T.astype(BF)
        last.start()
        output.forward()
        outer_two.forward()
        outer_one.forward()
        vector_all.start(vector_seq.sum())
        last.wait()

        heads = heads_got[...].reshape(columns, PAIR)

        def weight_rows(owner, carry):
            at = pl.ds(pl.multiple_of(owner * 128, 128), 128)
            grads[owner] = dot(rows_ref[at, :], heads, ((1,), (1,))).astype(BF)
            bias[owner] = dot(jnp.ones((8, PAIR), BF), heads_got[owner], ((1,), (1,)))
            return carry

        lax.fori_loop(0, SEQ, weight_rows, 0)
        qkv_two.start()
        qkv_one.start()
        bias_seq.start()
        inner_one.forward_z()
        inner_two.start()
        output_sum[...] = output.sum().astype(BF).reshape(output_sum.shape)
        output_z.start()
        outer_sum[2:] = outer_two.sum().astype(BF).reshape(2, 64, D)
        outer_sum[:2] = outer_one.sum().astype(BF).reshape(2, 64, D)
        outer_z.start()
        turned = dot(weight_ref[...].reshape(D, columns), heads).T
        partial[0] = turned[:ROWS]
        partial[1] = turned[ROWS:]
        token.start()
        qkv_two.forward()
        qkv_one.forward()
        inner_one.forward()
        output_mine[...] = output_z.sum().astype(BF)
        output_half.start()
        outer_mine[...] = outer_z.sum().astype(BF)
        outer_half.start()
        bias_all.start(bias_seq.sum())
        upper = qkv_one.sum().reshape(CHIPS, 8, columns)
        lower = qkv_two.sum().reshape(CHIPS, 8, columns)
        qkv_sum[...] = jnp.concatenate([upper, lower], axis=1).astype(BF)
        qkv_chip.start()
        inner_two.forward_z()
        output_all.start(output_half.sum())
        outer_all.start(outer_half.sum())
        inner_mine[:16] = inner_one.sum().astype(BF)
        token.wait()
        token_out[...] = residual_ref[...] + partial[group_me("core")] + token_got[...]
        qkv_all.start(qkv_chip.sum())
        inner_two.forward()
        vector_all.forward()
        bias_all.forward()
        inner_mine[16:] = inner_two.sum().astype(BF)
        inner_half.start()
        output_all.forward()
        outer_all.forward()
        qkv_all.forward()
        inner_all.start(inner_half.sum())
        inner_all.forward()
        for one in (vector_all, bias_all, output_all, outer_all, qkv_all, inner_all):
            one.wait()

    return pl.pallas_call(
        kernel,
        out_shape=[
            jax.ShapeDtypeStruct((ROWS, D), F32),
            jax.ShapeDtypeStruct((2, CHIPS) + chip_piece, BF),
            jax.ShapeDtypeStruct((2, 4, 16, D), BF),
            jax.ShapeDtypeStruct((2, 4, 32, FF // 2), BF),
            jax.ShapeDtypeStruct((2, 4, 64, D), BF),
            jax.ShapeDtypeStruct((2, CHIPS) + vector, F32),
            jax.ShapeDtypeStruct((2, CHIPS, 8, 3 * HD), F32),
        ],
        in_specs=[VMEM] * 9 + [ANY] * 3,
        out_specs=[VMEM] * 7,
        scratch_shapes=[
            pltpu.VMEM(grad.shape, BF),
            pltpu.VMEM(qkv_got.shape, BF),
            pltpu.VMEM((HD, LENGTH), BF),
            pltpu.VMEM((LENGTH, HD), BF),
            pltpu.VMEM((HD, LENGTH), BF),
            pltpu.VMEM((LENGTH, HD), BF),
            pltpu.VMEM((LENGTH, HD), BF),
            pltpu.VMEM((HD, LENGTH), BF),
            pltpu.VMEM((LENGTH, HD), BF),
            pltpu.VMEM((1, LENGTH), F32),
            pltpu.VMEM((HD, LENGTH), F32),
            pltpu.VMEM((LENGTH, HD), F32),
            pltpu.VMEM((LENGTH, HD), F32),
            pltpu.VMEM((CHIPS, 3 * HD, PAIR), BF),
            pltpu.VMEM((SEQ,) + vector, F32),
            pltpu.VMEM((SEQ, 128, columns), BF),
            pltpu.VMEM((SEQ, 8, 3 * HD), F32),
            pltpu.VMEM((2, ROWS, D), F32),
            pltpu.VMEM((ROWS, D), F32),
            dma(),
            dma(),
            pltpu.VMEM((4, 16, D), BF),
            pltpu.VMEM((4, 64, D), BF),
            pltpu.VMEM((16, D), BF),
            pltpu.VMEM((32, FF // 2), BF),
            pltpu.VMEM((64, D), BF),
            pltpu.VMEM((CHIPS,) + chip_piece, BF),
        ]
        + Exchange.scratch("a2a", "chip", grad)
        + Exchange.scratch("a2a", "chip", qkv_got)
        + SplitReduce.scratch(inner_half_shape)
        + SplitReduce.scratch(inner_half_shape)
        + RelayReduce.scratch(output_grad, (0, HD), "xy")
        + RelayReduce.scratch(outer_grad, (0, 128), "xy")
        + RelayReduce.scratch(outer_grad, (128, 128), "yx")
        + RelayReduce.scratch(grads_shape, (0, half), "xy")
        + RelayReduce.scratch(grads_shape, (half, half), "yx")
        + Scatter.scratch("seq", vector, F32)
        + Scatter.scratch("seq", (8, 3 * HD), F32)
        + Scatter.scratch("z", (16, D), BF)
        + Scatter.scratch("z", (64, D), BF)
        + Swap.scratch((16, D), BF)
        + Swap.scratch((64, D), BF)
        + Swap.scratch((32, FF // 2), BF)
        + Scatter.scratch("chip", chip_piece, BF)
        + Spread.scratch("z")
        + Spread.scratch("z")
        + Spread.scratch("z")
        + Spread.scratch("chip")
        + Spread.scratch("chip")
        + Spread.scratch("chip"),
        compiler_params=params(identifier, 56),
        name="backward",
    )(
        qkv_got,
        summed,
        stat,
        grad,
        rows_t,
        qkv_weight,
        residual,
        row_sums,
        bias_sums,
        output_grad,
        inner_grad,
        outer_grad,
    )


def unpack(qkv, output, inner, outer, vectors, biases):
    def kernel(*refs):
        refs = Refs(refs)
        qkv_ref, output_ref, inner_ref, outer_ref, vectors_ref, biases_ref = refs.take(6)
        query, key, value, output_out, inner_out, outer_out = refs.take(6)
        query_bias, value_bias, inner_bias = refs.take(3)
        vector = [jnp.sum(vectors_ref[core], axis=0) for core in range(2)]
        bias = [jnp.sum(biases_ref[core], axis=0)[0:1] for core in range(2)]
        for row, out in enumerate(refs.left()):
            out[...] = vector[0][row : row + 1] + vector[1][row : row + 1]
        query_bias[...] = jnp.concatenate([part[:, :HD] for part in bias], axis=1)
        value_bias[...] = jnp.concatenate([part[:, 2 * HD :] for part in bias], axis=1)
        for core in range(2):
            for row in range(2):
                start = core * 256 + row * 128
                inner_bias[:, start : start + 128] = vector[core][6 + row : 7 + row]

        def place(pair, rows):
            for kind, out in enumerate((query, key, value)):
                for head in range(SEQ):
                    at = head * 3 * HD + kind * HD
                    out[rows, head * 128 : (head + 1) * 128] = jnp.concatenate(
                        [part[:, at : at + HD] for part in pair], axis=1
                    )

        for chip in range(CHIPS):
            pair = [qkv_ref[core, chip].astype(F32) for core in range(2)]
            place([part[:8] for part in pair], slice(chip * 8, (chip + 1) * 8))
            place([part[8:] for part in pair], slice(64 + chip * 8, 64 + (chip + 1) * 8))
        for core in range(2):
            for quarter in range(4):
                start = core * HD + quarter * 16
                output_out[start : start + 16] = output_ref[core, quarter].astype(F32)
                start = core * 256 + quarter * 64
                outer_out[start : start + 64] = outer_ref[core, quarter].astype(F32)
                for half in range(2):
                    rows = slice(half * 64 + quarter * 16, half * 64 + (quarter + 1) * 16)
                    for owner in range(SEQ):
                        start = owner * 512 + core * 256
                        inner_out[rows, start : start + 256] = inner_ref[
                            core, quarter, half * 16 : (half + 1) * 16, owner * 256 : (owner + 1) * 256
                        ].astype(F32)

    shapes = [(128, D)] * 4 + [(128, FF), (512, D), (1, 128), (1, 128), (1, 512)] + [(1, 128)] * 6
    return pl.pallas_call(
        kernel,
        out_shape=[jax.ShapeDtypeStruct(shape, F32) for shape in shapes],
        in_specs=[VMEM] * 6,
        out_specs=[VMEM] * 15,
        compiler_params=pltpu.CompilerParams(vmem_limit_bytes=32 * 1024 * 1024),
        name="unpack",
    )(qkv, output, inner, outer, vectors, biases)


def normalize(hidden):
    centered = hidden - jnp.mean(hidden, axis=-1, keepdims=True)
    inverse = lax.rsqrt(jnp.mean(centered * centered, axis=-1, keepdims=True) + 1e-05)
    return centered * inverse, inverse


def normalize_back(upstream, normed, inverse, gain):
    scaled = upstream * gain
    return inverse * (
        scaled
        - jnp.mean(scaled, axis=-1, keepdims=True)
        - normed * jnp.mean(scaled * normed, axis=-1, keepdims=True)
    )


def sum_rows(value):
    return jnp.sum(value, axis=0, keepdims=True)


def feed_forward(identifier, rows, cotangent, attended, output_weight, inner_weight, outer_weight, small, inner_bias):
    units, tile = FF // 2, 512

    def kernel(*refs):
        refs = Refs(refs)
        rows_ref, upstream_ref, attended_ref, small_ref, bias_ref = refs.take(5)
        output_hbm, inner_hbm, outer_hbm = refs.take(3)
        result_ref, residual_ref, turned_ref, sums_ref, bias_sum_ref = refs.take(5)
        grad_output_hbm, grad_inner_hbm, grad_outer_hbm = refs.take(3)
        output_w, inner_w, outer_w, load_sems = refs.take(4)
        grad_output, grad_inner, grad_outer, store_sems = refs.take(4)
        partial, got, pairs, send_sum, recv_sum, send_pair, recv_pair = refs.take(7)
        attended_rows, middle, unit_one, slope, active, grad_hidden = refs.take(6)
        me, other = group_me("core"), group_peer("core", 1)
        loads = [
            pltpu.make_async_copy(source, target, load_sems.at[at])
            for at, (source, target) in enumerate(
                ((output_hbm, output_w), (inner_hbm, inner_w), (outer_hbm, outer_w))
            )
        ]
        stores = [
            pltpu.make_async_copy(source, target, store_sems.at[at])
            for at, (source, target) in enumerate(
                ((grad_outer, grad_outer_hbm), (grad_inner, grad_inner_hbm), (grad_output, grad_output_hbm))
            )
        ]
        sums = [
            remote(partial.at[other], got.at[at], send_sum.at[at], recv_sum.at[at], "core", other)
            for at in range(3)
        ]
        gathers = [
            remote(pairs.at[at, me], pairs.at[at, me], send_pair.at[at], recv_pair.at[at], "core", other)
            for at in range(3)
        ]
        output_bias, first_gain, first_shift, outer_bias, second_gain, second_shift = (
            small_ref[at : at + 1, :] for at in range(6)
        )

        def pair_of(at):
            return pairs[at].reshape(PAIR, D)

        for load in loads:
            load.start()
        enter(["core"])
        attended_rows[...] = attended_ref[...].astype(F32).T.astype(BF).reshape(2, ROWS, D // 2)
        loads[0].wait()
        partial[other] = dot(attended_rows[other], output_w[...])
        sums[0].start()
        partial[me] = dot(attended_rows[me], output_w[...])
        sums[0].wait()
        hidden = rows_ref[...].astype(F32) + (partial[me] + got[0] + output_bias)
        normed, inverse_one = normalize(hidden)
        unit_one[...] = normed
        middle[...] = normed * first_gain + first_shift
        pairs[0, me] = middle[...].astype(BF)
        gathers[0].start()
        loads[1].wait()

        def inner_half(half):
            def one_tile(at, carry):
                here = pl.ds(pl.multiple_of(at * tile, tile), tile)
                value = dot(pairs[0, half], inner_w[:, here]) + bias_ref[:, here]
                part = 0.5 * (1.0 + lax.erf(value * (0.5**0.5)))
                active[half, :, here] = (value * part).astype(BF)
                density = jnp.exp(-0.5 * value * value) * ((2.0 * math.pi) ** -0.5)
                slope[half, :, here] = part + value * density
                return carry

            lax.fori_loop(0, units // tile, one_tile, 0)

        inner_half(me)
        gathers[0].wait()
        inner_half(other)
        loads[2].wait()
        partial[other] = dot(active[other], outer_w[...])
        sums[1].start()
        partial[me] = dot(active[me], outer_w[...])
        sums[1].wait()
        unit_two, inverse_two = normalize(middle[...] + (partial[me] + got[1] + outer_bias))
        result_ref[...] = (unit_two * second_gain + second_shift).astype(BF)
        upstream = upstream_ref[...].astype(F32)
        grad_mid = normalize_back(upstream, unit_two, inverse_two, second_gain)
        pairs[1, me] = grad_mid.astype(BF)
        gathers[1].start()
        middle[...] = grad_mid
        sums_ref[3:4, :] = sum_rows(grad_mid.astype(BF).astype(F32))
        sums_ref[4:5, :] = sum_rows(upstream * unit_two)
        sums_ref[5:6, :] = sum_rows(upstream)
        bias_sum_ref[...] = jnp.zeros_like(bias_sum_ref)

        def hidden_half(half):
            def one_tile(at, carry):
                here = pl.ds(pl.multiple_of(at * tile, tile), tile)
                value = dot(pairs[1, half], outer_w[here, :], ((1,), (1,)))
                value = (value * slope[half, :, here]).astype(BF)
                grad_hidden[half, :, here] = value
                bias_sum_ref[:, here] += sum_rows(value.astype(F32))
                return carry

            lax.fori_loop(0, units // tile, one_tile, 0)

        hidden_half(me)
        gathers[1].wait()
        hidden_half(other)
        partial[other] = dot(grad_hidden[other], inner_w[...], ((1,), (1,)))
        sums[2].start()
        partial[me] = dot(grad_hidden[me], inner_w[...], ((1,), (1,)))

        def outer_tile(at, carry):
            here = pl.ds(pl.multiple_of(at * tile, tile), tile)
            hidden = active[:, :, here].reshape(PAIR, tile)
            grad_outer[here, :] = dot(hidden, pair_of(1), ((0,), (0,))).astype(BF)
            return carry

        lax.fori_loop(0, units // tile, outer_tile, 0)
        stores[0].start()
        sums[2].wait()
        grad_middle = partial[me] + got[2] + middle[...]
        normed = unit_one[...]
        residual = normalize_back(grad_middle, normed, inverse_one, first_gain)
        pairs[2, me] = residual.astype(BF)
        gathers[2].start()
        residual_ref[...] = residual
        sums_ref[0:1, :] = sum_rows(residual.astype(BF).astype(F32))
        sums_ref[1:2, :] = sum_rows(grad_middle * normed)
        sums_ref[2:3, :] = sum_rows(grad_middle)
        sums_ref[6:8, :] = jnp.zeros((2, D), F32)

        def inner_tile(at, carry):
            here = pl.ds(pl.multiple_of(at * tile, tile), tile)
            hidden = grad_hidden[:, :, here].reshape(PAIR, tile)
            grad_inner[:, here] = dot(pair_of(0), hidden, ((0,), (0,))).astype(BF)
            return carry

        lax.fori_loop(0, units // tile, inner_tile, 0)
        stores[1].start()
        gathers[2].wait()
        grad_output[...] = dot(attended_ref[...], pair_of(2)).astype(BF)
        stores[2].start()
        turned_ref[...] = dot(output_w[...], pair_of(2), ((1,), (1,))).astype(BF)
        for store in stores:
            store.wait()

    grads = [(D // 2, D), (D, units), (units, D)]
    return pl.pallas_call(
        kernel,
        out_shape=[
            jax.ShapeDtypeStruct((ROWS, D), BF),
            jax.ShapeDtypeStruct((ROWS, D), F32),
            jax.ShapeDtypeStruct((D // 2, PAIR), BF),
            jax.ShapeDtypeStruct((8, D), F32),
            jax.ShapeDtypeStruct((1, units), F32),
        ]
        + [jax.ShapeDtypeStruct(shape, BF) for shape in grads],
        in_specs=[VMEM] * 5 + [ANY] * 3,
        out_specs=[VMEM] * 5 + [ANY] * 3,
        scratch_shapes=[pltpu.VMEM(shape, BF) for shape in grads]
        + [dma(3)]
        + [pltpu.VMEM(shape, BF) for shape in grads]
        + [
            dma(3),
            pltpu.VMEM((2, ROWS, D), F32),
            pltpu.VMEM((3, ROWS, D), F32),
            pltpu.VMEM((3, 2, ROWS, D), BF),
            dma(3),
            dma(3),
            dma(3),
            dma(3),
            pltpu.VMEM((2, ROWS, D // 2), BF),
            pltpu.VMEM((ROWS, D), F32),
            pltpu.VMEM((ROWS, D), F32),
            pltpu.VMEM((2, ROWS, units), F32),
            pltpu.VMEM((2, ROWS, units), BF),
            pltpu.VMEM((2, ROWS, units), BF),
        ],
        compiler_params=params(identifier, 56),
        name="feed_forward",
    )(rows, cotangent, attended, small, inner_bias, output_weight, inner_weight, outer_weight)


def per_device(
    tokens,
    cotangent,
    w_query,
    b_query,
    w_key,
    w_value,
    b_value,
    w_output,
    b_output,
    first_gain,
    first_shift,
    w_inner,
    b_inner,
    w_outer,
    b_outer,
    second_gain,
    second_shift,
):
    rows = tokens[0]

    small_part = jnp.concatenate(
        [
            jnp.stack(
                [b_query, b_value, b_output, first_gain, first_shift, b_outer, second_gain, second_shift]
            ),
            b_inner.reshape(4, 128),
            jnp.zeros((4, 128), BF),
        ]
    )
    (
        rows_turned,
        qkv_weight,
        rows_small,
        inner_bias,
        output_weight,
        inner_weight,
        outer_weight,
        qkv_got,
        summed,
        attended,
        stat,
    ) = forward(0, rows, w_query, w_key, w_value, small_part, w_output, w_inner, w_outer)
    (
        result,
        grad_residual,
        grad_attended,
        row_sums,
        grad_inner_bias,
        grad_output_weight,
        grad_inner_weight,
        grad_outer_weight,
    ) = feed_forward(
        1,
        rows,
        cotangent[0],
        attended.reshape(D // 2, PAIR),
        output_weight.reshape(D // 2, D),
        inner_weight.reshape(D, FF // 2),
        outer_weight.reshape(FF // 2, D),
        rows_small,
        inner_bias,
    )
    token_grad, *shares = backward(
        2,
        qkv_got,
        summed,
        stat,
        grad_attended.reshape(CHIPS, HD, PAIR),
        rows_turned,
        qkv_weight,
        grad_residual,
        row_sums,
        grad_inner_bias,
        grad_output_weight.reshape(SEQ, HD, D),
        grad_inner_weight.reshape(SEQ, 128, FF // 2),
        grad_outer_weight.reshape(SEQ, 256, D),
    )
    query, key, value, output, inner, outer, query_bias, value_bias, inner_bias, *whole = unpack(*shares)
    whole = [row.reshape(128) for row in whole]
    return (
        result[None],
        token_grad[None],
        query,
        query_bias.reshape(128),
        key,
        value,
        value_bias.reshape(128),
        output,
        whole[0],
        whole[1],
        whole[2],
        inner,
        inner_bias.reshape(512),
        outer,
        whole[3],
        whole[4],
        whole[5],
    )


def solution(mesh):
    row = P("seq", None)
    vector = P("seq")
    placed = P("seq", "ctx", None)
    return jax.shard_map(
        per_device,
        mesh=mesh,
        in_specs=(
            placed,
            placed,
            row,
            vector,
            row,
            row,
            vector,
            row,
            vector,
            vector,
            vector,
            row,
            vector,
            row,
            vector,
            vector,
            vector,
        ),
        out_specs=(
            placed,
            placed,
            row,
            vector,
            row,
            row,
            vector,
            row,
            vector,
            vector,
            vector,
            row,
            vector,
            row,
            vector,
            vector,
            vector,
        ),
        check_vma=False,
    )
```

```python
import functools
import math

import jax
import jax.numpy as jnp
from jax import lax
from jax.experimental import pallas as pl
from jax.experimental.pallas import tpu as pltpu
from jax.sharding import PartitionSpec as P

D = 1024
HEADS = 16
HD = 64
FF = 4096
SEQ = 8
CHIPS = 8
ROWS = 192
PAIR = 2 * ROWS
LENGTH = CHIPS * PAIR
SCALE2 = HD ** (-0.5) * math.log2(math.e)
BLOCK = 512
BF = jnp.bfloat16
F32 = jnp.float32
ANY = pl.BlockSpec(memory_space=pl.ANY)
VMEM = pl.BlockSpec(memory_space=pltpu.VMEM)


def dot(left, right, dims=((1,), (0,))):
    return lax.dot_general(left, right, (dims, ((), ())), preferred_element_type=F32)


SIZES = {"seq": 8, "chip": 8, "x": 4, "y": 2, "z": 4, "half": 2, "core": 2}


def group_size(group):
    return SIZES[group]


def group_me(group):
    seq, ctx = lax.axis_index("seq"), lax.axis_index("ctx")
    if group == "seq":
        return seq
    if group == "x":
        return lax.rem(seq, 4)
    if group == "y":
        return lax.div(seq, 4)
    if group == "core":
        return lax.rem(ctx, 2)
    if group == "half":
        return lax.div(ctx, 8)
    if group == "z":
        return lax.rem(lax.div(ctx, 2), 4)
    return lax.div(ctx, 2)


def group_device(group, index):
    seq, ctx = lax.axis_index("seq"), lax.axis_index("ctx")
    if group == "seq":
        return (index, ctx)
    if group == "x":
        return (lax.div(seq, 4) * 4 + index, ctx)
    if group == "y":
        return (index * 4 + lax.rem(seq, 4), ctx)
    if group == "core":
        return (seq, lax.div(ctx, 2) * 2 + index)
    if group == "half":
        return (seq, index * 8 + lax.rem(ctx, 8))
    if group == "z":
        return (seq, lax.div(ctx, 8) * 8 + index * 2 + lax.rem(ctx, 2))
    return (seq, index * 2 + lax.rem(ctx, 2))


def group_peer(group, step):
    return lax.rem(group_me(group) + step, group_size(group))


def enter(groups):
    barrier = pltpu.get_barrier_semaphore()
    count = 0
    for group in groups:
        for step in range(1, group_size(group)):
            pl.semaphore_signal(
                barrier,
                inc=1,
                device_id=group_device(group, group_peer(group, step)),
                device_id_type=pl.DeviceIdType.MESH,
            )
            count += 1
    pl.semaphore_wait(barrier, count)


def remote(source, target, send, recv, group, peer):
    return pltpu.make_async_remote_copy(
        src_ref=source,
        dst_ref=target,
        send_sem=send,
        recv_sem=recv,
        device_id=group_device(group, peer),
        device_id_type=pl.DeviceIdType.MESH,
    )


def dma(*shape):
    return pltpu.SemaphoreType.DMA(shape)


class Exchange:
    def __init__(self, kind, group, source, target, refs, rows=None):
        self.kind, self.group = kind, group
        self.source, self.target, self.rows = source, target, rows
        self.send, self.recv = refs[:2]
        if rows is None:
            self.own, self.own_held = refs[2:]

    @staticmethod
    def scratch(kind, group, value, rows=None):
        count = group_size(group) - 1
        if rows is not None:
            return [dma(count), dma(count)]
        piece = value.shape if kind == "ag" else value.shape[1:]
        return [dma(count), dma(count), dma(2), pltpu.VMEM(piece, value.dtype)]

    def copies(self):
        me = group_me(self.group)
        made = []
        for step in range(1, group_size(self.group)):
            peer = group_peer(self.group, step)
            piece = self.source if self.kind == "ag" else self.source.at[peer]
            target = self.target.at[me]
            if self.rows is not None:
                piece, target = piece.at[pl.ds(*self.rows)], target.at[pl.ds(*self.rows)]
            made.append(
                remote(piece, target, self.send.at[step - 1], self.recv.at[step - 1], self.group, peer)
            )
        return made

    def own_copies(self):
        me = group_me(self.group)
        piece = self.source if self.kind == "ag" else self.source.at[me]
        return (
            pltpu.make_async_copy(piece, self.own_held, self.own.at[0]),
            pltpu.make_async_copy(self.own_held, self.target.at[me], self.own.at[1]),
        )

    def start(self):
        for copy in self.copies():
            copy.start()
        if self.rows is None:
            self.own_copies()[0].start()

    def wait(self):
        if self.rows is None:
            own_in, own_out = self.own_copies()
            own_in.wait()
            own_out.start()
            own_out.wait()
        for copy in self.copies():
            copy.wait()


class Own:
    def __init__(self, source, target, refs):
        self.source, self.target = source, target.at[group_me("seq")]
        self.sems, self.held = refs

    @staticmethod
    def scratch(value):
        return [dma(2), pltpu.VMEM(value.shape, value.dtype)]

    def start(self):
        pltpu.make_async_copy(self.source, self.held, self.sems.at[0]).start()

    def wait(self):
        pltpu.make_async_copy(self.source, self.held, self.sems.at[0]).wait()
        copy = pltpu.make_async_copy(self.held, self.target, self.sems.at[1])
        copy.start()
        copy.wait()


class RelayGather:
    def __init__(self, source, target, span, order, refs):
        self.source, self.target, self.span, self.order = source, target, span, order
        self.send, self.recv = refs
        x, y = group_me("x"), group_me("y")
        back = [lax.rem(x + 4 - step, 4) for step in range(1, 4)]
        if order == "yx":
            self.owners = [(1 - y) * 4 + x] + [y * 4 + at for at in back] + [(1 - y) * 4 + at for at in back]
        else:
            self.owners = [y * 4 + at for at in back] + [(1 - y) * 4 + x] + [(1 - y) * 4 + at for at in back]

    @staticmethod
    def scratch():
        return [dma(7), dma(7)]

    def slot(self, at):
        x, y = group_me("x"), group_me("y")
        piece = self.source.at[self.span]
        place = self.target.at[y * 4 + x, self.span]
        if self.order == "yx":
            group, step = ("y", 1) if at == 0 else ("x", (at - 1) % 3 + 1)
            if at >= 4:
                piece = place = self.target.at[self.owners[0], self.span]
        else:
            group, step = ("x", at + 1) if at < 3 else ("y", 1)
            if at >= 4:
                piece = place = self.target.at[self.owners[at - 4], self.span]
        return remote(piece, place, self.send.at[at], self.recv.at[at], group, group_peer(group, step))

    def start(self):
        for at in range(4):
            self.slot(at).start()

    def forward(self):
        if self.order == "yx":
            self.slot(0).wait_recv()
            for at in range(4, 7):
                self.slot(at).start()
        else:
            for at in range(3):
                self.slot(at).wait_recv()
                self.slot(at + 4).start()

    def waited(self):
        return (0,) if self.order == "yx" else (0, 1, 2)

    def wait_recv(self):
        for at in range(7):
            if at not in self.waited():
                self.slot(at).wait_recv()

    def wait_send(self):
        for at in range(7):
            self.slot(at).wait_send()

    def wait(self):
        self.wait_recv()
        self.wait_send()


class SplitGather:
    def __init__(self, source, target, refs):
        rows = source.shape[0] // 4
        self.span = pl.ds(pl.multiple_of(group_me("z") * rows, 16), rows)
        self.target = target
        self.relay = RelayGather(source, target, self.span, "yx", refs[:2])
        self.send, self.recv = refs[2:]

    @staticmethod
    def scratch():
        return RelayGather.scratch() + [dma(21), dma(21)]

    def second(self, slot, hop):
        at = slot * 3 + hop - 1
        piece = self.target.at[self.relay.owners[slot], self.span]
        return remote(piece, piece, self.send.at[at], self.recv.at[at], "z", group_peer("z", hop))

    def start(self):
        self.relay.start()

    def forward_x(self):
        self.relay.forward()
        for hop in range(1, 4):
            self.second(0, hop).start()

    def forward_z(self):
        for slot in range(1, 7):
            self.relay.slot(slot).wait_recv()
            for hop in range(1, 4):
                self.second(slot, hop).start()

    def wait(self):
        self.relay.wait_send()
        for slot in range(7):
            for hop in range(1, 4):
                self.second(slot, hop).wait()


class RelayReduce:
    def __init__(self, source, rows, order, refs):
        self.source, self.span, self.order = source, pl.ds(*rows), order
        self.group, self.group_two = order
        self.size, self.size_two = group_size(order[0]), group_size(order[1])
        self.send, self.recv, self.local, self.got, self.total, self.send_two, self.recv_two, self.got_two = refs

    @staticmethod
    def scratch(value, rows, order):
        piece, kind = (rows[1], value.shape[2]), value.dtype
        one, two = group_size(order[0]), group_size(order[1])
        pieces = (one - 1) * two
        return [
            dma(pieces),
            dma(pieces),
            dma(two),
            pltpu.VMEM((pieces,) + piece, kind),
            pltpu.VMEM((two,) + piece, kind),
            dma(two - 1),
            dma(two - 1),
            pltpu.VMEM((two - 1,) + piece, kind),
        ]

    def piece(self, one, two):
        return self.source.at[one * 4 + two if self.order == "yx" else two * 4 + one, self.span]

    def first(self):
        made = []
        for step in range(1, self.size):
            peer = group_peer(self.group, step)
            for two in range(self.size_two):
                at = (step - 1) * self.size_two + two
                made.append(
                    remote(
                        self.piece(peer, two), self.got.at[at], self.send.at[at], self.recv.at[at], self.group, peer
                    )
                )
        return made

    def own(self):
        return [
            pltpu.make_async_copy(
                self.piece(group_me(self.group), two), self.total.at[two], self.local.at[two]
            )
            for two in range(self.size_two)
        ]

    def second(self):
        made = []
        for step in range(1, self.size_two):
            peer = group_peer(self.group_two, step)
            made.append(
                remote(
                    self.total.at[peer],
                    self.got_two.at[step - 1],
                    self.send_two.at[step - 1],
                    self.recv_two.at[step - 1],
                    self.group_two,
                    peer,
                )
            )
        return made

    def start(self):
        for copy in self.first() + self.own():
            copy.start()

    def forward(self):
        for copy in self.own() + self.first():
            copy.wait()
        for two in range(self.size_two):
            value = self.total[two].astype(F32)
            for step in range(self.size - 1):
                value += self.got[step * self.size_two + two].astype(F32)
            self.total[two] = value.astype(self.total.dtype)
        for copy in self.second():
            copy.start()

    def sum(self):
        for copy in self.second():
            copy.wait()
        value = self.total[group_me(self.group_two)].astype(F32)
        for step in range(self.size_two - 1):
            value += self.got_two[step].astype(F32)
        return value


class SplitReduce:
    def __init__(self, source, refs):
        self.source, self.quarter = source, source.shape[1] // 4
        self.send, self.recv, self.local, self.got, self.total = refs[:5]
        self.relay = RelayReduce(self.total, (0, self.quarter), "xy", refs[5:])

    @staticmethod
    def scratch(value):
        quarter, columns = value.shape[1] // 4, value.shape[2]
        return [dma(3), dma(3), dma()] + [
            pltpu.VMEM((3, 8, quarter, columns), BF),
            pltpu.VMEM((8, quarter, columns), BF),
        ] + RelayReduce.scratch(value, (0, quarter), "xy")

    def part(self, index):
        return self.source.at[:, pl.ds(pl.multiple_of(index * self.quarter, 16), self.quarter)]

    def first(self, hop):
        peer = group_peer("z", hop)
        return remote(
            self.part(peer), self.got.at[hop - 1], self.send.at[hop - 1], self.recv.at[hop - 1], "z", peer
        )

    def own_copy(self):
        return pltpu.make_async_copy(self.part(group_me("z")), self.total, self.local)

    def start(self):
        for hop in range(1, 4):
            self.first(hop).start()
        self.own_copy().start()

    def forward_z(self):
        self.own_copy().wait()
        for hop in range(1, 4):
            self.first(hop).wait()

        def add(at, carry):
            value = self.total[at].astype(F32)
            for hop in range(3):
                value += self.got[hop, at].astype(F32)
            self.total[at] = value.astype(BF)
            return carry

        lax.fori_loop(0, 8, add, 0)
        self.relay.start()

    def forward(self):
        self.relay.forward()

    def sum(self):
        return self.relay.sum()


class Refs:
    def __init__(self, refs):
        self.refs, self.at = refs, 0

    def take(self, count):
        self.at += count
        return self.refs[self.at - count : self.at]

    def left(self):
        return self.refs[self.at :]


def target_shape(kind, group, value):
    shape = value.shape if kind == "a2a" else (group_size(group),) + value.shape
    return jax.ShapeDtypeStruct(shape, value.dtype)


def params(identifier, mebibytes):
    return pltpu.CompilerParams(
        collective_id=identifier,
        has_side_effects=True,
        vmem_limit_bytes=mebibytes * 1024 * 1024,
    )


def forward(identifier, rows, w_query, w_key, w_value, small_part, w_output, w_inner, w_outer):
    columns = SEQ * 3 * HD
    qkv_part = jax.ShapeDtypeStruct((128, columns), BF)
    heads_shape = jax.ShapeDtypeStruct((CHIPS, 3 * HD, PAIR), BF)
    low_shape = jax.ShapeDtypeStruct((CHIPS, HD, PAIR), BF)
    output_part = jax.ShapeDtypeStruct((HD, D), BF)
    inner_part = jax.ShapeDtypeStruct((128, FF // 2), BF)
    outer_part = jax.ShapeDtypeStruct((256, D), BF)

    def kernel(*refs):
        refs = Refs(refs)
        rows_ref, query_ref, key_ref, value_ref, small_ref, output_ref, inner_ref, outer_ref = refs.take(8)
        turned_out, qkv_out, small_out, bias_out, output_out, inner_out, outer_out = refs.take(7)
        qkv_got, summed_ref, back_ref, stat_ref = refs.take(4)
        qkv_ref, inner_held, rows_out, small_got, heads, query_t, keys, value_t, low = refs.take(9)
        core = group_me("core")

        def mine(value, axis):
            half = value.shape[axis] // 2
            low_half = lax.slice_in_dim(value, 0, half, axis=axis)
            return jnp.where(core == 0, low_half, lax.slice_in_dim(value, half, 2 * half, axis=axis))

        output_ref = output_ref.at[pl.ds(pl.multiple_of(core * HD, HD), HD)]
        outer_ref = outer_ref.at[pl.ds(pl.multiple_of(core * 256, 256), 256)]
        split = SplitGather(qkv_ref.at[pl.ds(0, 64)], qkv_out, refs.take(4))
        one_way = RelayGather(qkv_ref, qkv_out, pl.ds(64, 32), "yx", refs.take(2))
        other_way = RelayGather(qkv_ref, qkv_out, pl.ds(96, 32), "xy", refs.take(2))
        qkv_own = Own(qkv_ref, qkv_out, refs.take(2))
        small = Exchange("ag", "seq", small_ref, small_got, refs.take(4))
        pair = Exchange("ag", "core", rows_ref, rows_out, refs.take(4))
        first = Exchange("a2a", "chip", heads, qkv_got, refs.take(4))
        last = Exchange("a2a", "chip", low, back_ref, refs.take(4))
        inner = SplitGather(inner_held, inner_out, refs.take(4))
        output = RelayGather(output_ref, output_out, pl.ds(0, HD), "yx", refs.take(2))
        outer_one = RelayGather(outer_ref, outer_out, pl.ds(0, 128), "yx", refs.take(2))
        outer_two = RelayGather(outer_ref, outer_out, pl.ds(128, 128), "xy", refs.take(2))
        owns = [
            Own(source, target, refs.take(2))
            for source, target in (
                (output_ref, output_out),
                (inner_held, inner_out),
                (outer_ref, outer_out),
            )
        ]
        for owner in range(0, SEQ, 2):
            parts = []
            for head in (owner, owner + 1):
                for ref in (query_ref, key_ref, value_ref):
                    parts.append(mine(ref[:, head * 128 : (head + 1) * 128].astype(F32), 1))
            qkv_ref[:, owner * 192 : (owner + 2) * 192] = jnp.concatenate(parts, axis=1).astype(BF)
        enter(["seq", "chip", "core"])
        for one in (split, one_way, other_way, qkv_own, small, pair):
            one.start()
        for owner in range(SEQ):
            here = pl.ds(pl.multiple_of(owner * 512 + core * 256, 256), 256)
            inner_held[:, owner * 256 : (owner + 1) * 256] = inner_ref[:, here]
        for own in owns:
            own.start()
        split.forward_x()
        one_way.forward()
        split.forward_z()
        inner.start()
        other_way.forward()
        for one in (pair, small, qkv_own, one_way, other_way, split):
            one.wait()
        inner.forward_x()
        weight = qkv_out[...].reshape(D, columns)
        turned = dot(rows_out[...].reshape(PAIR, D), weight).T
        for chip in range(CHIPS):
            shift = mine(small_got[chip].astype(F32).T, 0)
            part = turned[chip * 3 * HD : (chip + 1) * 3 * HD]
            heads[chip, 0:HD, :] = (part[:HD] + shift[:, 0:1]).astype(BF)
            heads[chip, HD : 2 * HD, :] = part[HD : 2 * HD].astype(BF)
            heads[chip, 2 * HD :, :] = (part[2 * HD :] + shift[:, 1:2]).astype(BF)
        first.start()
        inner.forward_z()
        outer_two.start()
        output.start()
        outer_one.start()
        output.forward()
        turned_out[...] = rows_out[...].reshape(PAIR, D).astype(F32).T.astype(BF)
        for owner in range(SEQ):
            at = slice(owner * 128, (owner + 1) * 128)
            values = small_got[owner].astype(F32)
            small_out[:, at] = values[2:10]
            for row in range(2):
                at = slice(owner * 256 + row * 128, owner * 256 + (row + 1) * 128)
                bias_out[:, at] = jnp.where(core == 0, values[8 + row : 9 + row], values[10 + row : 11 + row])
        first.wait()
        for chip in range(CHIPS):
            at = pl.ds(chip * PAIR, PAIR)
            query_t[:, at] = qkv_got[chip, 0:HD, :]
            keys[at, :] = qkv_got[chip, HD : 2 * HD, :].astype(F32).T.astype(BF)
            value_t[:, at] = qkv_got[chip, 2 * HD : 3 * HD, :]
        outer_one.forward()

        def one_block(block, carry):
            at = pl.ds(pl.multiple_of(block * BLOCK, BLOCK), BLOCK)
            query = query_t[:, at]
            top = jnp.full((1, BLOCK), -1e30, F32)
            total = jnp.zeros((1, BLOCK), F32)
            summed = jnp.zeros((HD, BLOCK), F32)
            for part in range(LENGTH // BLOCK):
                here = slice(part * BLOCK, (part + 1) * BLOCK)
                scores = dot(keys[here, :], query) * SCALE2
                new_top = jnp.maximum(top, jnp.max(scores, axis=0, keepdims=True))
                factor = jnp.exp2(top - new_top)
                weights = jnp.exp2(scores - new_top)
                total = total * factor + jnp.sum(weights, axis=0, keepdims=True)
                summed = summed * factor + dot(value_t[:, here], weights.astype(BF))
                top = new_top
            summed_ref[:, at] = summed / total
            stat_ref[:, at] = top + jnp.log2(total)
            return carry

        lax.fori_loop(0, 2, one_block, 0)
        outer_two.forward()
        lax.fori_loop(2, LENGTH // BLOCK, one_block, 0)
        for chip in range(CHIPS):
            low[chip] = summed_ref[:, chip * PAIR : (chip + 1) * PAIR].astype(BF)
        last.start()
        for one in [last, output, inner, outer_one, outer_two] + owns:
            one.wait()

    return pl.pallas_call(
        kernel,
        out_shape=[
            jax.ShapeDtypeStruct((D, PAIR), BF),
            target_shape("ag", "seq", qkv_part),
            jax.ShapeDtypeStruct((8, D), F32),
            jax.ShapeDtypeStruct((1, FF // 2), F32),
            target_shape("ag", "seq", output_part),
            target_shape("ag", "seq", inner_part),
            target_shape("ag", "seq", outer_part),
            heads_shape,
            jax.ShapeDtypeStruct((HD, LENGTH), F32),
            low_shape,
            jax.ShapeDtypeStruct((1, LENGTH), F32),
        ],
        in_specs=[ANY] + [VMEM] * 3 + [ANY] * 2 + [VMEM, ANY],
        out_specs=[VMEM] * 4 + [ANY] * 3 + [VMEM] * 4,
        scratch_shapes=[
            pltpu.VMEM(qkv_part.shape, BF),
            pltpu.VMEM(inner_part.shape, BF),
            pltpu.VMEM((2, ROWS, D), BF),
            pltpu.VMEM((SEQ, 16, 128), BF),
            pltpu.VMEM(heads_shape.shape, BF),
            pltpu.VMEM((HD, LENGTH), BF),
            pltpu.VMEM((LENGTH, HD), BF),
            pltpu.VMEM((HD, LENGTH), BF),
            pltpu.VMEM(low_shape.shape, BF),
        ]
        + SplitGather.scratch()
        + RelayGather.scratch()
        + RelayGather.scratch()
        + Own.scratch(qkv_part)
        + Exchange.scratch("ag", "seq", small_part)
        + Exchange.scratch("ag", "core", rows)
        + Exchange.scratch("a2a", "chip", heads_shape)
        + Exchange.scratch("a2a", "chip", low_shape)
        + SplitGather.scratch()
        + RelayGather.scratch()
        + RelayGather.scratch()
        + RelayGather.scratch()
        + Own.scratch(output_part)
        + Own.scratch(inner_part)
        + Own.scratch(outer_part),
        compiler_params=params(identifier, 62),
        name="forward",
    )(rows, w_query, w_key, w_value, small_part, w_output, w_inner, w_outer)


class Scatter:
    def __init__(self, group, source, refs):
        self.group, self.source = group, source
        send, recv, self.got = refs
        self.copies = [
            remote(
                source.at[group_peer(group, step)],
                self.got.at[step - 1],
                send.at[step - 1],
                recv.at[step - 1],
                group,
                group_peer(group, step),
            )
            for step in range(1, group_size(group))
        ]

    @staticmethod
    def scratch(group, piece, kind):
        count = group_size(group) - 1
        return [dma(count), dma(count), pltpu.VMEM((count,) + piece, kind)]

    def start(self):
        for copy in self.copies:
            copy.start()

    def sum(self):
        for copy in self.copies:
            copy.wait()
        own = self.source[group_me(self.group)].astype(F32)
        return sum((self.got[at].astype(F32) for at in range(group_size(self.group) - 1)), own)


class Swap:
    def __init__(self, group, source, refs):
        send, recv, self.got = refs
        self.source = source
        self.copy = remote(source, self.got, send, recv, group, group_peer(group, 1))

    @staticmethod
    def scratch(piece, kind):
        return [dma(), dma(), pltpu.VMEM(piece, kind)]

    def start(self):
        self.copy.start()

    def sum(self):
        self.copy.wait()
        return self.source[...].astype(F32) + self.got[...].astype(F32)


class Spread:
    def __init__(self, group, held, refs):
        send, recv, send_core, recv_core = refs
        self.group, self.held = group, held
        mine = held.at[group_me("core")]
        self.mine = mine
        piece = mine.at[group_me(group)]
        self.copies = [
            remote(piece, piece, send.at[step - 1], recv.at[step - 1], group, group_peer(group, step))
            for step in range(1, group_size(group))
        ]
        self.last = remote(mine, mine, send_core, recv_core, "core", group_peer("core", 1))

    @staticmethod
    def scratch(group):
        count = group_size(group) - 1
        return [dma(count), dma(count), dma(), dma()]

    def start(self, value):
        self.mine[group_me(self.group)] = value.astype(self.held.dtype)
        for copy in self.copies:
            copy.start()

    def forward(self):
        for copy in self.copies:
            copy.wait()
        self.last.start()

    def wait(self):
        self.last.wait()


def backward(
    identifier,
    qkv_got,
    summed,
    stat,
    grad,
    rows_t,
    qkv_weight,
    residual,
    row_sums,
    bias_sums,
    output_grad,
    inner_grad,
    outer_grad,
):
    columns = SEQ * 3 * HD
    half = 64
    chip_piece = (16, columns)
    vector = (8, 128)
    grads_shape = jax.ShapeDtypeStruct((SEQ, 128, columns), BF)
    inner_half_shape = jax.ShapeDtypeStruct((SEQ, 64, FF // 2), BF)

    def kernel(*refs):
        refs = Refs(refs)
        qkv_ref, summed_ref, stat_ref, grad_ref, rows_ref, weight_ref = refs.take(6)
        residual_ref, row_sums_ref, bias_sums_ref = refs.take(3)
        output_ref, inner_ref, outer_ref = refs.take(3)
        token_out, qkv_out, output_out, inner_out, outer_out, vector_out, bias_out = refs.take(7)
        grad_got, heads_got, query_t, queries, key_t, keys, values, up_t, ups, delta_ref = refs.take(10)
        grad_query, grad_key, grad_value, low = refs.take(4)
        vectors_ref, grads, bias, partial, token_got, token_send, token_recv = refs.take(7)
        output_sum, outer_sum, output_mine, inner_mine, outer_mine, qkv_sum = refs.take(6)
        first = Exchange("a2a", "chip", grad_ref, grad_got, refs.take(4))
        last = Exchange("a2a", "chip", low, heads_got, refs.take(4))
        inner_one = SplitReduce(inner_ref.at[:, pl.ds(0, 64)], refs.take(13))
        inner_two = SplitReduce(inner_ref.at[:, pl.ds(64, 64)], refs.take(13))
        output = RelayReduce(output_ref, (0, HD), "xy", refs.take(8))
        outer_one = RelayReduce(outer_ref, (0, 128), "xy", refs.take(8))
        outer_two = RelayReduce(outer_ref, (128, 128), "yx", refs.take(8))
        qkv_one = RelayReduce(grads, (0, half), "xy", refs.take(8))
        qkv_two = RelayReduce(grads, (half, half), "yx", refs.take(8))
        vector_seq = Scatter("seq", vectors_ref, refs.take(3))
        bias_seq = Scatter("seq", bias, refs.take(3))
        output_z = Scatter("z", output_sum, refs.take(3))
        outer_z = Scatter("z", outer_sum, refs.take(3))
        output_half = Swap("half", output_mine, refs.take(3))
        outer_half = Swap("half", outer_mine, refs.take(3))
        inner_half = Swap("half", inner_mine, refs.take(3))
        qkv_chip = Scatter("chip", qkv_sum, refs.take(3))
        output_all = Spread("z", output_out, refs.take(4))
        outer_all = Spread("z", outer_out, refs.take(4))
        inner_all = Spread("z", inner_out, refs.take(4))
        qkv_all = Spread("chip", qkv_out, refs.take(4))
        vector_all = Spread("chip", vector_out, refs.take(4))
        bias_all = Spread("chip", bias_out, refs.take(4))
        other = group_peer("core", 1)
        token = remote(partial.at[other], token_got, token_send, token_recv, "core", other)

        for owner in range(SEQ):
            vectors_ref[owner, 0:6, :] = row_sums_ref[0:6, owner * 128 : (owner + 1) * 128]
            for row in range(2):
                at = slice(owner * 256 + row * 128, owner * 256 + (row + 1) * 128)
                vectors_ref[owner, 6 + row : 7 + row, :] = bias_sums_ref[:, at]
        enter(["seq", "chip", "core"])
        for one in (first, inner_one, outer_two, output, outer_one, vector_seq):
            one.start()
        for chip in range(CHIPS):
            at = pl.ds(chip * PAIR, PAIR)
            query_t[:, at] = qkv_ref[chip, 0:HD, :]
            queries[at, :] = qkv_ref[chip, 0:HD, :].astype(F32).T.astype(BF)
            key_t[:, at] = qkv_ref[chip, HD : 2 * HD, :]
            keys[at, :] = qkv_ref[chip, HD : 2 * HD, :].astype(F32).T.astype(BF)
            values[at, :] = qkv_ref[chip, 2 * HD : 3 * HD, :].astype(F32).T.astype(BF)
        grad_key[...] = jnp.zeros_like(grad_key)
        grad_value[...] = jnp.zeros_like(grad_value)
        first.wait()
        for chip in range(CHIPS):
            at = pl.ds(chip * PAIR, PAIR)
            up = grad_got[chip].astype(F32)
            up_t[:, at] = grad_got[chip]
            ups[at, :] = up.T.astype(BF)
            delta_ref[:, at] = jnp.sum(up * summed_ref[:, at], axis=0, keepdims=True)

        def one_block(block, carry):
            at = pl.ds(pl.multiple_of(block * BLOCK, BLOCK), BLOCK)
            query, up = query_t[:, at], up_t[:, at]
            query_rows, up_rows = queries[at, :], ups[at, :]
            stat, delta = stat_ref[:, at], delta_ref[:, at]
            gathered = jnp.zeros((HD, BLOCK), F32)
            for part in range(LENGTH // BLOCK):
                here = slice(part * BLOCK, (part + 1) * BLOCK)
                scores = dot(keys[here, :], query) * SCALE2
                probs = jnp.exp2(scores - stat)
                grad_value[here, :] += dot(probs.astype(BF), up_rows)
                slope = dot(values[here, :], up) - delta
                grad_scores = (probs * slope).astype(BF)
                grad_key[here, :] += dot(grad_scores, query_rows)
                gathered += dot(key_t[:, here], grad_scores)
            grad_query[:, at] = gathered
            return carry

        lax.fori_loop(0, LENGTH // BLOCK, one_block, 0)
        scale = HD ** (-0.5)
        for chip in range(CHIPS):
            at = slice(chip * PAIR, (chip + 1) * PAIR)
            low[chip, 0:HD, :] = (grad_query[:, at] * scale).astype(BF)
            low[chip, HD : 2 * HD, :] = (grad_key[at, :] * scale).T.astype(BF)
            low[chip, 2 * HD : 3 * HD, :] = grad_value[at, :].T.astype(BF)
        last.start()
        output.forward()
        outer_two.forward()
        outer_one.forward()
        vector_all.start(vector_seq.sum())
        last.wait()

        heads = heads_got[...].reshape(columns, PAIR)

        def weight_rows(owner, carry):
            at = pl.ds(pl.multiple_of(owner * 128, 128), 128)
            grads[owner] = dot(rows_ref[at, :], heads, ((1,), (1,))).astype(BF)
            bias[owner] = dot(jnp.ones((8, PAIR), BF), heads_got[owner], ((1,), (1,)))
            return carry

        lax.fori_loop(0, SEQ, weight_rows, 0)
        qkv_two.start()
        qkv_one.start()
        bias_seq.start()
        inner_one.forward_z()
        inner_two.start()
        output_sum[...] = output.sum().astype(BF).reshape(output_sum.shape)
        output_z.start()
        outer_sum[2:] = outer_two.sum().astype(BF).reshape(2, 64, D)
        outer_sum[:2] = outer_one.sum().astype(BF).reshape(2, 64, D)
        outer_z.start()
        turned = dot(weight_ref[...].reshape(D, columns), heads).T
        partial[0] = turned[:ROWS]
        partial[1] = turned[ROWS:]
        token.start()
        qkv_two.forward()
        qkv_one.forward()
        inner_one.forward()
        output_mine[...] = output_z.sum().astype(BF)
        output_half.start()
        outer_mine[...] = outer_z.sum().astype(BF)
        outer_half.start()
        bias_all.start(bias_seq.sum())
        upper = qkv_one.sum().reshape(CHIPS, 8, columns)
        lower = qkv_two.sum().reshape(CHIPS, 8, columns)
        qkv_sum[...] = jnp.concatenate([upper, lower], axis=1).astype(BF)
        qkv_chip.start()
        inner_two.forward_z()
        output_all.start(output_half.sum())
        outer_all.start(outer_half.sum())
        inner_mine[:16] = inner_one.sum().astype(BF)
        token.wait()
        token_out[...] = residual_ref[...] + partial[group_me("core")] + token_got[...]
        qkv_all.start(qkv_chip.sum())
        inner_two.forward()
        vector_all.forward()
        bias_all.forward()
        inner_mine[16:] = inner_two.sum().astype(BF)
        inner_half.start()
        output_all.forward()
        outer_all.forward()
        qkv_all.forward()
        inner_all.start(inner_half.sum())
        inner_all.forward()
        for one in (vector_all, bias_all, output_all, outer_all, qkv_all, inner_all):
            one.wait()

    return pl.pallas_call(
        kernel,
        out_shape=[
            jax.ShapeDtypeStruct((ROWS, D), F32),
            jax.ShapeDtypeStruct((2, CHIPS) + chip_piece, BF),
            jax.ShapeDtypeStruct((2, 4, 16, D), BF),
            jax.ShapeDtypeStruct((2, 4, 32, FF // 2), BF),
            jax.ShapeDtypeStruct((2, 4, 64, D), BF),
            jax.ShapeDtypeStruct((2, CHIPS) + vector, F32),
            jax.ShapeDtypeStruct((2, CHIPS, 8, 3 * HD), F32),
        ],
        in_specs=[VMEM] * 9 + [ANY] * 3,
        out_specs=[VMEM] * 7,
        scratch_shapes=[
            pltpu.VMEM(grad.shape, BF),
            pltpu.VMEM(qkv_got.shape, BF),
            pltpu.VMEM((HD, LENGTH), BF),
            pltpu.VMEM((LENGTH, HD), BF),
            pltpu.VMEM((HD, LENGTH), BF),
            pltpu.VMEM((LENGTH, HD), BF),
            pltpu.VMEM((LENGTH, HD), BF),
            pltpu.VMEM((HD, LENGTH), BF),
            pltpu.VMEM((LENGTH, HD), BF),
            pltpu.VMEM((1, LENGTH), F32),
            pltpu.VMEM((HD, LENGTH), F32),
            pltpu.VMEM((LENGTH, HD), F32),
            pltpu.VMEM((LENGTH, HD), F32),
            pltpu.VMEM((CHIPS, 3 * HD, PAIR), BF),
            pltpu.VMEM((SEQ,) + vector, F32),
            pltpu.VMEM((SEQ, 128, columns), BF),
            pltpu.VMEM((SEQ, 8, 3 * HD), F32),
            pltpu.VMEM((2, ROWS, D), F32),
            pltpu.VMEM((ROWS, D), F32),
            dma(),
            dma(),
            pltpu.VMEM((4, 16, D), BF),
            pltpu.VMEM((4, 64, D), BF),
            pltpu.VMEM((16, D), BF),
            pltpu.VMEM((32, FF // 2), BF),
            pltpu.VMEM((64, D), BF),
            pltpu.VMEM((CHIPS,) + chip_piece, BF),
        ]
        + Exchange.scratch("a2a", "chip", grad)
        + Exchange.scratch("a2a", "chip", qkv_got)
        + SplitReduce.scratch(inner_half_shape)
        + SplitReduce.scratch(inner_half_shape)
        + RelayReduce.scratch(output_grad, (0, HD), "xy")
        + RelayReduce.scratch(outer_grad, (0, 128), "xy")
        + RelayReduce.scratch(outer_grad, (128, 128), "yx")
        + RelayReduce.scratch(grads_shape, (0, half), "xy")
        + RelayReduce.scratch(grads_shape, (half, half), "yx")
        + Scatter.scratch("seq", vector, F32)
        + Scatter.scratch("seq", (8, 3 * HD), F32)
        + Scatter.scratch("z", (16, D), BF)
        + Scatter.scratch("z", (64, D), BF)
        + Swap.scratch((16, D), BF)
        + Swap.scratch((64, D), BF)
        + Swap.scratch((32, FF // 2), BF)
        + Scatter.scratch("chip", chip_piece, BF)
        + Spread.scratch("z")
        + Spread.scratch("z")
        + Spread.scratch("z")
        + Spread.scratch("chip")
        + Spread.scratch("chip")
        + Spread.scratch("chip"),
        compiler_params=params(identifier, 62),
        name="backward",
    )(
        qkv_got,
        summed,
        stat,
        grad,
        rows_t,
        qkv_weight,
        residual,
        row_sums,
        bias_sums,
        output_grad,
        inner_grad,
        outer_grad,
    )


def unpack(qkv, output, inner, outer, vectors, biases):
    def kernel(*refs):
        refs = Refs(refs)
        qkv_ref, output_ref, inner_ref, outer_ref, vectors_ref, biases_ref = refs.take(6)
        query, key, value, output_out, inner_out, outer_out = refs.take(6)
        query_bias, value_bias, inner_bias = refs.take(3)
        vector = [jnp.sum(vectors_ref[core], axis=0) for core in range(2)]
        bias = [jnp.sum(biases_ref[core], axis=0)[0:1] for core in range(2)]
        for row, out in enumerate(refs.left()):
            out[...] = vector[0][row : row + 1] + vector[1][row : row + 1]
        query_bias[...] = jnp.concatenate([part[:, :HD] for part in bias], axis=1)
        value_bias[...] = jnp.concatenate([part[:, 2 * HD :] for part in bias], axis=1)
        for core in range(2):
            for row in range(2):
                start = core * 256 + row * 128
                inner_bias[:, start : start + 128] = vector[core][6 + row : 7 + row]

        def place(pair, rows):
            for kind, out in enumerate((query, key, value)):
                for head in range(SEQ):
                    at = head * 3 * HD + kind * HD
                    out[rows, head * 128 : (head + 1) * 128] = jnp.concatenate(
                        [part[:, at : at + HD] for part in pair], axis=1
                    )

        for chip in range(CHIPS):
            pair = [qkv_ref[core, chip].astype(F32) for core in range(2)]
            place([part[:8] for part in pair], slice(chip * 8, (chip + 1) * 8))
            place([part[8:] for part in pair], slice(64 + chip * 8, 64 + (chip + 1) * 8))
        for core in range(2):
            for quarter in range(4):
                start = core * HD + quarter * 16
                output_out[start : start + 16] = output_ref[core, quarter].astype(F32)
                start = core * 256 + quarter * 64
                outer_out[start : start + 64] = outer_ref[core, quarter].astype(F32)
                for half in range(2):
                    rows = slice(half * 64 + quarter * 16, half * 64 + (quarter + 1) * 16)
                    for owner in range(SEQ):
                        start = owner * 512 + core * 256
                        inner_out[rows, start : start + 256] = inner_ref[
                            core, quarter, half * 16 : (half + 1) * 16, owner * 256 : (owner + 1) * 256
                        ].astype(F32)

    shapes = [(128, D)] * 4 + [(128, FF), (512, D), (1, 128), (1, 128), (1, 512)] + [(1, 128)] * 6
    return pl.pallas_call(
        kernel,
        out_shape=[jax.ShapeDtypeStruct(shape, F32) for shape in shapes],
        in_specs=[VMEM] * 6,
        out_specs=[VMEM] * 15,
        compiler_params=pltpu.CompilerParams(vmem_limit_bytes=62 * 1024 * 1024),
        name="unpack",
    )(qkv, output, inner, outer, vectors, biases)


def normalize(hidden):
    centered = hidden - jnp.mean(hidden, axis=-1, keepdims=True)
    inverse = lax.rsqrt(jnp.mean(centered * centered, axis=-1, keepdims=True) + 1e-05)
    return centered * inverse, inverse


def normalize_back(upstream, normed, inverse, gain):
    scaled = upstream * gain
    return inverse * (
        scaled
        - jnp.mean(scaled, axis=-1, keepdims=True)
        - normed * jnp.mean(scaled * normed, axis=-1, keepdims=True)
    )


def sum_rows(value):
    return jnp.sum(value, axis=0, keepdims=True)


def feed_forward(identifier, rows, cotangent, attended, output_weight, inner_weight, outer_weight, small, inner_bias):
    units, tile = FF // 2, 512

    def kernel(*refs):
        refs = Refs(refs)
        rows_ref, upstream_ref, attended_ref, small_ref, bias_ref = refs.take(5)
        output_hbm, inner_hbm, outer_hbm = refs.take(3)
        result_ref, residual_ref, turned_ref, sums_ref, bias_sum_ref = refs.take(5)
        grad_output_hbm, grad_inner_hbm, grad_outer_hbm = refs.take(3)
        output_w, inner_w, outer_w, load_sems = refs.take(4)
        grad_output, grad_inner, grad_outer, store_sems = refs.take(4)
        partial, got, pairs, send_sum, recv_sum, send_pair, recv_pair = refs.take(7)
        attended_rows, middle, unit_one, slope, active, grad_hidden = refs.take(6)
        me, other = group_me("core"), group_peer("core", 1)
        loads = [
            pltpu.make_async_copy(source, target, load_sems.at[at])
            for at, (source, target) in enumerate(
                ((output_hbm, output_w), (inner_hbm, inner_w), (outer_hbm, outer_w))
            )
        ]
        stores = [
            pltpu.make_async_copy(source, target, store_sems.at[at])
            for at, (source, target) in enumerate(
                ((grad_outer, grad_outer_hbm), (grad_inner, grad_inner_hbm), (grad_output, grad_output_hbm))
            )
        ]
        sums = [
            remote(partial.at[other], got.at[at], send_sum.at[at], recv_sum.at[at], "core", other)
            for at in range(3)
        ]
        gathers = [
            remote(pairs.at[at, me], pairs.at[at, me], send_pair.at[at], recv_pair.at[at], "core", other)
            for at in range(3)
        ]
        output_bias, first_gain, first_shift, outer_bias, second_gain, second_shift = (
            small_ref[at : at + 1, :] for at in range(6)
        )

        def pair_of(at):
            return pairs[at].reshape(PAIR, D)

        for load in loads:
            load.start()
        enter(["core"])
        attended_rows[...] = attended_ref[...].astype(F32).T.astype(BF).reshape(2, ROWS, D // 2)
        loads[0].wait()
        partial[other] = dot(attended_rows[other], output_w[...])
        sums[0].start()
        partial[me] = dot(attended_rows[me], output_w[...])
        sums[0].wait()
        hidden = rows_ref[...].astype(F32) + (partial[me] + got[0] + output_bias)
        normed, inverse_one = normalize(hidden)
        unit_one[...] = normed
        middle[...] = normed * first_gain + first_shift
        pairs[0, me] = middle[...].astype(BF)
        gathers[0].start()
        loads[1].wait()

        def inner_half(half):
            def one_tile(at, carry):
                here = pl.ds(pl.multiple_of(at * tile, tile), tile)
                value = dot(pairs[0, half], inner_w[:, here]) + bias_ref[:, here]
                part = 0.5 * (1.0 + lax.erf(value * (0.5**0.5)))
                active[half, :, here] = (value * part).astype(BF)
                density = jnp.exp(-0.5 * value * value) * ((2.0 * math.pi) ** -0.5)
                slope[half, :, here] = part + value * density
                return carry

            lax.fori_loop(0, units // tile, one_tile, 0)

        inner_half(me)
        gathers[0].wait()
        inner_half(other)
        loads[2].wait()
        partial[other] = dot(active[other], outer_w[...])
        sums[1].start()
        partial[me] = dot(active[me], outer_w[...])
        sums[1].wait()
        unit_two, inverse_two = normalize(middle[...] + (partial[me] + got[1] + outer_bias))
        result_ref[...] = (unit_two * second_gain + second_shift).astype(BF)
        upstream = upstream_ref[...].astype(F32)
        grad_mid = normalize_back(upstream, unit_two, inverse_two, second_gain)
        pairs[1, me] = grad_mid.astype(BF)
        gathers[1].start()
        middle[...] = grad_mid
        sums_ref[3:4, :] = sum_rows(grad_mid.astype(BF).astype(F32))
        sums_ref[4:5, :] = sum_rows(upstream * unit_two)
        sums_ref[5:6, :] = sum_rows(upstream)
        bias_sum_ref[...] = jnp.zeros_like(bias_sum_ref)

        def hidden_half(half):
            def one_tile(at, carry):
                here = pl.ds(pl.multiple_of(at * tile, tile), tile)
                value = dot(pairs[1, half], outer_w[here, :], ((1,), (1,)))
                value = (value * slope[half, :, here]).astype(BF)
                grad_hidden[half, :, here] = value
                bias_sum_ref[:, here] += sum_rows(value.astype(F32))
                return carry

            lax.fori_loop(0, units // tile, one_tile, 0)

        hidden_half(me)
        gathers[1].wait()
        hidden_half(other)
        partial[other] = dot(grad_hidden[other], inner_w[...], ((1,), (1,)))
        sums[2].start()
        partial[me] = dot(grad_hidden[me], inner_w[...], ((1,), (1,)))

        def outer_tile(at, carry):
            here = pl.ds(pl.multiple_of(at * tile, tile), tile)
            hidden = active[:, :, here].reshape(PAIR, tile)
            grad_outer[here, :] = dot(hidden, pair_of(1), ((0,), (0,))).astype(BF)
            return carry

        lax.fori_loop(0, units // tile, outer_tile, 0)
        stores[0].start()
        sums[2].wait()
        grad_middle = partial[me] + got[2] + middle[...]
        normed = unit_one[...]
        residual = normalize_back(grad_middle, normed, inverse_one, first_gain)
        pairs[2, me] = residual.astype(BF)
        gathers[2].start()
        residual_ref[...] = residual
        sums_ref[0:1, :] = sum_rows(residual.astype(BF).astype(F32))
        sums_ref[1:2, :] = sum_rows(grad_middle * normed)
        sums_ref[2:3, :] = sum_rows(grad_middle)
        sums_ref[6:8, :] = jnp.zeros((2, D), F32)

        def inner_tile(at, carry):
            here = pl.ds(pl.multiple_of(at * tile, tile), tile)
            hidden = grad_hidden[:, :, here].reshape(PAIR, tile)
            grad_inner[:, here] = dot(pair_of(0), hidden, ((0,), (0,))).astype(BF)
            return carry

        lax.fori_loop(0, units // tile, inner_tile, 0)
        stores[1].start()
        gathers[2].wait()
        grad_output[...] = dot(attended_ref[...], pair_of(2)).astype(BF)
        stores[2].start()
        turned_ref[...] = dot(output_w[...], pair_of(2), ((1,), (1,))).astype(BF)
        for store in stores:
            store.wait()

    grads = [(D // 2, D), (D, units), (units, D)]
    return pl.pallas_call(
        kernel,
        out_shape=[
            jax.ShapeDtypeStruct((ROWS, D), BF),
            jax.ShapeDtypeStruct((ROWS, D), F32),
            jax.ShapeDtypeStruct((D // 2, PAIR), BF),
            jax.ShapeDtypeStruct((8, D), F32),
            jax.ShapeDtypeStruct((1, units), F32),
        ]
        + [jax.ShapeDtypeStruct(shape, BF) for shape in grads],
        in_specs=[VMEM] * 5 + [ANY] * 3,
        out_specs=[VMEM] * 5 + [ANY] * 3,
        scratch_shapes=[pltpu.VMEM(shape, BF) for shape in grads]
        + [dma(3)]
        + [pltpu.VMEM(shape, BF) for shape in grads]
        + [
            dma(3),
            pltpu.VMEM((2, ROWS, D), F32),
            pltpu.VMEM((3, ROWS, D), F32),
            pltpu.VMEM((3, 2, ROWS, D), BF),
            dma(3),
            dma(3),
            dma(3),
            dma(3),
            pltpu.VMEM((2, ROWS, D // 2), BF),
            pltpu.VMEM((ROWS, D), F32),
            pltpu.VMEM((ROWS, D), F32),
            pltpu.VMEM((2, ROWS, units), F32),
            pltpu.VMEM((2, ROWS, units), BF),
            pltpu.VMEM((2, ROWS, units), BF),
        ],
        compiler_params=params(identifier, 62),
        name="feed_forward",
    )(rows, cotangent, attended, small, inner_bias, output_weight, inner_weight, outer_weight)


def per_device(
    tokens,
    cotangent,
    w_query,
    b_query,
    w_key,
    w_value,
    b_value,
    w_output,
    b_output,
    first_gain,
    first_shift,
    w_inner,
    b_inner,
    w_outer,
    b_outer,
    second_gain,
    second_shift,
):
    rows = tokens[0]

    small_part = jnp.concatenate(
        [
            jnp.stack(
                [b_query, b_value, b_output, first_gain, first_shift, b_outer, second_gain, second_shift]
            ),
            b_inner.reshape(4, 128),
            jnp.zeros((4, 128), BF),
        ]
    )
    (
        rows_turned,
        qkv_weight,
        rows_small,
        inner_bias,
        output_weight,
        inner_weight,
        outer_weight,
        qkv_got,
        summed,
        attended,
        stat,
    ) = forward(0, rows, w_query, w_key, w_value, small_part, w_output, w_inner, w_outer)
    (
        result,
        grad_residual,
        grad_attended,
        row_sums,
        grad_inner_bias,
        grad_output_weight,
        grad_inner_weight,
        grad_outer_weight,
    ) = feed_forward(
        1,
        rows,
        cotangent[0],
        attended.reshape(D // 2, PAIR),
        output_weight.reshape(D // 2, D),
        inner_weight.reshape(D, FF // 2),
        outer_weight.reshape(FF // 2, D),
        rows_small,
        inner_bias,
    )
    token_grad, *shares = backward(
        2,
        qkv_got,
        summed,
        stat,
        grad_attended.reshape(CHIPS, HD, PAIR),
        rows_turned,
        qkv_weight,
        grad_residual,
        row_sums,
        grad_inner_bias,
        grad_output_weight.reshape(SEQ, HD, D),
        grad_inner_weight.reshape(SEQ, 128, FF // 2),
        grad_outer_weight.reshape(SEQ, 256, D),
    )
    query, key, value, output, inner, outer, query_bias, value_bias, inner_bias, *whole = unpack(*shares)
    whole = [row.reshape(128) for row in whole]
    return (
        result[None],
        token_grad[None],
        query,
        query_bias.reshape(128),
        key,
        value,
        value_bias.reshape(128),
        output,
        whole[0],
        whole[1],
        whole[2],
        inner,
        inner_bias.reshape(512),
        outer,
        whole[3],
        whole[4],
        whole[5],
    )


def solution(mesh):
    row = P("seq", None)
    vector = P("seq")
    placed = P("seq", "ctx", None)
    return jax.shard_map(
        per_device,
        mesh=mesh,
        in_specs=(
            placed,
            placed,
            row,
            vector,
            row,
            row,
            vector,
            row,
            vector,
            vector,
            vector,
            row,
            vector,
            row,
            vector,
            vector,
            vector,
        ),
        out_specs=(
            placed,
            placed,
            row,
            vector,
            row,
            row,
            vector,
            row,
            vector,
            vector,
            vector,
            row,
            vector,
            row,
            vector,
            vector,
            vector,
        ),
        check_vma=False,
    )
```

```python
import functools
import math

import jax
import jax.numpy as jnp
from jax import lax
from jax.experimental import pallas as pl
from jax.experimental.pallas import tpu as pltpu
from jax.sharding import PartitionSpec as P

D = 1024
HEADS = 16
HD = 64
FF = 4096
SEQ = 8
CHIPS = 8
ROWS = 192
PAIR = 2 * ROWS
LENGTH = CHIPS * PAIR
SCALE2 = HD ** (-0.5) * math.log2(math.e)
BLOCK = 512
BF = jnp.bfloat16
F32 = jnp.float32
ANY = pl.BlockSpec(memory_space=pl.ANY)
VMEM = pl.BlockSpec(memory_space=pltpu.VMEM)


def dot(left, right, dims=((1,), (0,))):
    return lax.dot_general(left, right, (dims, ((), ())), preferred_element_type=F32)


SIZES = {"seq": 8, "chip": 8, "x": 4, "y": 2, "z": 4, "half": 2, "core": 2}


def group_size(group):
    return SIZES[group]


def group_me(group):
    seq, ctx = lax.axis_index("seq"), lax.axis_index("ctx")
    if group == "seq":
        return seq
    if group == "x":
        return lax.rem(seq, 4)
    if group == "y":
        return lax.div(seq, 4)
    if group == "core":
        return lax.rem(ctx, 2)
    if group == "half":
        return lax.div(ctx, 8)
    if group == "z":
        return lax.rem(lax.div(ctx, 2), 4)
    return lax.div(ctx, 2)


def group_device(group, index):
    seq, ctx = lax.axis_index("seq"), lax.axis_index("ctx")
    if group == "seq":
        return (index, ctx)
    if group == "x":
        return (lax.div(seq, 4) * 4 + index, ctx)
    if group == "y":
        return (index * 4 + lax.rem(seq, 4), ctx)
    if group == "core":
        return (seq, lax.div(ctx, 2) * 2 + index)
    if group == "half":
        return (seq, index * 8 + lax.rem(ctx, 8))
    if group == "z":
        return (seq, lax.div(ctx, 8) * 8 + index * 2 + lax.rem(ctx, 2))
    return (seq, index * 2 + lax.rem(ctx, 2))


def group_peer(group, step):
    return lax.rem(group_me(group) + step, group_size(group))


def enter(groups):
    barrier = pltpu.get_barrier_semaphore()
    count = 0
    for group in groups:
        for step in range(1, group_size(group)):
            pl.semaphore_signal(
                barrier,
                inc=1,
                device_id=group_device(group, group_peer(group, step)),
                device_id_type=pl.DeviceIdType.MESH,
            )
            count += 1
    pl.semaphore_wait(barrier, count)


def remote(source, target, send, recv, group, peer):
    return pltpu.make_async_remote_copy(
        src_ref=source,
        dst_ref=target,
        send_sem=send,
        recv_sem=recv,
        device_id=group_device(group, peer),
        device_id_type=pl.DeviceIdType.MESH,
    )


def dma(*shape):
    return pltpu.SemaphoreType.DMA(shape)


class Exchange:
    def __init__(self, kind, group, source, target, refs, rows=None):
        self.kind, self.group = kind, group
        self.source, self.target, self.rows = source, target, rows
        self.send, self.recv = refs[:2]
        if rows is None:
            self.own, self.own_held = refs[2:]

    @staticmethod
    def scratch(kind, group, value, rows=None):
        count = group_size(group) - 1
        if rows is not None:
            return [dma(count), dma(count)]
        piece = value.shape if kind == "ag" else value.shape[1:]
        return [dma(count), dma(count), dma(2), pltpu.VMEM(piece, value.dtype)]

    def copies(self):
        me = group_me(self.group)
        made = []
        for step in range(1, group_size(self.group)):
            peer = group_peer(self.group, step)
            piece = self.source if self.kind == "ag" else self.source.at[peer]
            target = self.target.at[me]
            if self.rows is not None:
                piece, target = piece.at[pl.ds(*self.rows)], target.at[pl.ds(*self.rows)]
            made.append(
                remote(piece, target, self.send.at[step - 1], self.recv.at[step - 1], self.group, peer)
            )
        return made

    def own_copies(self):
        me = group_me(self.group)
        piece = self.source if self.kind == "ag" else self.source.at[me]
        return (
            pltpu.make_async_copy(piece, self.own_held, self.own.at[0]),
            pltpu.make_async_copy(self.own_held, self.target.at[me], self.own.at[1]),
        )

    def start(self):
        for copy in self.copies():
            copy.start()
        if self.rows is None:
            self.own_copies()[0].start()

    def wait(self):
        if self.rows is None:
            own_in, own_out = self.own_copies()
            own_in.wait()
            own_out.start()
            own_out.wait()
        for copy in self.copies():
            copy.wait()


class Own:
    def __init__(self, source, target, refs):
        self.source, self.target = source, target.at[group_me("seq")]
        self.sems, self.held = refs

    @staticmethod
    def scratch(value):
        return [dma(2), pltpu.VMEM(value.shape, value.dtype)]

    def start(self):
        pltpu.make_async_copy(self.source, self.held, self.sems.at[0]).start()

    def wait(self):
        pltpu.make_async_copy(self.source, self.held, self.sems.at[0]).wait()
        copy = pltpu.make_async_copy(self.held, self.target, self.sems.at[1])
        copy.start()
        copy.wait()


class RelayGather:
    def __init__(self, source, target, span, order, refs):
        self.source, self.target, self.span, self.order = source, target, span, order
        self.send, self.recv = refs
        x, y = group_me("x"), group_me("y")
        back = [lax.rem(x + 4 - step, 4) for step in range(1, 4)]
        if order == "yx":
            self.owners = [(1 - y) * 4 + x] + [y * 4 + at for at in back] + [(1 - y) * 4 + at for at in back]
        else:
            self.owners = [y * 4 + at for at in back] + [(1 - y) * 4 + x] + [(1 - y) * 4 + at for at in back]

    @staticmethod
    def scratch():
        return [dma(7), dma(7)]

    def slot(self, at):
        x, y = group_me("x"), group_me("y")
        piece = self.source.at[self.span]
        place = self.target.at[y * 4 + x, self.span]
        if self.order == "yx":
            group, step = ("y", 1) if at == 0 else ("x", (at - 1) % 3 + 1)
            if at >= 4:
                piece = place = self.target.at[self.owners[0], self.span]
        else:
            group, step = ("x", at + 1) if at < 3 else ("y", 1)
            if at >= 4:
                piece = place = self.target.at[self.owners[at - 4], self.span]
        return remote(piece, place, self.send.at[at], self.recv.at[at], group, group_peer(group, step))

    def start(self):
        for at in range(4):
            self.slot(at).start()

    def forward(self):
        if self.order == "yx":
            self.slot(0).wait_recv()
            for at in range(4, 7):
                self.slot(at).start()
        else:
            for at in range(3):
                self.slot(at).wait_recv()
                self.slot(at + 4).start()

    def waited(self):
        return (0,) if self.order == "yx" else (0, 1, 2)

    def wait_recv(self):
        for at in range(7):
            if at not in self.waited():
                self.slot(at).wait_recv()

    def wait_send(self):
        for at in range(7):
            self.slot(at).wait_send()

    def wait(self):
        self.wait_recv()
        self.wait_send()


class SplitGather:
    def __init__(self, source, target, refs):
        rows = source.shape[0] // 4
        self.span = pl.ds(pl.multiple_of(group_me("z") * rows, 16), rows)
        self.target = target
        self.relay = RelayGather(source, target, self.span, "yx", refs[:2])
        self.send, self.recv = refs[2:]

    @staticmethod
    def scratch():
        return RelayGather.scratch() + [dma(21), dma(21)]

    def second(self, slot, hop):
        at = slot * 3 + hop - 1
        piece = self.target.at[self.relay.owners[slot], self.span]
        return remote(piece, piece, self.send.at[at], self.recv.at[at], "z", group_peer("z", hop))

    def start(self):
        self.relay.start()

    def forward_x(self):
        self.relay.forward()
        for hop in range(1, 4):
            self.second(0, hop).start()

    def forward_z(self):
        for slot in range(1, 7):
            self.relay.slot(slot).wait_recv()
            for hop in range(1, 4):
                self.second(slot, hop).start()

    def wait(self):
        self.relay.wait_send()
        for slot in range(7):
            for hop in range(1, 4):
                self.second(slot, hop).wait()


class RelayReduce:
    def __init__(self, source, rows, order, refs):
        self.source, self.span, self.order = source, pl.ds(*rows), order
        self.group, self.group_two = order
        self.size, self.size_two = group_size(order[0]), group_size(order[1])
        self.send, self.recv, self.local, self.got, self.total, self.send_two, self.recv_two, self.got_two = refs

    @staticmethod
    def scratch(value, rows, order):
        piece, kind = (rows[1], value.shape[2]), value.dtype
        one, two = group_size(order[0]), group_size(order[1])
        pieces = (one - 1) * two
        return [
            dma(pieces),
            dma(pieces),
            dma(two),
            pltpu.VMEM((pieces,) + piece, kind),
            pltpu.VMEM((two,) + piece, kind),
            dma(two - 1),
            dma(two - 1),
            pltpu.VMEM((two - 1,) + piece, kind),
        ]

    def piece(self, one, two):
        return self.source.at[one * 4 + two if self.order == "yx" else two * 4 + one, self.span]

    def first(self):
        made = []
        for step in range(1, self.size):
            peer = group_peer(self.group, step)
            for two in range(self.size_two):
                at = (step - 1) * self.size_two + two
                made.append(
                    remote(
                        self.piece(peer, two), self.got.at[at], self.send.at[at], self.recv.at[at], self.group, peer
                    )
                )
        return made

    def own(self):
        return [
            pltpu.make_async_copy(
                self.piece(group_me(self.group), two), self.total.at[two], self.local.at[two]
            )
            for two in range(self.size_two)
        ]

    def second(self):
        made = []
        for step in range(1, self.size_two):
            peer = group_peer(self.group_two, step)
            made.append(
                remote(
                    self.total.at[peer],
                    self.got_two.at[step - 1],
                    self.send_two.at[step - 1],
                    self.recv_two.at[step - 1],
                    self.group_two,
                    peer,
                )
            )
        return made

    def start(self):
        for copy in self.first() + self.own():
            copy.start()

    def forward(self):
        for copy in self.own() + self.first():
            copy.wait()
        for two in range(self.size_two):
            value = self.total[two].astype(F32)
            for step in range(self.size - 1):
                value += self.got[step * self.size_two + two].astype(F32)
            self.total[two] = value.astype(self.total.dtype)
        for copy in self.second():
            copy.start()

    def sum(self):
        for copy in self.second():
            copy.wait()
        value = self.total[group_me(self.group_two)].astype(F32)
        for step in range(self.size_two - 1):
            value += self.got_two[step].astype(F32)
        return value


class SplitReduce:
    def __init__(self, source, refs):
        self.source, self.quarter = source, source.shape[1] // 4
        self.send, self.recv, self.local, self.got, self.total = refs[:5]
        self.relay = RelayReduce(self.total, (0, self.quarter), "xy", refs[5:])

    @staticmethod
    def scratch(value):
        quarter, columns = value.shape[1] // 4, value.shape[2]
        return [dma(3), dma(3), dma()] + [
            pltpu.VMEM((3, 8, quarter, columns), BF),
            pltpu.VMEM((8, quarter, columns), BF),
        ] + RelayReduce.scratch(value, (0, quarter), "xy")

    def part(self, index):
        return self.source.at[:, pl.ds(pl.multiple_of(index * self.quarter, 16), self.quarter)]

    def first(self, hop):
        peer = group_peer("z", hop)
        return remote(
            self.part(peer), self.got.at[hop - 1], self.send.at[hop - 1], self.recv.at[hop - 1], "z", peer
        )

    def own_copy(self):
        return pltpu.make_async_copy(self.part(group_me("z")), self.total, self.local)

    def start(self):
        for hop in range(1, 4):
            self.first(hop).start()
        self.own_copy().start()

    def forward_z(self):
        self.own_copy().wait()
        for hop in range(1, 4):
            self.first(hop).wait()

        def add(at, carry):
            value = self.total[at].astype(F32)
            for hop in range(3):
                value += self.got[hop, at].astype(F32)
            self.total[at] = value.astype(BF)
            return carry

        lax.fori_loop(0, 8, add, 0)
        self.relay.start()

    def forward(self):
        self.relay.forward()

    def sum(self):
        return self.relay.sum()


class Refs:
    def __init__(self, refs):
        self.refs, self.at = refs, 0

    def take(self, count):
        self.at += count
        return self.refs[self.at - count : self.at]

    def left(self):
        return self.refs[self.at :]


def target_shape(kind, group, value):
    shape = value.shape if kind == "a2a" else (group_size(group),) + value.shape
    return jax.ShapeDtypeStruct(shape, value.dtype)


def params(identifier, mebibytes):
    return pltpu.CompilerParams(
        collective_id=identifier,
        has_side_effects=True,
        vmem_limit_bytes=mebibytes * 1024 * 1024,
    )


def forward(identifier, rows, w_query, w_key, w_value, small_part, w_output, w_inner, w_outer):
    columns = SEQ * 3 * HD
    qkv_part = jax.ShapeDtypeStruct((128, columns), BF)
    heads_shape = jax.ShapeDtypeStruct((CHIPS, 3 * HD, PAIR), BF)
    low_shape = jax.ShapeDtypeStruct((CHIPS, HD, PAIR), BF)
    output_part = jax.ShapeDtypeStruct((HD, D), BF)
    inner_part = jax.ShapeDtypeStruct((128, FF // 2), BF)
    outer_part = jax.ShapeDtypeStruct((256, D), BF)

    def kernel(*refs):
        refs = Refs(refs)
        rows_ref, query_ref, key_ref, value_ref, small_ref, output_ref, inner_ref, outer_ref = refs.take(8)
        turned_out, qkv_out, small_out, bias_out, output_out, inner_out, outer_out = refs.take(7)
        qkv_got, summed_ref, back_ref, stat_ref = refs.take(4)
        qkv_ref, inner_held, rows_out, small_got, heads, query_t, keys, value_t, low = refs.take(9)
        core = group_me("core")

        def mine(value, axis):
            half = value.shape[axis] // 2
            low_half = lax.slice_in_dim(value, 0, half, axis=axis)
            return jnp.where(core == 0, low_half, lax.slice_in_dim(value, half, 2 * half, axis=axis))

        output_ref = output_ref.at[pl.ds(pl.multiple_of(core * HD, HD), HD)]
        outer_ref = outer_ref.at[pl.ds(pl.multiple_of(core * 256, 256), 256)]
        split = SplitGather(qkv_ref.at[pl.ds(0, 64)], qkv_out, refs.take(4))
        one_way = RelayGather(qkv_ref, qkv_out, pl.ds(64, 32), "yx", refs.take(2))
        other_way = RelayGather(qkv_ref, qkv_out, pl.ds(96, 32), "xy", refs.take(2))
        qkv_own = Own(qkv_ref, qkv_out, refs.take(2))
        small = Exchange("ag", "seq", small_ref, small_got, refs.take(4))
        pair = Exchange("ag", "core", rows_ref, rows_out, refs.take(4))
        first = Exchange("a2a", "chip", heads, qkv_got, refs.take(4))
        last = Exchange("a2a", "chip", low, back_ref, refs.take(4))
        inner = SplitGather(inner_held, inner_out, refs.take(4))
        output = RelayGather(output_ref, output_out, pl.ds(0, HD), "yx", refs.take(2))
        outer_one = RelayGather(outer_ref, outer_out, pl.ds(0, 128), "yx", refs.take(2))
        outer_two = RelayGather(outer_ref, outer_out, pl.ds(128, 128), "xy", refs.take(2))
        owns = [
            Own(source, target, refs.take(2))
            for source, target in (
                (output_ref, output_out),
                (inner_held, inner_out),
                (outer_ref, outer_out),
            )
        ]
        for owner in range(0, SEQ, 2):
            parts = []
            for head in (owner, owner + 1):
                for ref in (query_ref, key_ref, value_ref):
                    parts.append(mine(ref[:, head * 128 : (head + 1) * 128].astype(F32), 1))
            qkv_ref[:, owner * 192 : (owner + 2) * 192] = jnp.concatenate(parts, axis=1).astype(BF)
        enter(["seq", "chip", "core"])
        for one in (split, one_way, other_way, qkv_own, small, pair):
            one.start()
        for owner in range(SEQ):
            here = pl.ds(pl.multiple_of(owner * 512 + core * 256, 256), 256)
            inner_held[:, owner * 256 : (owner + 1) * 256] = inner_ref[:, here]
        for own in owns:
            own.start()
        split.forward_x()
        one_way.forward()
        split.forward_z()
        inner.start()
        other_way.forward()
        for one in (pair, small, qkv_own, one_way, other_way, split):
            one.wait()
        inner.forward_x()
        weight = qkv_out[...].reshape(D, columns)
        turned = dot(rows_out[...].reshape(PAIR, D), weight).T
        for chip in range(CHIPS):
            shift = mine(small_got[chip].astype(F32).T, 0)
            part = turned[chip * 3 * HD : (chip + 1) * 3 * HD]
            heads[chip, 0:HD, :] = (part[:HD] + shift[:, 0:1]).astype(BF)
            heads[chip, HD : 2 * HD, :] = part[HD : 2 * HD].astype(BF)
            heads[chip, 2 * HD :, :] = (part[2 * HD :] + shift[:, 1:2]).astype(BF)
        first.start()
        inner.forward_z()
        outer_two.start()
        output.start()
        outer_one.start()
        output.forward()
        turned_out[...] = rows_out[...].reshape(PAIR, D).astype(F32).T.astype(BF)
        for owner in range(SEQ):
            at = slice(owner * 128, (owner + 1) * 128)
            values = small_got[owner].astype(F32)
            small_out[:, at] = values[2:10]
            for row in range(2):
                at = slice(owner * 256 + row * 128, owner * 256 + (row + 1) * 128)
                bias_out[:, at] = jnp.where(core == 0, values[8 + row : 9 + row], values[10 + row : 11 + row])
        first.wait()
        for chip in range(CHIPS):
            at = pl.ds(chip * PAIR, PAIR)
            query_t[:, at] = qkv_got[chip, 0:HD, :]
            keys[at, :] = qkv_got[chip, HD : 2 * HD, :].astype(F32).T.astype(BF)
            value_t[:, at] = qkv_got[chip, 2 * HD : 3 * HD, :]
        outer_one.forward()

        def one_block(block, carry):
            at = pl.ds(pl.multiple_of(block * BLOCK, BLOCK), BLOCK)
            query = query_t[:, at]
            top = jnp.full((1, BLOCK), -1e30, F32)
            total = jnp.zeros((1, BLOCK), F32)
            summed = jnp.zeros((HD, BLOCK), F32)
            for part in range(LENGTH // BLOCK):
                here = slice(part * BLOCK, (part + 1) * BLOCK)
                scores = dot(keys[here, :], query) * SCALE2
                new_top = jnp.maximum(top, jnp.max(scores, axis=0, keepdims=True))
                factor = jnp.exp2(top - new_top)
                weights = jnp.exp2(scores - new_top)
                total = total * factor + jnp.sum(weights, axis=0, keepdims=True)
                summed = summed * factor + dot(value_t[:, here], weights.astype(BF))
                top = new_top
            summed_ref[:, at] = summed / total
            stat_ref[:, at] = top + jnp.log2(total)
            return carry

        lax.fori_loop(0, 2, one_block, 0)
        outer_two.forward()
        lax.fori_loop(2, LENGTH // BLOCK, one_block, 0)
        for chip in range(CHIPS):
            low[chip] = summed_ref[:, chip * PAIR : (chip + 1) * PAIR].astype(BF)
        last.start()
        for one in [last, output, inner, outer_one, outer_two] + owns:
            one.wait()

    return pl.pallas_call(
        kernel,
        out_shape=[
            jax.ShapeDtypeStruct((D, PAIR), BF),
            target_shape("ag", "seq", qkv_part),
            jax.ShapeDtypeStruct((8, D), F32),
            jax.ShapeDtypeStruct((1, FF // 2), F32),
            target_shape("ag", "seq", output_part),
            target_shape("ag", "seq", inner_part),
            target_shape("ag", "seq", outer_part),
            heads_shape,
            jax.ShapeDtypeStruct((HD, LENGTH), F32),
            low_shape,
            jax.ShapeDtypeStruct((1, LENGTH), F32),
        ],
        in_specs=[ANY] + [VMEM] * 3 + [ANY] * 2 + [VMEM, ANY],
        out_specs=[VMEM] * 4 + [ANY] * 3 + [VMEM] * 4,
        scratch_shapes=[
            pltpu.VMEM(qkv_part.shape, BF),
            pltpu.VMEM(inner_part.shape, BF),
            pltpu.VMEM((2, ROWS, D), BF),
            pltpu.VMEM((SEQ, 16, 128), BF),
            pltpu.VMEM(heads_shape.shape, BF),
            pltpu.VMEM((HD, LENGTH), BF),
            pltpu.VMEM((LENGTH, HD), BF),
            pltpu.VMEM((HD, LENGTH), BF),
            pltpu.VMEM(low_shape.shape, BF),
        ]
        + SplitGather.scratch()
        + RelayGather.scratch()
        + RelayGather.scratch()
        + Own.scratch(qkv_part)
        + Exchange.scratch("ag", "seq", small_part)
        + Exchange.scratch("ag", "core", rows)
        + Exchange.scratch("a2a", "chip", heads_shape)
        + Exchange.scratch("a2a", "chip", low_shape)
        + SplitGather.scratch()
        + RelayGather.scratch()
        + RelayGather.scratch()
        + RelayGather.scratch()
        + Own.scratch(output_part)
        + Own.scratch(inner_part)
        + Own.scratch(outer_part),
        compiler_params=params(identifier, 62),
        name="forward",
    )(rows, w_query, w_key, w_value, small_part, w_output, w_inner, w_outer)


class Scatter:
    def __init__(self, group, source, refs):
        self.group, self.source = group, source
        send, recv, self.got = refs
        self.copies = [
            remote(
                source.at[group_peer(group, step)],
                self.got.at[step - 1],
                send.at[step - 1],
                recv.at[step - 1],
                group,
                group_peer(group, step),
            )
            for step in range(1, group_size(group))
        ]

    @staticmethod
    def scratch(group, piece, kind):
        count = group_size(group) - 1
        return [dma(count), dma(count), pltpu.VMEM((count,) + piece, kind)]

    def start(self):
        for copy in self.copies:
            copy.start()

    def sum(self):
        for copy in self.copies:
            copy.wait()
        own = self.source[group_me(self.group)].astype(F32)
        return sum((self.got[at].astype(F32) for at in range(group_size(self.group) - 1)), own)


class Swap:
    def __init__(self, group, source, refs):
        send, recv, self.got = refs
        self.source = source
        self.copy = remote(source, self.got, send, recv, group, group_peer(group, 1))

    @staticmethod
    def scratch(piece, kind):
        return [dma(), dma(), pltpu.VMEM(piece, kind)]

    def start(self):
        self.copy.start()

    def sum(self):
        self.copy.wait()
        return self.source[...].astype(F32) + self.got[...].astype(F32)


class Spread:
    def __init__(self, group, held, refs):
        send, recv, send_core, recv_core = refs
        self.group, self.held = group, held
        mine = held.at[group_me("core")]
        self.mine = mine
        piece = mine.at[group_me(group)]
        self.copies = [
            remote(piece, piece, send.at[step - 1], recv.at[step - 1], group, group_peer(group, step))
            for step in range(1, group_size(group))
        ]
        self.last = remote(mine, mine, send_core, recv_core, "core", group_peer("core", 1))

    @staticmethod
    def scratch(group):
        count = group_size(group) - 1
        return [dma(count), dma(count), dma(), dma()]

    def start(self, value):
        self.mine[group_me(self.group)] = value.astype(self.held.dtype)
        for copy in self.copies:
            copy.start()

    def forward(self):
        for copy in self.copies:
            copy.wait()
        self.last.start()

    def wait(self):
        self.last.wait()


def backward(
    identifier,
    qkv_got,
    summed,
    stat,
    grad,
    rows_t,
    qkv_weight,
    residual,
    row_sums,
    bias_sums,
    output_grad,
    inner_grad,
    outer_grad,
):
    columns = SEQ * 3 * HD
    half = 64
    chip_piece = (16, columns)
    vector = (8, 128)
    grads_shape = jax.ShapeDtypeStruct((SEQ, 128, columns), BF)
    inner_half_shape = jax.ShapeDtypeStruct((SEQ, 64, FF // 2), BF)

    def kernel(*refs):
        refs = Refs(refs)
        qkv_ref, summed_ref, stat_ref, grad_ref, rows_ref, weight_ref = refs.take(6)
        residual_ref, row_sums_ref, bias_sums_ref = refs.take(3)
        output_ref, inner_ref, outer_ref = refs.take(3)
        token_out, qkv_out, output_out, inner_out, outer_out, vector_out, bias_out = refs.take(7)
        grad_got, heads_got, query_t, queries, key_t, keys, values, up_t, ups, delta_ref = refs.take(10)
        grad_query, grad_key, grad_value, low = refs.take(4)
        vectors_ref, grads, bias, partial, token_got, token_send, token_recv = refs.take(7)
        output_sum, outer_sum, output_mine, inner_mine, outer_mine, qkv_sum = refs.take(6)
        first = Exchange("a2a", "chip", grad_ref, grad_got, refs.take(4))
        last = Exchange("a2a", "chip", low, heads_got, refs.take(4))
        inner_one = SplitReduce(inner_ref.at[:, pl.ds(0, 64)], refs.take(13))
        inner_two = SplitReduce(inner_ref.at[:, pl.ds(64, 64)], refs.take(13))
        output = RelayReduce(output_ref, (0, HD), "xy", refs.take(8))
        outer_one = RelayReduce(outer_ref, (0, 128), "xy", refs.take(8))
        outer_two = RelayReduce(outer_ref, (128, 128), "yx", refs.take(8))
        qkv_one = RelayReduce(grads, (0, half), "xy", refs.take(8))
        qkv_two = RelayReduce(grads, (half, half), "yx", refs.take(8))
        vector_seq = Scatter("seq", vectors_ref, refs.take(3))
        bias_seq = Scatter("seq", bias, refs.take(3))
        output_z = Scatter("z", output_sum, refs.take(3))
        outer_z = Scatter("z", outer_sum, refs.take(3))
        output_half = Swap("half", output_mine, refs.take(3))
        outer_half = Swap("half", outer_mine, refs.take(3))
        inner_half = Swap("half", inner_mine, refs.take(3))
        qkv_chip = Scatter("chip", qkv_sum, refs.take(3))
        output_all = Spread("z", output_out, refs.take(4))
        outer_all = Spread("z", outer_out, refs.take(4))
        inner_all = Spread("z", inner_out, refs.take(4))
        qkv_all = Spread("chip", qkv_out, refs.take(4))
        vector_all = Spread("chip", vector_out, refs.take(4))
        bias_all = Spread("chip", bias_out, refs.take(4))
        other = group_peer("core", 1)
        token = remote(partial.at[other], token_got, token_send, token_recv, "core", other)

        for owner in range(SEQ):
            vectors_ref[owner, 0:6, :] = row_sums_ref[0:6, owner * 128 : (owner + 1) * 128]
            for row in range(2):
                at = slice(owner * 256 + row * 128, owner * 256 + (row + 1) * 128)
                vectors_ref[owner, 6 + row : 7 + row, :] = bias_sums_ref[:, at]
        enter(["seq", "chip", "core"])
        for one in (first, inner_one, outer_two, output, outer_one, vector_seq):
            one.start()
        for chip in range(CHIPS):
            at = pl.ds(chip * PAIR, PAIR)
            query_t[:, at] = qkv_ref[chip, 0:HD, :]
            queries[at, :] = qkv_ref[chip, 0:HD, :].astype(F32).T.astype(BF)
            key_t[:, at] = qkv_ref[chip, HD : 2 * HD, :]
            keys[at, :] = qkv_ref[chip, HD : 2 * HD, :].astype(F32).T.astype(BF)
            values[at, :] = qkv_ref[chip, 2 * HD : 3 * HD, :].astype(F32).T.astype(BF)
        grad_key[...] = jnp.zeros_like(grad_key)
        grad_value[...] = jnp.zeros_like(grad_value)
        first.wait()
        for chip in range(CHIPS):
            at = pl.ds(chip * PAIR, PAIR)
            up = grad_got[chip].astype(F32)
            up_t[:, at] = grad_got[chip]
            ups[at, :] = up.T.astype(BF)
            delta_ref[:, at] = jnp.sum(up * summed_ref[:, at], axis=0, keepdims=True)

        def one_block(block, carry):
            at = pl.ds(pl.multiple_of(block * BLOCK, BLOCK), BLOCK)
            query, up = query_t[:, at], up_t[:, at]
            query_rows, up_rows = queries[at, :], ups[at, :]
            stat, delta = stat_ref[:, at], delta_ref[:, at]
            gathered = jnp.zeros((HD, BLOCK), F32)
            for part in range(LENGTH // BLOCK):
                here = slice(part * BLOCK, (part + 1) * BLOCK)
                scores = dot(keys[here, :], query) * SCALE2
                probs = jnp.exp2(scores - stat)
                grad_value[here, :] += dot(probs.astype(BF), up_rows)
                slope = dot(values[here, :], up) - delta
                grad_scores = (probs * slope).astype(BF)
                grad_key[here, :] += dot(grad_scores, query_rows)
                gathered += dot(key_t[:, here], grad_scores)
            grad_query[:, at] = gathered
            return carry

        lax.fori_loop(0, LENGTH // BLOCK, one_block, 0)
        scale = HD ** (-0.5)
        for chip in range(CHIPS):
            at = slice(chip * PAIR, (chip + 1) * PAIR)
            low[chip, 0:HD, :] = (grad_query[:, at] * scale).astype(BF)
            low[chip, HD : 2 * HD, :] = (grad_key[at, :] * scale).T.astype(BF)
            low[chip, 2 * HD : 3 * HD, :] = grad_value[at, :].T.astype(BF)
        last.start()
        output.forward()
        outer_two.forward()
        outer_one.forward()
        vector_all.start(vector_seq.sum())
        last.wait()

        heads = heads_got[...].reshape(columns, PAIR)

        def weight_rows(owner, carry):
            at = pl.ds(pl.multiple_of(owner * 128, 128), 128)
            grads[owner] = dot(rows_ref[at, :], heads, ((1,), (1,))).astype(BF)
            bias[owner] = dot(jnp.ones((8, PAIR), BF), heads_got[owner], ((1,), (1,)))
            return carry

        lax.fori_loop(0, SEQ, weight_rows, 0)
        qkv_two.start()
        qkv_one.start()
        bias_seq.start()
        inner_one.forward_z()
        inner_two.start()
        output_sum[...] = output.sum().astype(BF).reshape(output_sum.shape)
        output_z.start()
        outer_sum[2:] = outer_two.sum().astype(BF).reshape(2, 64, D)
        outer_sum[:2] = outer_one.sum().astype(BF).reshape(2, 64, D)
        outer_z.start()
        turned = dot(weight_ref[...].reshape(D, columns), heads).T
        partial[0] = turned[:ROWS]
        partial[1] = turned[ROWS:]
        token.start()
        qkv_two.forward()
        qkv_one.forward()
        inner_one.forward()
        output_mine[...] = output_z.sum().astype(BF)
        output_half.start()
        outer_mine[...] = outer_z.sum().astype(BF)
        outer_half.start()
        bias_all.start(bias_seq.sum())
        inner_two.forward_z()
        upper = qkv_one.sum().reshape(CHIPS, 8, columns)
        lower = qkv_two.sum().reshape(CHIPS, 8, columns)
        qkv_sum[...] = jnp.concatenate([upper, lower], axis=1).astype(BF)
        qkv_chip.start()
        output_all.start(output_half.sum())
        outer_all.start(outer_half.sum())
        inner_mine[:16] = inner_one.sum().astype(BF)
        token.wait()
        token_out[...] = residual_ref[...] + partial[group_me("core")] + token_got[...]
        qkv_all.start(qkv_chip.sum())
        inner_two.forward()
        vector_all.forward()
        bias_all.forward()
        inner_mine[16:] = inner_two.sum().astype(BF)
        inner_half.start()
        output_all.forward()
        outer_all.forward()
        qkv_all.forward()
        inner_all.start(inner_half.sum())
        inner_all.forward()
        for one in (vector_all, bias_all, output_all, outer_all, qkv_all, inner_all):
            one.wait()

    return pl.pallas_call(
        kernel,
        out_shape=[
            jax.ShapeDtypeStruct((ROWS, D), F32),
            jax.ShapeDtypeStruct((2, CHIPS) + chip_piece, BF),
            jax.ShapeDtypeStruct((2, 4, 16, D), BF),
            jax.ShapeDtypeStruct((2, 4, 32, FF // 2), BF),
            jax.ShapeDtypeStruct((2, 4, 64, D), BF),
            jax.ShapeDtypeStruct((2, CHIPS) + vector, F32),
            jax.ShapeDtypeStruct((2, CHIPS, 8, 3 * HD), F32),
        ],
        in_specs=[VMEM] * 9 + [ANY] * 3,
        out_specs=[VMEM] * 7,
        scratch_shapes=[
            pltpu.VMEM(grad.shape, BF),
            pltpu.VMEM(qkv_got.shape, BF),
            pltpu.VMEM((HD, LENGTH), BF),
            pltpu.VMEM((LENGTH, HD), BF),
            pltpu.VMEM((HD, LENGTH), BF),
            pltpu.VMEM((LENGTH, HD), BF),
            pltpu.VMEM((LENGTH, HD), BF),
            pltpu.VMEM((HD, LENGTH), BF),
            pltpu.VMEM((LENGTH, HD), BF),
            pltpu.VMEM((1, LENGTH), F32),
            pltpu.VMEM((HD, LENGTH), F32),
            pltpu.VMEM((LENGTH, HD), F32),
            pltpu.VMEM((LENGTH, HD), F32),
            pltpu.VMEM((CHIPS, 3 * HD, PAIR), BF),
            pltpu.VMEM((SEQ,) + vector, F32),
            pltpu.VMEM((SEQ, 128, columns), BF),
            pltpu.VMEM((SEQ, 8, 3 * HD), F32),
            pltpu.VMEM((2, ROWS, D), F32),
            pltpu.VMEM((ROWS, D), F32),
            dma(),
            dma(),
            pltpu.VMEM((4, 16, D), BF),
            pltpu.VMEM((4, 64, D), BF),
            pltpu.VMEM((16, D), BF),
            pltpu.VMEM((32, FF // 2), BF),
            pltpu.VMEM((64, D), BF),
            pltpu.VMEM((CHIPS,) + chip_piece, BF),
        ]
        + Exchange.scratch("a2a", "chip", grad)
        + Exchange.scratch("a2a", "chip", qkv_got)
        + SplitReduce.scratch(inner_half_shape)
        + SplitReduce.scratch(inner_half_shape)
        + RelayReduce.scratch(output_grad, (0, HD), "xy")
        + RelayReduce.scratch(outer_grad, (0, 128), "xy")
        + RelayReduce.scratch(outer_grad, (128, 128), "yx")
        + RelayReduce.scratch(grads_shape, (0, half), "xy")
        + RelayReduce.scratch(grads_shape, (half, half), "yx")
        + Scatter.scratch("seq", vector, F32)
        + Scatter.scratch("seq", (8, 3 * HD), F32)
        + Scatter.scratch("z", (16, D), BF)
        + Scatter.scratch("z", (64, D), BF)
        + Swap.scratch((16, D), BF)
        + Swap.scratch((64, D), BF)
        + Swap.scratch((32, FF // 2), BF)
        + Scatter.scratch("chip", chip_piece, BF)
        + Spread.scratch("z")
        + Spread.scratch("z")
        + Spread.scratch("z")
        + Spread.scratch("chip")
        + Spread.scratch("chip")
        + Spread.scratch("chip"),
        compiler_params=params(identifier, 62),
        name="backward",
    )(
        qkv_got,
        summed,
        stat,
        grad,
        rows_t,
        qkv_weight,
        residual,
        row_sums,
        bias_sums,
        output_grad,
        inner_grad,
        outer_grad,
    )


def unpack(qkv, output, inner, outer, vectors, biases):
    def kernel(*refs):
        refs = Refs(refs)
        qkv_ref, output_ref, inner_ref, outer_ref, vectors_ref, biases_ref = refs.take(6)
        query, key, value, output_out, inner_out, outer_out = refs.take(6)
        query_bias, value_bias, inner_bias = refs.take(3)
        vector = [jnp.sum(vectors_ref[core], axis=0) for core in range(2)]
        bias = [jnp.sum(biases_ref[core], axis=0)[0:1] for core in range(2)]
        for row, out in enumerate(refs.left()):
            out[...] = vector[0][row : row + 1] + vector[1][row : row + 1]
        query_bias[...] = jnp.concatenate([part[:, :HD] for part in bias], axis=1)
        value_bias[...] = jnp.concatenate([part[:, 2 * HD :] for part in bias], axis=1)
        for core in range(2):
            for row in range(2):
                start = core * 256 + row * 128
                inner_bias[:, start : start + 128] = vector[core][6 + row : 7 + row]

        def place(pair, rows):
            for kind, out in enumerate((query, key, value)):
                for head in range(SEQ):
                    at = head * 3 * HD + kind * HD
                    out[rows, head * 128 : (head + 1) * 128] = jnp.concatenate(
                        [part[:, at : at + HD] for part in pair], axis=1
                    )

        for chip in range(CHIPS):
            pair = [qkv_ref[core, chip].astype(F32) for core in range(2)]
            place([part[:8] for part in pair], slice(chip * 8, (chip + 1) * 8))
            place([part[8:] for part in pair], slice(64 + chip * 8, 64 + (chip + 1) * 8))
        for core in range(2):
            for quarter in range(4):
                start = core * HD + quarter * 16
                output_out[start : start + 16] = output_ref[core, quarter].astype(F32)
                start = core * 256 + quarter * 64
                outer_out[start : start + 64] = outer_ref[core, quarter].astype(F32)
                for half in range(2):
                    rows = slice(half * 64 + quarter * 16, half * 64 + (quarter + 1) * 16)
                    for owner in range(SEQ):
                        start = owner * 512 + core * 256
                        inner_out[rows, start : start + 256] = inner_ref[
                            core, quarter, half * 16 : (half + 1) * 16, owner * 256 : (owner + 1) * 256
                        ].astype(F32)

    shapes = [(128, D)] * 4 + [(128, FF), (512, D), (1, 128), (1, 128), (1, 512)] + [(1, 128)] * 6
    return pl.pallas_call(
        kernel,
        out_shape=[jax.ShapeDtypeStruct(shape, F32) for shape in shapes],
        in_specs=[VMEM] * 6,
        out_specs=[VMEM] * 15,
        compiler_params=pltpu.CompilerParams(vmem_limit_bytes=62 * 1024 * 1024),
        name="unpack",
    )(qkv, output, inner, outer, vectors, biases)


def normalize(hidden):
    centered = hidden - jnp.mean(hidden, axis=-1, keepdims=True)
    inverse = lax.rsqrt(jnp.mean(centered * centered, axis=-1, keepdims=True) + 1e-05)
    return centered * inverse, inverse


def normalize_back(upstream, normed, inverse, gain):
    scaled = upstream * gain
    return inverse * (
        scaled
        - jnp.mean(scaled, axis=-1, keepdims=True)
        - normed * jnp.mean(scaled * normed, axis=-1, keepdims=True)
    )


def sum_rows(value):
    return jnp.sum(value, axis=0, keepdims=True)


def feed_forward(identifier, rows, cotangent, attended, output_weight, inner_weight, outer_weight, small, inner_bias):
    units, tile = FF // 2, 512

    def kernel(*refs):
        refs = Refs(refs)
        rows_ref, upstream_ref, attended_ref, small_ref, bias_ref = refs.take(5)
        output_hbm, inner_hbm, outer_hbm = refs.take(3)
        result_ref, residual_ref, turned_ref, sums_ref, bias_sum_ref = refs.take(5)
        grad_output_hbm, grad_inner_hbm, grad_outer_hbm = refs.take(3)
        output_w, inner_w, outer_w, load_sems = refs.take(4)
        grad_output, grad_inner, grad_outer, store_sems = refs.take(4)
        partial, got, pairs, send_sum, recv_sum, send_pair, recv_pair = refs.take(7)
        attended_rows, middle, unit_one, slope, active, grad_hidden = refs.take(6)
        me, other = group_me("core"), group_peer("core", 1)
        loads = [
            pltpu.make_async_copy(source, target, load_sems.at[at])
            for at, (source, target) in enumerate(
                ((output_hbm, output_w), (inner_hbm, inner_w), (outer_hbm, outer_w))
            )
        ]
        stores = [
            pltpu.make_async_copy(source, target, store_sems.at[at])
            for at, (source, target) in enumerate(
                ((grad_outer, grad_outer_hbm), (grad_inner, grad_inner_hbm), (grad_output, grad_output_hbm))
            )
        ]
        sums = [
            remote(partial.at[other], got.at[at], send_sum.at[at], recv_sum.at[at], "core", other)
            for at in range(3)
        ]
        gathers = [
            remote(pairs.at[at, me], pairs.at[at, me], send_pair.at[at], recv_pair.at[at], "core", other)
            for at in range(3)
        ]
        output_bias, first_gain, first_shift, outer_bias, second_gain, second_shift = (
            small_ref[at : at + 1, :] for at in range(6)
        )

        def pair_of(at):
            return pairs[at].reshape(PAIR, D)

        for load in loads:
            load.start()
        enter(["core"])
        attended_rows[...] = attended_ref[...].astype(F32).T.astype(BF).reshape(2, ROWS, D // 2)
        loads[0].wait()
        partial[other] = dot(attended_rows[other], output_w[...])
        sums[0].start()
        partial[me] = dot(attended_rows[me], output_w[...])
        sums[0].wait()
        hidden = rows_ref[...].astype(F32) + (partial[me] + got[0] + output_bias)
        normed, inverse_one = normalize(hidden)
        unit_one[...] = normed
        middle[...] = normed * first_gain + first_shift
        pairs[0, me] = middle[...].astype(BF)
        gathers[0].start()
        loads[1].wait()

        def inner_half(half):
            def one_tile(at, carry):
                here = pl.ds(pl.multiple_of(at * tile, tile), tile)
                value = dot(pairs[0, half], inner_w[:, here]) + bias_ref[:, here]
                part = 0.5 * (1.0 + lax.erf(value * (0.5**0.5)))
                active[half, :, here] = (value * part).astype(BF)
                density = jnp.exp(-0.5 * value * value) * ((2.0 * math.pi) ** -0.5)
                slope[half, :, here] = part + value * density
                return carry

            lax.fori_loop(0, units // tile, one_tile, 0)

        inner_half(me)
        gathers[0].wait()
        inner_half(other)
        loads[2].wait()
        partial[other] = dot(active[other], outer_w[...])
        sums[1].start()
        partial[me] = dot(active[me], outer_w[...])
        sums[1].wait()
        unit_two, inverse_two = normalize(middle[...] + (partial[me] + got[1] + outer_bias))
        result_ref[...] = (unit_two * second_gain + second_shift).astype(BF)
        upstream = upstream_ref[...].astype(F32)
        grad_mid = normalize_back(upstream, unit_two, inverse_two, second_gain)
        pairs[1, me] = grad_mid.astype(BF)
        gathers[1].start()
        middle[...] = grad_mid
        sums_ref[3:4, :] = sum_rows(grad_mid.astype(BF).astype(F32))
        sums_ref[4:5, :] = sum_rows(upstream * unit_two)
        sums_ref[5:6, :] = sum_rows(upstream)
        bias_sum_ref[...] = jnp.zeros_like(bias_sum_ref)

        def hidden_half(half):
            def one_tile(at, carry):
                here = pl.ds(pl.multiple_of(at * tile, tile), tile)
                value = dot(pairs[1, half], outer_w[here, :], ((1,), (1,)))
                value = (value * slope[half, :, here]).astype(BF)
                grad_hidden[half, :, here] = value
                bias_sum_ref[:, here] += sum_rows(value.astype(F32))
                return carry

            lax.fori_loop(0, units // tile, one_tile, 0)

        hidden_half(me)
        gathers[1].wait()
        hidden_half(other)
        partial[other] = dot(grad_hidden[other], inner_w[...], ((1,), (1,)))
        sums[2].start()
        partial[me] = dot(grad_hidden[me], inner_w[...], ((1,), (1,)))

        def outer_tile(at, carry):
            here = pl.ds(pl.multiple_of(at * tile, tile), tile)
            hidden = active[:, :, here].reshape(PAIR, tile)
            grad_outer[here, :] = dot(hidden, pair_of(1), ((0,), (0,))).astype(BF)
            return carry

        lax.fori_loop(0, units // tile, outer_tile, 0)
        stores[0].start()
        sums[2].wait()
        grad_middle = partial[me] + got[2] + middle[...]
        normed = unit_one[...]
        residual = normalize_back(grad_middle, normed, inverse_one, first_gain)
        pairs[2, me] = residual.astype(BF)
        gathers[2].start()
        residual_ref[...] = residual
        sums_ref[0:1, :] = sum_rows(residual.astype(BF).astype(F32))
        sums_ref[1:2, :] = sum_rows(grad_middle * normed)
        sums_ref[2:3, :] = sum_rows(grad_middle)
        sums_ref[6:8, :] = jnp.zeros((2, D), F32)

        def inner_tile(at, carry):
            here = pl.ds(pl.multiple_of(at * tile, tile), tile)
            hidden = grad_hidden[:, :, here].reshape(PAIR, tile)
            grad_inner[:, here] = dot(pair_of(0), hidden, ((0,), (0,))).astype(BF)
            return carry

        lax.fori_loop(0, units // tile, inner_tile, 0)
        stores[1].start()
        gathers[2].wait()
        grad_output[...] = dot(attended_ref[...], pair_of(2)).astype(BF)
        stores[2].start()
        turned_ref[...] = dot(output_w[...], pair_of(2), ((1,), (1,))).astype(BF)
        for store in stores:
            store.wait()

    grads = [(D // 2, D), (D, units), (units, D)]
    return pl.pallas_call(
        kernel,
        out_shape=[
            jax.ShapeDtypeStruct((ROWS, D), BF),
            jax.ShapeDtypeStruct((ROWS, D), F32),
            jax.ShapeDtypeStruct((D // 2, PAIR), BF),
            jax.ShapeDtypeStruct((8, D), F32),
            jax.ShapeDtypeStruct((1, units), F32),
        ]
        + [jax.ShapeDtypeStruct(shape, BF) for shape in grads],
        in_specs=[VMEM] * 5 + [ANY] * 3,
        out_specs=[VMEM] * 5 + [ANY] * 3,
        scratch_shapes=[pltpu.VMEM(shape, BF) for shape in grads]
        + [dma(3)]
        + [pltpu.VMEM(shape, BF) for shape in grads]
        + [
            dma(3),
            pltpu.VMEM((2, ROWS, D), F32),
            pltpu.VMEM((3, ROWS, D), F32),
            pltpu.VMEM((3, 2, ROWS, D), BF),
            dma(3),
            dma(3),
            dma(3),
            dma(3),
            pltpu.VMEM((2, ROWS, D // 2), BF),
            pltpu.VMEM((ROWS, D), F32),
            pltpu.VMEM((ROWS, D), F32),
            pltpu.VMEM((2, ROWS, units), F32),
            pltpu.VMEM((2, ROWS, units), BF),
            pltpu.VMEM((2, ROWS, units), BF),
        ],
        compiler_params=params(identifier, 62),
        name="feed_forward",
    )(rows, cotangent, attended, small, inner_bias, output_weight, inner_weight, outer_weight)


def per_device(
    tokens,
    cotangent,
    w_query,
    b_query,
    w_key,
    w_value,
    b_value,
    w_output,
    b_output,
    first_gain,
    first_shift,
    w_inner,
    b_inner,
    w_outer,
    b_outer,
    second_gain,
    second_shift,
):
    rows = tokens[0]

    small_part = jnp.concatenate(
        [
            jnp.stack(
                [b_query, b_value, b_output, first_gain, first_shift, b_outer, second_gain, second_shift]
            ),
            b_inner.reshape(4, 128),
            jnp.zeros((4, 128), BF),
        ]
    )
    (
        rows_turned,
        qkv_weight,
        rows_small,
        inner_bias,
        output_weight,
        inner_weight,
        outer_weight,
        qkv_got,
        summed,
        attended,
        stat,
    ) = forward(0, rows, w_query, w_key, w_value, small_part, w_output, w_inner, w_outer)
    (
        result,
        grad_residual,
        grad_attended,
        row_sums,
        grad_inner_bias,
        grad_output_weight,
        grad_inner_weight,
        grad_outer_weight,
    ) = feed_forward(
        1,
        rows,
        cotangent[0],
        attended.reshape(D // 2, PAIR),
        output_weight.reshape(D // 2, D),
        inner_weight.reshape(D, FF // 2),
        outer_weight.reshape(FF // 2, D),
        rows_small,
        inner_bias,
    )
    token_grad, *shares = backward(
        2,
        qkv_got,
        summed,
        stat,
        grad_attended.reshape(CHIPS, HD, PAIR),
        rows_turned,
        qkv_weight,
        grad_residual,
        row_sums,
        grad_inner_bias,
        grad_output_weight.reshape(SEQ, HD, D),
        grad_inner_weight.reshape(SEQ, 128, FF // 2),
        grad_outer_weight.reshape(SEQ, 256, D),
    )
    query, key, value, output, inner, outer, query_bias, value_bias, inner_bias, *whole = unpack(*shares)
    whole = [row.reshape(128) for row in whole]
    return (
        result[None],
        token_grad[None],
        query,
        query_bias.reshape(128),
        key,
        value,
        value_bias.reshape(128),
        output,
        whole[0],
        whole[1],
        whole[2],
        inner,
        inner_bias.reshape(512),
        outer,
        whole[3],
        whole[4],
        whole[5],
    )


def solution(mesh):
    row = P("seq", None)
    vector = P("seq")
    placed = P("seq", "ctx", None)
    return jax.shard_map(
        per_device,
        mesh=mesh,
        in_specs=(
            placed,
            placed,
            row,
            vector,
            row,
            row,
            vector,
            row,
            vector,
            vector,
            vector,
            row,
            vector,
            row,
            vector,
            vector,
            vector,
        ),
        out_specs=(
            placed,
            placed,
            row,
            vector,
            row,
            row,
            vector,
            row,
            vector,
            vector,
            vector,
            row,
            vector,
            row,
            vector,
            vector,
            vector,
        ),
        check_vma=False,
    )
```
